32 devices in a mesh: img: 4 (over z), ori: 8 (over y, x, core).
Axes of the slice: x: 2, y: 2, z: 4, core: 2. Of those that a mesh axis runs over, the one named last changes fastest.
Arguments:
- images: bfloat16 [64, 16384], P(('img', 'ori')), may hold values from -8 to 8
- references: bfloat16 [128, 16384], P('ori'), may hold values from -6 to 6
- shifts: float32 [12, 2], replicated, may hold values from -3 to 3
- owners: int32 [16384, 1], P(('ori', 'img')), may hold values from 0 to 7; in each aligned block of 512 rows (0 to 511, 512 to 1023, ...) at most 256 rows name the same one
- slot_rows: int32 [16384], P(('ori', 'img')), may hold values from 0 to 255
- interpolation: float32 [4096, 128], P(('ori', 'img')), may hold values from -0.5 to 0.5
- regularizer: float32 [8192], P(('ori', 'img')), may hold values from 1 to 16
Outputs:
- volume: float32 [8192, 128], P(('ori', 'img'))
- resampled: float32 [128, 16384], P(('ori', 'img'))
The draws below stay inside these ranges and needn't reach their ends.
Inputs may be any that keep to these rules, and one draw needn't show every extreme that they name: `owners`: among the 512 segments of one device (aligned blocks of rows), no owner is named more than 256 times, a bound that some block reaches.
All inputs are finite; a program needn't handle non-finite values.
Results may differ from the reference program's by a relative error of at most 0.014.
Values may be sent and summed in bfloat16 or wider, within the bound.
No kernel may reach another device: no remote copies, remote signals or barrier semaphores. Data moves between devices by JAX's collectives and lax.ppermute only.
A program may use at most 64 MiB of HBM per device.

```python
import math
import jax
import jax.numpy as jnp
import numpy as np
from jax import lax

COEF = 16384
SEGLEN = 128
SHIFTS = 12
O_DEV = 16
IMG_DEV = 2
SEGS = 128
ORIENT = 128
IMAGES = 64
SEG_DEV = 512
CAP = 256
VR_DEV = 256
VROWS = 8192
NSEG = 16384
N_IMG = 4
N_ORI = 8
DEVICES = 32


grid_width = 64


image_side = 128.0


def phase_tables_drawn(shifts):
    half_len = COEF // 2
    positions = jnp.arange(half_len, dtype=jnp.int32)
    freq_x = (positions % grid_width).astype(jnp.float32)
    freq_y = (positions // grid_width - half_len // grid_width // 2).astype(jnp.float32)
    angles = 2.0 * math.pi / image_side * (shifts[:, 0:1] * freq_x[None, :] + shifts[:, 1:2] * freq_y[None, :])
    return (jnp.cos(angles), jnp.sin(angles))


def common_references(key):
    ref_key = jax.random.fold_in(key, 11)
    values = jnp.clip(jax.random.normal(ref_key, (ORIENT, COEF), jnp.float32), -6.0, 6.0)
    return values


def common_shifts(key):
    return jax.random.uniform(jax.random.fold_in(key, 12), (SHIFTS, 2), jnp.float32, -3.0, 3.0)


def draw_references(key, part):
    return common_references(key).astype(jnp.bfloat16)


def draw_shifts(key, part):
    return common_shifts(key)


def aligned_rows(key, base):
    refs_rounded = common_references(key).astype(jnp.bfloat16).astype(jnp.float32)
    cosine_table, sine_table = phase_tables_drawn(common_shifts(key))
    keys_list = jax.random.split(jax.random.fold_in(key, 14), 5)
    first_pick = jax.random.randint(keys_list[0], (IMAGES,), 0, ORIENT)
    second_pick = (first_pick + 1 + jax.random.randint(keys_list[1], (IMAGES,), 0, ORIENT - 1)) % ORIENT
    shift_pick = jax.random.randint(keys_list[2], (IMAGES,), 0, SHIFTS)
    chosen = jax.random.randint(keys_list[3], (IMAGES,), 0, 16) == 0
    amplify = math.sqrt(16384.0 / COEF)
    strength = amplify * jax.random.uniform(keys_list[4], (IMAGES,), jnp.float32, 0.6, 1.5)
    half_len = COEF // 2
    paired = refs_rounded[first_pick] + refs_rounded[second_pick]
    cos_rows = cosine_table[shift_pick]
    sin_rows = sine_table[shift_pick]
    aligned_re = paired[:, :half_len] * cos_rows - paired[:, half_len:] * sin_rows
    aligned_im = paired[:, :half_len] * sin_rows + paired[:, half_len:] * cos_rows
    aligned = jnp.clip(strength[:, None] * jnp.concatenate([aligned_re, aligned_im], axis=1), -8.0, 8.0)
    return jnp.where(chosen[:, None], aligned, base)


def draw_images(key, part):
    image_key = jax.random.fold_in(key, 13)
    base = jnp.clip(jax.random.normal(image_key, (IMAGES, COEF), jnp.float32), -6.0, 6.0)
    values = aligned_rows(key, base)
    return values.astype(jnp.bfloat16)


def plant(drawn, key, least, largest):
    extent = drawn.shape
    spot = [jax.random.randint(jax.random.fold_in(key, axis), (), 0, extent[axis]) for axis in range(len(extent))]
    drawn = drawn.at[tuple(spot)].set(least)
    longest = extent.index(max(extent))
    spot[longest] = (spot[longest] + 1) % extent[longest]
    return drawn.at[tuple(spot)].set(largest)


def steps_of(stream_key, extent, cuts, least, high):
    level, own = 1.0, jax.random.fold_in(stream_key, 6)
    for dim, blocks in cuts:
        steps = jnp.exp(jax.random.uniform(jax.random.fold_in(own, dim), (blocks,), jnp.float32, least / len(cuts), high / len(cuts)))
        level = level * jnp.repeat(steps, extent[dim] // blocks).reshape([-1 if axis == dim else 1 for axis in range(len(extent))])
    return level


def routed_block(key, own, number, rows, number_of, top, most, skew):
    sequence = jax.random.permutation(key, number_of)
    packed, common = load_shares(number_of, rows * top, most, skew, True), load_shares(number_of, rows * top, most, skew, False)
    places = jnp.arange(number_of)

    def named(tallies, offset_by):
        used = int((tallies > 0).sum())
        fixed = max(1, used // 4)
        shifted = fixed + (places - fixed + offset_by * (used - fixed)) % max(1, number_of - fixed)
        return jnp.zeros((number_of,), jnp.int32).at[sequence[jnp.where(places < fixed, places, shifted)]].set(jnp.asarray(tallies, jnp.int32))

    tallies = jnp.where(number % 4 == 0, named(packed, number // 4), named(common, number - number // 4 - 1))
    mixed = jax.random.permutation(jax.random.fold_in(own, 3), number_of)
    giver, receiver = mixed[0:number_of // 2 * 2:2], mixed[1:number_of // 2 * 2:2]
    room = jnp.minimum(tallies[giver] - 1, most - tallies[receiver]) // 2
    room = jnp.where((giver == sequence[0]) | (receiver == sequence[0]) | (tallies[receiver] == 0), 0, jnp.maximum(room, 0))
    shifted = jax.random.randint(jax.random.fold_in(own, 4), (number_of // 2,), 0, 1 << 20) % (room + 1)
    tallies = tallies.at[giver].add(-shifted).at[receiver].add(shifted)
    members = jnp.searchsorted(jnp.cumsum(tallies), jnp.arange(rows * top), side="right").astype(jnp.int32)
    table = members.reshape(top, rows).T
    table = table[jax.random.permutation(jax.random.fold_in(own, 1), rows)]
    offset_by = jax.random.randint(jax.random.fold_in(own, 2), (rows, 1), 0, top)
    return jnp.take_along_axis(table, (jnp.arange(top)[None, :] + offset_by) % top, axis=1)


def load_shares(number_of, total, bound, skew, full):
    weights = [(1 << 20) // math.isqrt(standing ** skew) + 1 for standing in range(1, number_of + 1)]
    largest = bound if full else min(bound, max(-(-total // number_of), total * weights[0] // sum(weights)))
    least = 1 if total - largest >= number_of - 1 else 0
    holding, spare = [largest] + [least] * (number_of - 1), total - largest - least * (number_of - 1)
    while spare > 0:
        movable = [i for i in range(1, number_of) if holding[i] < largest] or [i for i in range(1, number_of) if holding[i] < bound]
        mass, left = sum([weights[i] for i in movable]), spare
        for i in movable:
            more = min(bound - holding[i], max(1, left * weights[i] // mass), spare)
            holding[i] = holding[i] + more
            spare = spare - more
    return np.array(holding)


def centred(rng, dims, scale, most, shards=(), kind=jnp.bfloat16):
    drawn = jax.random.normal(rng, dims, jnp.float32) * scale
    if len(shards) > 0:
        drawn = steps_of(rng, dims, shards, -0.22, 0.18) * drawn
    return jnp.clip(drawn, min=-most, max=most).astype(kind)


def setup_inputs(seed: int = 0) -> dict:
    key_list = jax.random.split(jax.random.key(seed), 8)
    images = draw_images(jax.random.fold_in(key_list[7], 71), 0)
    references = draw_references(jax.random.fold_in(key_list[7], 71), 0)
    shifts = draw_shifts(jax.random.fold_in(key_list[7], 71), 0)
    owners_keys = jax.random.split(jax.random.fold_in(key_list[3], 1), NSEG // SEG_DEV)
    owners_turns = jax.random.permutation(jax.random.fold_in(key_list[3], 3), NSEG // SEG_DEV)
    owners = jax.vmap(lambda own, number: routed_block(jax.random.fold_in(key_list[3], 2), own, number, SEG_DEV, N_ORI, 1, CAP, 2))(owners_keys, owners_turns).reshape((NSEG, 1))
    slot_rows = plant(jax.random.randint(key_list[4], (NSEG,), 0, VR_DEV), jax.random.fold_in(key_list[4], 1), 0, VR_DEV - 1).astype(jnp.int32)
    interpolation = centred(key_list[5], (DEVICES * SEGLEN, SEGLEN), SEGLEN ** -0.5, 0.5, ((0, 32),), jnp.float32)
    regularizer = jnp.clip(jnp.exp(math.log(16.0) - 2.7725887 * jax.random.uniform(key_list[6], (VROWS,), jnp.float32) ** steps_of(key_list[6], (VROWS,), ((0, 32),), -0.2, 0.2)), 1.0, 16.0)
    return dict(images=images, references=references, shifts=shifts, owners=owners, slot_rows=slot_rows, interpolation=interpolation, regularizer=regularizer)


grid_width = 64
image_side = 128.0

def phase_tables(shifts):
    half_len = COEF // 2
    positions = jnp.arange(half_len, dtype=jnp.int32)
    freq_x = (positions % grid_width).astype(jnp.float32)
    freq_y = (positions // grid_width - half_len // grid_width // 2).astype(jnp.float32)
    angles = 2.0 * math.pi / image_side * (shifts[:, 0:1] * freq_x[None, :] + shifts[:, 1:2] * freq_y[None, :])
    return (jnp.cos(angles), jnp.sin(angles))

def shifted_slices(references, cosine_table, sine_table):
    half_len = COEF // 2
    real_part = references[:, :half_len].astype(jnp.float32)
    imag_part = references[:, half_len:].astype(jnp.float32)
    rotated_re = real_part[:, None, :] * cosine_table[None] - imag_part[:, None, :] * sine_table[None]
    rotated_im = real_part[:, None, :] * sine_table[None] + imag_part[:, None, :] * cosine_table[None]
    stacked = jnp.concatenate([rotated_re, rotated_im], axis=2)
    return stacked.reshape(-1, COEF).astype(jnp.bfloat16)

def backproject(weights_b, group_images, cosine_table, sine_table):
    half_len = COEF // 2
    orient_count = weights_b.shape[1]
    total_re = jnp.zeros((orient_count, half_len), jnp.float32)
    total_im = jnp.zeros((orient_count, half_len), jnp.float32)
    for shift_number in range(SHIFTS):
        summed = lax.dot_general(weights_b[:, :, shift_number], group_images, (((0,), (0,)), ((), ())), preferred_element_type=jnp.float32)
        sum_re = summed[:, :half_len]
        sum_im = summed[:, half_len:]
        total_re = total_re + sum_re * cosine_table[shift_number] + sum_im * sine_table[shift_number]
        total_im = total_im - sum_re * sine_table[shift_number] + sum_im * cosine_table[shift_number]
    return jnp.concatenate([total_re, total_im], axis=1)

def reference(images, references, shifts, owners, slot_rows, interpolation, regularizer):
    cosine_table, sine_table = phase_tables(shifts)
    rotated = shifted_slices(references, cosine_table, sine_table)
    score_scale = 2.0 / math.sqrt(COEF)
    group_rows = IMG_DEV * N_ORI
    grouped = images.reshape(N_IMG, group_rows, COEF)

    def one_group(running, group_images):
        scores = lax.dot_general(group_images, rotated, (((1,), (1,)), ((), ())), preferred_element_type=jnp.float32) * score_scale
        row_peak = lax.optimization_barrier(jnp.max(scores, axis=1, keepdims=True))
        exponent = jnp.exp(scores - row_peak)
        weights = exponent / lax.optimization_barrier(jnp.sum(exponent, axis=1, keepdims=True))
        weights3 = weights.reshape(group_rows, ORIENT, SHIFTS)
        orient_mass = lax.optimization_barrier(jnp.sum(weights3, axis=(0, 2)))
        summed = backproject(weights3.astype(jnp.bfloat16), group_images, cosine_table, sine_table)
        return ((running[0] + summed, running[1] + orient_mass), None)
    start_state = (jnp.zeros((ORIENT, COEF), jnp.float32), jnp.zeros((ORIENT,), jnp.float32))
    (slices, orient_mass), _ = lax.scan(one_group, start_state, grouped)
    device_count = N_IMG * N_ORI
    total_rows = regularizer.shape[0]
    brick_rows = total_rows // device_count
    seg_device = O_DEV // N_IMG * SEGS
    segments = slices.reshape(ORIENT * SEGS, SEGLEN)
    seg_mass = jnp.repeat(orient_mass, SEGS)
    positions = jnp.arange(ORIENT * SEGS, dtype=jnp.int32)
    group_of = positions // seg_device % N_IMG
    target = ((owners[:, 0] * N_IMG + group_of) * brick_rows + slot_rows).astype(jnp.int32)
    inserted = jnp.zeros((total_rows, SEGLEN), jnp.float32).at[target].add(segments)
    weight_sum = jnp.zeros((total_rows,), jnp.float32).at[target].add(seg_mass)
    kernels = interpolation.reshape(device_count, SEGLEN, SEGLEN)
    mapped = jnp.einsum('drk,dkl->drl', inserted.reshape(device_count, brick_rows, SEGLEN), kernels, precision=lax.Precision.HIGHEST)
    volume = mapped.reshape(total_rows, SEGLEN) / (weight_sum + regularizer)[:, None]
    back_values = jnp.einsum('drl,dkl->drk', volume.reshape(device_count, brick_rows, SEGLEN), kernels, precision=lax.Precision.HIGHEST)
    resampled = back_values.reshape(total_rows, SEGLEN)[target].reshape(ORIENT, COEF)
    return (volume, resampled)
```

```python
import math

import jax
import jax.numpy as jnp
from jax import lax
from jax.sharding import PartitionSpec as P

SEGLEN = 128
grid_width = 64
image_side = 128.0
bf16 = jnp.bfloat16
f32 = jnp.float32


def hop(value, axis, distance):
    pairs = [(place, place ^ distance) for place in range(lax.axis_size(axis))]
    return lax.ppermute(value, axis, pairs)


def even_distances():
    return range(2, lax.axis_size("ori"), 2)


def gather_plane(value):
    near = jnp.concatenate([value] + [hop(value, "ori", k) for k in even_distances()], axis=0)
    return jnp.concatenate([near, hop(near, "ori", 1)], axis=0)


def phase_tables(shifts, coef):
    half_len = coef // 2
    positions = jnp.arange(half_len, dtype=jnp.int32)
    freq_x = (positions % grid_width).astype(f32)
    freq_y = (positions // grid_width - half_len // grid_width // 2).astype(f32)
    angles = (
        2.0
        * math.pi
        / image_side
        * (shifts[:, 0:1] * freq_x[None, :] + shifts[:, 1:2] * freq_y[None, :])
    )
    return (jnp.cos(angles), jnp.sin(angles))


def rotate(real_part, imag_part, cosine_row, sine_row):
    rotated_re = real_part * cosine_row[None, :] - imag_part * sine_row[None, :]
    rotated_im = real_part * sine_row[None, :] + imag_part * cosine_row[None, :]
    return jnp.concatenate([rotated_re, rotated_im], axis=1).astype(bf16)


def backproject(weights_b, group_images, cosine_table, sine_table):
    half_len = group_images.shape[1] // 2
    orient_count = weights_b.shape[1]
    total_re = jnp.zeros((orient_count, half_len), f32)
    total_im = jnp.zeros((orient_count, half_len), f32)
    for s in range(cosine_table.shape[0]):
        summed = lax.dot_general(
            weights_b[:, :, s],
            group_images,
            (((0,), (0,)), ((), ())),
            preferred_element_type=f32,
        )
        sum_re = summed[:, :half_len]
        sum_im = summed[:, half_len:]
        total_re = total_re + sum_re * cosine_table[s] + sum_im * sine_table[s]
        total_im = total_im - sum_re * sine_table[s] + sum_im * cosine_table[s]
    return jnp.concatenate([total_re, total_im], axis=1)


def merge_stats(stats, distance):
    far = hop(stats, "ori", distance)
    if distance == 1:
        return far[:, ::-1]
    half = distance // 2
    return jnp.stack([far[:, :, e ^ half] for e in range(far.shape[2])], axis=2)


def join(pairs):
    peak = pairs[0][0]
    for pair in pairs[1:]:
        peak = jnp.maximum(peak, pair[0])
    total = sum(pair[1] * jnp.exp(pair[0] - peak) for pair in pairs)
    return jnp.stack([peak, total])


def shards(images, references, shifts, owners, slot_rows, interpolation, regularizer):
    ori_count, img_count = lax.axis_size("ori"), lax.axis_size("img")
    ori, img = lax.axis_index("ori"), lax.axis_index("img")
    shift_count = shifts.shape[0]
    coef = images.shape[1]
    own_images = images.shape[0]
    segs = coef // SEGLEN
    row_count = regularizer.shape[0]
    orient_count = references.shape[0]
    sub_rows = orient_count // img_count
    half_len = coef // 2

    group_images = gather_plane(images)
    group_rows = group_images.shape[0]
    cosine_table, sine_table = phase_tables(shifts, coef)
    references = jnp.concatenate(
        [
            lax.dynamic_slice_in_dim(references, (img ^ m) * sub_rows, sub_rows, 0)
            for m in range(img_count)
        ],
        axis=0,
    )
    real_part = references[:, :half_len].astype(f32)
    imag_part = references[:, half_len:].astype(f32)
    distance = owners[:, 0] ^ ori
    place = (distance >> 1) + (distance & 1) * (ori_count // 2)
    target = place * row_count + slot_rows
    all_rows = ori_count * row_count
    chosen = (jnp.arange(all_rows, dtype=jnp.int32)[:, None] == target[None, :]).astype(bf16)

    score_list = []
    for s in range(shift_count):
        rotated = rotate(real_part, imag_part, cosine_table[s], sine_table[s])
        score_list.append(
            lax.dot_general(
                group_images, rotated, (((1,), (1,)), ((), ())), preferred_element_type=f32
            )
        )
    scores = jnp.stack(score_list, axis=2).reshape(group_rows, -1) * (2.0 / math.sqrt(coef))
    local_peak = jnp.max(scores, axis=1)
    local_total = jnp.sum(jnp.exp(scores - local_peak[:, None]), axis=1)
    stats = jnp.stack([local_peak, local_total]).reshape(2, 2, ori_count // 2, own_images)
    stats = join([stats, merge_stats(stats, 1)])
    stats = join([stats] + [merge_stats(stats, k) for k in even_distances()])
    stats = stats.reshape(2, group_rows)
    weights = jnp.exp(scores - stats[0][:, None]) / stats[1][:, None]
    weights3 = weights.reshape(group_rows, orient_count, shift_count)
    orient_mass = jnp.sum(weights3, axis=(0, 2))
    summed = backproject(weights3.astype(bf16), group_images, cosine_table, sine_table)

    blocks = summed.reshape(img_count, sub_rows, coef)
    masses = orient_mass.reshape(img_count, sub_rows, 1)
    outgoing = jnp.concatenate(
        [blocks, jnp.broadcast_to(masses, (img_count, sub_rows, SEGLEN))], axis=2
    ).astype(bf16)
    incoming = [hop(outgoing[m], "img", m).astype(f32) for m in range(1, img_count)]
    own = blocks[0] + sum(value[:, :coef] for value in incoming)
    own_mass = masses[0] + sum(value[:, coef : coef + 1] for value in incoming)
    segments = own.astype(bf16).reshape(-1, SEGLEN)
    seg_mass = jnp.repeat(own_mass[:, 0], segs)[None, :]

    part = jnp.dot(chosen, segments, preferred_element_type=f32)
    part_mass = lax.dot_general(
        seg_mass.astype(bf16), chosen, (((1,), (1,)), ((), ())), preferred_element_type=f32
    )
    mass_rows = max(16, row_count // SEGLEN)
    part_mass = part_mass.reshape(ori_count, row_count)
    part_mass = jnp.pad(part_mass, ((0, 0), (0, mass_rows * SEGLEN - row_count)))
    parcel = jnp.concatenate(
        [part.reshape(ori_count, row_count, SEGLEN), part_mass.reshape(ori_count, -1, SEGLEN)], axis=1
    ).astype(bf16)
    half = ori_count // 2
    parcel = parcel[:half].astype(f32) + hop(parcel[half:], "ori", 1).astype(f32)
    small = parcel.astype(bf16)
    brick = parcel[0] + sum(hop(small[k // 2], "ori", k).astype(f32) for k in even_distances())
    inserted = brick[:row_count]
    weight_sum = brick[row_count:].reshape(-1)[:row_count]
    mapped = jnp.dot(
        inserted, interpolation, precision=lax.Precision.HIGHEST, preferred_element_type=f32
    )
    volume = mapped / (weight_sum + regularizer)[:, None]
    back_values = lax.dot_general(
        volume,
        interpolation,
        (((1,), (1,)), ((), ())),
        precision=lax.Precision.HIGHEST,
        preferred_element_type=f32,
    )
    bricks = gather_plane(back_values.astype(bf16))
    resampled = lax.dot_general(
        chosen, bricks, (((0,), (0,)), ((), ())), preferred_element_type=f32
    )
    return (volume, resampled.reshape(sub_rows, coef))


def solution(mesh):
    in_specs = (
        P(("img", "ori"), None),
        P("ori", None),
        P(),
        P(("ori", "img"), None),
        P(("ori", "img")),
        P(("ori", "img"), None),
        P(("ori", "img")),
    )
    out_specs = (P(("ori", "img"), None), P(("ori", "img"), None))
    return jax.shard_map(shards, mesh=mesh, in_specs=in_specs, out_specs=out_specs, check_vma=False)
```

```python
import functools
import math

import jax
import jax.numpy as jnp
from jax import lax
from jax.experimental import pallas as pl
from jax.experimental.pallas import tpu as pltpu
from jax.sharding import PartitionSpec as P

SEGLEN = 128
grid_width = 64
image_side = 128.0
CHUNK = 256
LANES = (((1,), (1,)), ((), ()))
COST_SCORE = 10.0
COST_WEIGHT = 5.0
COST_PLACE = 1.0
COST_VOLUME = 10.0
bf16 = jnp.bfloat16
f32 = jnp.float32


def hop(value, axis, distance):
    pairs = [(place, place ^ distance) for place in range(lax.axis_size(axis))]
    return lax.ppermute(value, axis, pairs)


def even_distances():
    return range(2, lax.axis_size("ori"), 2)


def gather_plane(value):
    near = jnp.concatenate([value] + [hop(value, "ori", k) for k in even_distances()], axis=0)
    return jnp.concatenate([near, hop(near, "ori", 1)], axis=0)


def phase_tables(shifts, coef):
    half_len = coef // 2
    positions = jnp.arange(half_len, dtype=jnp.int32)
    freq_x = (positions % grid_width).astype(f32)
    freq_y = (positions // grid_width - half_len // grid_width // 2).astype(f32)
    angles = (
        2.0
        * math.pi
        / image_side
        * (shifts[:, 0:1] * freq_x[None, :] + shifts[:, 1:2] * freq_y[None, :])
    )
    return (jnp.cos(angles), jnp.sin(angles))


def rotate(real_part, imag_part, cosine_row, sine_row):
    rotated_re = real_part * cosine_row[None, :] - imag_part * sine_row[None, :]
    rotated_im = real_part * sine_row[None, :] + imag_part * cosine_row[None, :]
    return jnp.concatenate([rotated_re, rotated_im], axis=1).astype(bf16)


def backproject(weights_b, group_images, cosine_table, sine_table):
    half_len = group_images.shape[1] // 2
    orient_count = weights_b.shape[1]
    total_re = jnp.zeros((orient_count, half_len), f32)
    total_im = jnp.zeros((orient_count, half_len), f32)
    for s in range(cosine_table.shape[0]):
        summed = lax.dot_general(
            weights_b[:, :, s],
            group_images,
            (((0,), (0,)), ((), ())),
            preferred_element_type=f32,
        )
        sum_re = summed[:, :half_len]
        sum_im = summed[:, half_len:]
        total_re = total_re + sum_re * cosine_table[s] + sum_im * sine_table[s]
        total_im = total_im - sum_re * sine_table[s] + sum_im * cosine_table[s]
    return jnp.concatenate([total_re, total_im], axis=1)


def merge_stats(stats, distance):
    far = hop(stats, "ori", distance)
    if distance == 1:
        return far[:, ::-1]
    half = distance // 2
    return jnp.stack([far[:, :, e ^ half] for e in range(far.shape[2])], axis=2)


def join(pairs):
    peak = pairs[0][0]
    for pair in pairs[1:]:
        peak = jnp.maximum(peak, pair[0])
    total = sum(pair[1] * jnp.exp(pair[0] - peak) for pair in pairs)
    return jnp.stack([peak, total])


def reduced(images, references, shifts, owners, slot_rows, interpolation, regularizer):
    ori_count, img_count = lax.axis_size("ori"), lax.axis_size("img")
    ori, img = lax.axis_index("ori"), lax.axis_index("img")
    shift_count = shifts.shape[0]
    coef = images.shape[1]
    own_images = images.shape[0]
    segs = coef // SEGLEN
    row_count = regularizer.shape[0]
    orient_count = references.shape[0]
    sub_rows = orient_count // img_count
    half_len = coef // 2

    group_images = gather_plane(images)
    group_rows = group_images.shape[0]
    cosine_table, sine_table = phase_tables(shifts, coef)
    references = jnp.concatenate(
        [
            lax.dynamic_slice_in_dim(references, (img ^ m) * sub_rows, sub_rows, 0)
            for m in range(img_count)
        ],
        axis=0,
    )
    real_part = references[:, :half_len].astype(f32)
    imag_part = references[:, half_len:].astype(f32)
    distance = owners[:, 0] ^ ori
    place = (distance >> 1) + (distance & 1) * (ori_count // 2)
    target = place * row_count + slot_rows
    all_rows = ori_count * row_count
    chosen = (jnp.arange(all_rows, dtype=jnp.int32)[:, None] == target[None, :]).astype(bf16)

    score_list = []
    for s in range(shift_count):
        rotated = rotate(real_part, imag_part, cosine_table[s], sine_table[s])
        score_list.append(
            lax.dot_general(
                group_images, rotated, (((1,), (1,)), ((), ())), preferred_element_type=f32
            )
        )
    scores = jnp.stack(score_list, axis=2).reshape(group_rows, -1) * (2.0 / math.sqrt(coef))
    local_peak = jnp.max(scores, axis=1)
    local_total = jnp.sum(jnp.exp(scores - local_peak[:, None]), axis=1)
    stats = jnp.stack([local_peak, local_total]).reshape(2, 2, ori_count // 2, own_images)
    stats = join([stats, merge_stats(stats, 1)])
    stats = join([stats] + [merge_stats(stats, k) for k in even_distances()])
    stats = stats.reshape(2, group_rows)
    weights = jnp.exp(scores - stats[0][:, None]) / stats[1][:, None]
    weights3 = weights.reshape(group_rows, orient_count, shift_count)
    orient_mass = jnp.sum(weights3, axis=(0, 2))
    summed = backproject(weights3.astype(bf16), group_images, cosine_table, sine_table)

    blocks = summed.reshape(img_count, sub_rows, coef)
    masses = orient_mass.reshape(img_count, sub_rows, 1)
    outgoing = jnp.concatenate(
        [blocks, jnp.broadcast_to(masses, (img_count, sub_rows, SEGLEN))], axis=2
    ).astype(bf16)
    incoming = [hop(outgoing[m], "img", m).astype(f32) for m in range(1, img_count)]
    own = blocks[0] + sum(value[:, :coef] for value in incoming)
    own_mass = masses[0] + sum(value[:, coef : coef + 1] for value in incoming)
    segments = own.astype(bf16).reshape(-1, SEGLEN)
    seg_mass = jnp.repeat(own_mass[:, 0], segs)[None, :]

    part = jnp.dot(chosen, segments, preferred_element_type=f32)
    part_mass = lax.dot_general(
        seg_mass.astype(bf16), chosen, (((1,), (1,)), ((), ())), preferred_element_type=f32
    )
    mass_rows = max(16, row_count // SEGLEN)
    part_mass = part_mass.reshape(ori_count, row_count)
    part_mass = jnp.pad(part_mass, ((0, 0), (0, mass_rows * SEGLEN - row_count)))
    parcel = jnp.concatenate(
        [part.reshape(ori_count, row_count, SEGLEN), part_mass.reshape(ori_count, -1, SEGLEN)], axis=1
    ).astype(bf16)
    half = ori_count // 2
    parcel = parcel[:half].astype(f32) + hop(parcel[half:], "ori", 1).astype(f32)
    small = parcel.astype(bf16)
    brick = parcel[0] + sum(hop(small[k // 2], "ori", k).astype(f32) for k in even_distances())
    inserted = brick[:row_count]
    weight_sum = brick[row_count:].reshape(-1)[:row_count]
    mapped = jnp.dot(
        inserted, interpolation, precision=lax.Precision.HIGHEST, preferred_element_type=f32
    )
    volume = mapped / (weight_sum + regularizer)[:, None]
    back_values = lax.dot_general(
        volume,
        interpolation,
        (((1,), (1,)), ((), ())),
        precision=lax.Precision.HIGHEST,
        preferred_element_type=f32,
    )
    bricks = gather_plane(back_values.astype(bf16))
    resampled = lax.dot_general(
        chosen, bricks, (((0,), (0,)), ((), ())), preferred_element_type=f32
    )
    return (volume, resampled.reshape(sub_rows, coef))


def iota(shape, axis):
    return lax.broadcasted_iota(jnp.int32, shape, axis)


def distance_of(place, ori_count):
    half = ori_count // 2
    return jnp.where(place < half, 2 * place, 2 * (place - half) + 1)


def gather_pair(value):
    near = jnp.stack([value] + [hop(value, "ori", k) for k in even_distances()], axis=0)
    return near, hop(near, "ori", 1)


def first_phases(shifts):
    rows = jnp.pad(shifts, ((0, -shifts.shape[0] % 8), (0, 0)))
    lane = jnp.arange(CHUNK, dtype=jnp.int32)
    freq_x = (lane % grid_width).astype(f32)
    freq_y = (lane // grid_width).astype(f32) - image_side / 2
    unit = 2.0 * math.pi / image_side
    angles = unit * (rows[:, 0:1] * freq_x[None, :] + rows[:, 1:2] * freq_y[None, :])
    steps = unit * rows[:, 1:2] * jnp.full((1, CHUNK), float(CHUNK // grid_width), f32)
    angles = jnp.stack([angles, steps])
    return jnp.stack([jnp.cos(angles), jnp.sin(angles)])


def turn(phases, now):
    cosine, sine = now[0], now[1]
    cos_step, sin_step = phases[0, 1], phases[1, 1]
    now[0] = cosine * cos_step - sine * sin_step
    now[1] = sine * cos_step + cosine * sin_step


def place_images(near, far, first, order, out, row, group_rows):
    shares = 2 * near.shape[0]
    step = 16 * shares // group_rows
    for q in range(out.shape[1] // SEGLEN // step):
        rows = pl.ds(first + 16 * q, 16)
        block = jnp.concatenate([near[:, rows, :], far[:, rows, :]], axis=0)
        block = block.reshape(shares * 16, SEGLEN)
        placed = jnp.dot(order, block, preferred_element_type=f32).astype(bf16)
        for jj in range(step):
            lanes = pl.ds((q * step + jj) * SEGLEN, SEGLEN)
            out[row : row + group_rows, lanes] = placed[jj * group_rows : (jj + 1) * group_rows]


def score_kernel(shift_count, near, far, order, references, phases, scores, own, now):
    group_rows, coef = own.shape
    half_len = coef // 2
    place_images(near, far, 0, order[...], own, 0, group_rows)
    now[0] = phases[0, 0]
    now[1] = phases[1, 0]

    def step(t, total):
        re_lanes = pl.ds(pl.multiple_of(t * CHUNK, CHUNK), CHUNK)
        im_lanes = pl.ds(pl.multiple_of(half_len + t * CHUNK, CHUNK), CHUNK)
        real_part = references[:, re_lanes].astype(f32)
        imag_part = references[:, im_lanes].astype(f32)
        rotated_re, rotated_im = [], []
        for s in range(shift_count):
            c, d = now[0, s : s + 1, :], now[1, s : s + 1, :]
            rotated_re.append((real_part * c - imag_part * d).astype(bf16))
            rotated_im.append((real_part * d + imag_part * c).astype(bf16))
        total += lax.dot_general(
            jnp.concatenate(rotated_re, axis=0), own[:, re_lanes], LANES, preferred_element_type=f32
        )
        total += lax.dot_general(
            jnp.concatenate(rotated_im, axis=0), own[:, im_lanes], LANES, preferred_element_type=f32
        )
        turn(phases, now)
        return total

    columns = shift_count * references.shape[0]
    total = lax.fori_loop(
        0, half_len // CHUNK, step, jnp.zeros((columns, group_rows), f32), unroll=2
    )
    scores[...] = jnp.swapaxes(total, 0, 1) * (2.0 / math.sqrt(coef))


def weight_kernel(near, far, pick, messages):
    half = near.shape[0]
    parts = [near[p] for p in range(half)] + [far[p] for p in range(half)]
    peak = jnp.max(parts[0], axis=1, keepdims=True)
    for part in parts[1:]:
        peak = jnp.maximum(peak, jnp.max(part, axis=1, keepdims=True))
    exponents = [jnp.exp(part - peak) for part in parts]
    total = sum(jnp.sum(part, axis=1, keepdims=True) for part in exponents)
    weights = [(part / total).astype(bf16) for part in exponents]
    picked = jnp.dot(
        jnp.concatenate(weights[:half], axis=0), pick[0], preferred_element_type=f32
    ) + jnp.dot(jnp.concatenate(weights[half:], axis=0), pick[1], preferred_element_type=f32)
    for k in range(messages.shape[0]):
        messages[k] = picked[:, k * SEGLEN : (k + 1) * SEGLEN].astype(bf16)


def place_kernel(near, far, order, own, everything):
    group_rows, coef = own.shape
    everything[:group_rows, :] = own[...]
    rows = group_rows * coef // SEGLEN // (2 * near.shape[0])
    for k in range(1, everything.shape[0] // group_rows):
        place_images(
            near, far, (k - 1) * rows, order[...], everything, k * group_rows, group_rows
        )


def volume_kernel(shift_count, first, *refs):
    (
        *messages,
        images,
        phases,
        arrange,
        near,
        far,
        owner_ids,
        volume,
        resampled,
        now,
        raw,
        segments,
        chosen,
        result,
    ) = refs
    img_count = len(messages)
    half = near.shape[0]
    shares = 2 * half
    coef = images.shape[1]
    tiles = coef // SEGLEN
    half_len = coef // 2
    group_rows = images.shape[0] // img_count
    sub_rows = resampled.shape[0]
    orients = shares * sub_rows
    row_count = volume.shape[0]
    reg_rows = row_count // SEGLEN
    kernel_rows = pl.ds(first, SEGLEN)
    fact_rows = pl.ds(first + SEGLEN, near.shape[1] - first - SEGLEN)
    fact_count = near.shape[1] - first - SEGLEN

    facts = jnp.concatenate([near[:, fact_rows, :], far[:, fact_rows, :]], axis=0).astype(f32)
    facts = facts.reshape(shares * fact_count, SEGLEN)
    upright = jnp.swapaxes(facts, 0, 1)

    def column(share, fact):
        place = share * fact_count + fact
        return upright[:, place : place + 1]

    stacked = jnp.concatenate(
        [
            jnp.concatenate(
                [message[a * group_rows : (a + 1) * group_rows, :] for message in messages], axis=0
            )
            for a in range(half)
        ],
        axis=1,
    )
    weights = lax.dot_general(arrange[...], stacked, LANES, preferred_element_type=f32)
    mass = jnp.sum(weights, axis=1, keepdims=True)
    mass = sum(mass[s * orients : (s + 1) * orients] for s in range(shift_count))
    weights = weights.astype(bf16)

    slot_number = iota((row_count, SEGLEN), 0).astype(f32)
    for o in range(orients):
        place = o // sub_rows * fact_count + o % sub_rows
        chosen[:, o * tiles : (o + 1) * tiles] = jnp.where(
            slot_number == facts[place : place + 1, :], 1.0, 0.0
        ).astype(bf16)

    now[0] = phases[0, 0]
    now[1] = phases[1, 0]

    def step(t, carry):
        re_lanes = pl.ds(pl.multiple_of(t * CHUNK, CHUNK), CHUNK)
        im_lanes = pl.ds(pl.multiple_of(half_len + t * CHUNK, CHUNK), CHUNK)
        summed_re = jnp.dot(weights, images[:, re_lanes], preferred_element_type=f32)
        summed_im = jnp.dot(weights, images[:, im_lanes], preferred_element_type=f32)
        total_re = jnp.zeros((orients, CHUNK), f32)
        total_im = jnp.zeros((orients, CHUNK), f32)
        for s in range(shift_count):
            c, d = now[0, s : s + 1, :], now[1, s : s + 1, :]
            part_re = summed_re[s * orients : (s + 1) * orients]
            part_im = summed_im[s * orients : (s + 1) * orients]
            total_re += part_re * c + part_im * d
            total_im += part_im * c - part_re * d
        turn(phases, now)
        for h in range(CHUNK // SEGLEN):
            j = t * (CHUNK // SEGLEN) + h
            lanes = slice(h * SEGLEN, (h + 1) * SEGLEN)
            raw[pl.ds(j, orients, stride=tiles), :] = total_re[:, lanes]
            raw[pl.ds(half_len // SEGLEN + j, orients, stride=tiles), :] = total_im[:, lanes]
        return carry

    lax.fori_loop(0, half_len // CHUNK, step, 0, unroll=2)

    lane = iota((tiles, SEGLEN), 1)
    ids = [owner_ids[w].astype(bf16) for w in range(shares)]
    lane_owner = sum(
        jnp.where(lane % shares == w, owner_ids[w], 0) for w in range(shares)
    ).astype(bf16)
    zero = jnp.zeros((tiles, SEGLEN), bf16)
    for o in range(orients):
        share = o // sub_rows
        rows = slice(o * tiles, (o + 1) * tiles)
        part = raw[rows, :].astype(bf16)
        owner = jnp.broadcast_to(column(share, sub_rows + o % sub_rows), (tiles, SEGLEN))
        owner = owner.astype(bf16)
        for w in range(shares):
            segments[rows, w * SEGLEN : (w + 1) * SEGLEN] = jnp.where(owner == ids[w], part, zero)
        own_mass = jnp.broadcast_to(mass[o : o + 1, :], (tiles, SEGLEN))
        mass_hi = own_mass.astype(bf16)
        mass_lo = (own_mass - mass_hi.astype(f32)).astype(bf16)
        mass_part = jnp.where(lane < shares, mass_hi.astype(f32), mass_lo.astype(f32))
        mass_part = jnp.where(lane < 2 * shares, mass_part, 0.0).astype(bf16)
        segments[rows, shares * SEGLEN :] = jnp.where(owner == lane_owner, mass_part, zero)

    inserted = jnp.dot(chosen[...], segments[...], preferred_element_type=f32)
    tail = shares * SEGLEN
    weight_sum = inserted[:, tail : tail + shares] + inserted[:, tail + shares : tail + 2 * shares]
    back = []
    for w in range(shares):
        regularizer = jnp.concatenate(
            [
                column(w, 2 * sub_rows + h) + column(w, 2 * sub_rows + reg_rows + h)
                for h in range(reg_rows)
            ],
            axis=0,
        )
        kernel = near[w, kernel_rows, :] if w < half else far[w - half, kernel_rows, :]
        part = inserted[:, w * SEGLEN : (w + 1) * SEGLEN].astype(bf16)
        mapped = jnp.dot(part, kernel, preferred_element_type=f32)
        mapped = mapped / (weight_sum[:, w : w + 1] + regularizer)
        if w == 0:
            volume[...] = mapped
        back.append(
            lax.dot_general(
                mapped.astype(bf16), kernel, LANES, preferred_element_type=f32
            ).astype(bf16)
        )
    back = jnp.concatenate(back, axis=1)
    slot_lane = iota((tiles, row_count), 1).astype(f32)
    for o in range(sub_rows):
        own_slots = jnp.where(slot_lane == column(0, o), 1.0, 0.0).astype(bf16)
        taken = jnp.dot(own_slots, back, preferred_element_type=f32)
        owner = jnp.broadcast_to(column(0, sub_rows + o), (tiles, SEGLEN))
        total = jnp.zeros((tiles, SEGLEN), f32)
        for w in range(shares):
            total += jnp.where(
                owner == owner_ids[w].astype(f32), taken[:, w * SEGLEN : (w + 1) * SEGLEN], 0.0
            )
        result[o * tiles : (o + 1) * tiles, :] = total
    for j in range(tiles):
        resampled[:, j * SEGLEN : (j + 1) * SEGLEN] = result[pl.ds(j, sub_rows, stride=tiles), :]


def call(kernel, inputs, outputs, scratch=(), cost=1.0, small=()):
    inside = pl.BlockSpec(memory_space=pltpu.VMEM)
    scalars = pl.BlockSpec(memory_space=pltpu.SMEM)
    return pl.pallas_call(
        kernel,
        out_shape=[jax.ShapeDtypeStruct(shape, dtype) for shape, dtype in outputs],
        in_specs=[inside] * len(inputs) + [scalars] * len(small),
        out_specs=[inside] * len(outputs),
        scratch_shapes=list(scratch),
        compiler_params=pltpu.CompilerParams(vmem_limit_bytes=40 * 2**20),
        cost_estimate=pl.CostEstimate(
            flops=int(cost * 1e9), bytes_accessed=0, transcendentals=0
        ),
    )(*inputs, *small)


def whole_plane(images, references, shifts, owners, slot_rows, interpolation, regularizer):
    ori_count, img_count = lax.axis_size("ori"), lax.axis_size("img")
    ori, img = lax.axis_index("ori"), lax.axis_index("img")
    shift_count = shifts.shape[0]
    own_images, coef = images.shape
    tiles = coef // SEGLEN
    half = ori_count // 2
    row_count = regularizer.shape[0]
    orient_count = references.shape[0]
    sub_rows = orient_count // img_count
    group_rows = own_images * ori_count
    columns = shift_count * orient_count
    orients = ori_count * sub_rows

    piece = images.reshape(own_images, tiles, SEGLEN).transpose(1, 0, 2).reshape(-1, SEGLEN)
    near, far = gather_pair(piece)

    others = [hop(piece, "img", k) for k in range(1, img_count)]
    reg_rows = regularizer.reshape(-1, SEGLEN)
    reg_hi = reg_rows.astype(bf16)
    facts = jnp.concatenate(
        [
            slot_rows.reshape(-1, SEGLEN).astype(bf16),
            owners.reshape(-1, SEGLEN).astype(bf16),
            reg_hi,
            (reg_rows - reg_hi.astype(f32)).astype(bf16),
        ],
        axis=0,
    )
    facts = jnp.pad(facts, ((0, -facts.shape[0] % 16), (0, 0)))
    parcel = jnp.concatenate(others + [interpolation.astype(bf16), facts], axis=0)

    place = jnp.arange(ori_count * 16, dtype=jnp.int32)
    step = 16 // own_images
    image = (ori ^ distance_of(place // 16, ori_count)) * own_images + place % own_images
    out_row = place % 16 // own_images * group_rows + image
    order = (jnp.arange(step * group_rows)[:, None] == out_row[None, :]).astype(bf16)
    phases = first_phases(shifts)
    turning = pltpu.VMEM(phases.shape[1:], f32)

    scores, own = call(
        functools.partial(score_kernel, shift_count),
        (near, far, order, references, phases),
        (((group_rows, columns), f32), ((group_rows, coef), bf16)),
        scratch=(turning,),
        cost=COST_SCORE,
    )
    scores_near, scores_far = gather_pair(scores)

    column = jnp.arange(columns, dtype=jnp.int32)
    orient = column % orient_count
    lane = (orient // sub_rows ^ img) * SEGLEN + column // orient_count * sub_rows + orient % sub_rows
    pick = jnp.stack(
        [
            (jnp.arange(img_count * SEGLEN)[None, :] == (lane + h * (SEGLEN // 2))[:, None]).astype(bf16)
            for h in range(2)
        ]
    )
    (messages,) = call(
        weight_kernel,
        (scores_near, scores_far, pick),
        (((img_count, half * group_rows, SEGLEN), bf16),),
        cost=COST_WEIGHT,
    )
    arrived = [messages[0]] + [hop(messages[k], "img", k) for k in range(1, img_count)]

    parcel_near, parcel_far = gather_pair(parcel)
    (everything,) = call(
        place_kernel,
        (parcel_near, parcel_far, order, own),
        (((img_count * group_rows, coef), bf16),),
        cost=COST_PLACE,
    )

    row = jnp.arange(shift_count * orients, dtype=jnp.int32)
    share = row % orients // sub_rows
    source = (
        share % half * SEGLEN
        + share // half * (SEGLEN // 2)
        + row // orients * sub_rows
        + row % sub_rows
    )
    arrange = (source[:, None] == jnp.arange(half * SEGLEN)[None, :]).astype(bf16)
    owner_ids = ori ^ distance_of(jnp.arange(ori_count, dtype=jnp.int32), ori_count)
    volume, resampled = call(
        functools.partial(volume_kernel, shift_count, (img_count - 1) * piece.shape[0]),
        (*arrived, everything, phases, arrange, parcel_near, parcel_far),
        (((row_count, SEGLEN), f32), ((sub_rows, coef), f32)),
        scratch=(
            turning,
            pltpu.VMEM((orients * tiles, SEGLEN), f32),
            pltpu.VMEM((orients * tiles, (ori_count + 1) * SEGLEN), bf16),
            pltpu.VMEM((row_count, orients * tiles), bf16),
            pltpu.VMEM((sub_rows * tiles, SEGLEN), f32),
        ),
        small=(owner_ids,),
        cost=COST_VOLUME,
    )
    return (volume, resampled)


def shards(images, references, shifts, owners, slot_rows, interpolation, regularizer):
    arguments = (images, references, shifts, owners, slot_rows, interpolation, regularizer)
    whole_bytes = images.size * 2 * lax.axis_size("img") * lax.axis_size("ori")
    if whole_bytes <= 4 * 2**20:
        return whole_plane(*arguments)
    return reduced(*arguments)


def solution(mesh):
    in_specs = (
        P(("img", "ori"), None),
        P("ori", None),
        P(),
        P(("ori", "img"), None),
        P(("ori", "img")),
        P(("ori", "img"), None),
        P(("ori", "img")),
    )
    out_specs = (P(("ori", "img"), None), P(("ori", "img"), None))
    return jax.shard_map(shards, mesh=mesh, in_specs=in_specs, out_specs=out_specs, check_vma=False)
```

```python
import functools
import math

import jax
import jax.numpy as jnp
import numpy as np
from jax import lax
from jax.experimental import pallas as pl
from jax.experimental.pallas import tpu as pltpu
from jax.sharding import PartitionSpec as P

SEGLEN = 128
grid_width = 64
image_side = 128.0
CHUNK = 256
LANES = (((1,), (1,)), ((), ()))
COST_PHASE = 12.0
COST_SCORE = 0.001
COST_WEIGHT = 0.001
COST_STACK = 0.001
COST_FETCH = 0.001
COST_CHOICE = 0.001
COST_COUNT = 0.001
COST_SLICE = 0.001
COST_NEAR = 0.001
COST_VOLUME = 0.001
bf16 = jnp.bfloat16
f32 = jnp.float32


def hop(value, axis, distance):
    pairs = [(place, place ^ distance) for place in range(lax.axis_size(axis))]
    return lax.ppermute(value, axis, pairs)


def even_distances():
    return range(2, lax.axis_size("ori"), 2)


def gather_plane(value):
    near = jnp.concatenate([value] + [hop(value, "ori", k) for k in even_distances()], axis=0)
    return jnp.concatenate([near, hop(near, "ori", 1)], axis=0)


def phase_tables(shifts, coef):
    half_len = coef // 2
    positions = jnp.arange(half_len, dtype=jnp.int32)
    freq_x = (positions % grid_width).astype(f32)
    freq_y = (positions // grid_width - half_len // grid_width // 2).astype(f32)
    angles = (
        2.0
        * math.pi
        / image_side
        * (shifts[:, 0:1] * freq_x[None, :] + shifts[:, 1:2] * freq_y[None, :])
    )
    return (jnp.cos(angles), jnp.sin(angles))


def rotate(real_part, imag_part, cosine_row, sine_row):
    rotated_re = real_part * cosine_row[None, :] - imag_part * sine_row[None, :]
    rotated_im = real_part * sine_row[None, :] + imag_part * cosine_row[None, :]
    return jnp.concatenate([rotated_re, rotated_im], axis=1).astype(bf16)


def backproject(weights_b, group_images, cosine_table, sine_table):
    half_len = group_images.shape[1] // 2
    orient_count = weights_b.shape[1]
    total_re = jnp.zeros((orient_count, half_len), f32)
    total_im = jnp.zeros((orient_count, half_len), f32)
    for s in range(cosine_table.shape[0]):
        summed = lax.dot_general(
            weights_b[:, :, s],
            group_images,
            (((0,), (0,)), ((), ())),
            preferred_element_type=f32,
        )
        sum_re = summed[:, :half_len]
        sum_im = summed[:, half_len:]
        total_re = total_re + sum_re * cosine_table[s] + sum_im * sine_table[s]
        total_im = total_im - sum_re * sine_table[s] + sum_im * cosine_table[s]
    return jnp.concatenate([total_re, total_im], axis=1)


def merge_stats(stats, distance):
    far = hop(stats, "ori", distance)
    if distance == 1:
        return far[:, ::-1]
    half = distance // 2
    return jnp.stack([far[:, :, e ^ half] for e in range(far.shape[2])], axis=2)


def join(pairs):
    peak = pairs[0][0]
    for pair in pairs[1:]:
        peak = jnp.maximum(peak, pair[0])
    total = sum(pair[1] * jnp.exp(pair[0] - peak) for pair in pairs)
    return jnp.stack([peak, total])


def reduced(images, references, shifts, owners, slot_rows, interpolation, regularizer):
    ori_count, img_count = lax.axis_size("ori"), lax.axis_size("img")
    ori, img = lax.axis_index("ori"), lax.axis_index("img")
    shift_count = shifts.shape[0]
    coef = images.shape[1]
    own_images = images.shape[0]
    segs = coef // SEGLEN
    row_count = regularizer.shape[0]
    orient_count = references.shape[0]
    sub_rows = orient_count // img_count
    half_len = coef // 2

    group_images = gather_plane(images)
    group_rows = group_images.shape[0]
    cosine_table, sine_table = phase_tables(shifts, coef)
    references = jnp.concatenate(
        [
            lax.dynamic_slice_in_dim(references, (img ^ m) * sub_rows, sub_rows, 0)
            for m in range(img_count)
        ],
        axis=0,
    )
    real_part = references[:, :half_len].astype(f32)
    imag_part = references[:, half_len:].astype(f32)
    distance = owners[:, 0] ^ ori
    place = (distance >> 1) + (distance & 1) * (ori_count // 2)
    target = place * row_count + slot_rows
    all_rows = ori_count * row_count
    chosen = (jnp.arange(all_rows, dtype=jnp.int32)[:, None] == target[None, :]).astype(bf16)

    score_list = []
    for s in range(shift_count):
        rotated = rotate(real_part, imag_part, cosine_table[s], sine_table[s])
        score_list.append(
            lax.dot_general(
                group_images, rotated, (((1,), (1,)), ((), ())), preferred_element_type=f32
            )
        )
    scores = jnp.stack(score_list, axis=2).reshape(group_rows, -1) * (2.0 / math.sqrt(coef))
    local_peak = jnp.max(scores, axis=1)
    local_total = jnp.sum(jnp.exp(scores - local_peak[:, None]), axis=1)
    stats = jnp.stack([local_peak, local_total]).reshape(2, 2, ori_count // 2, own_images)
    stats = join([stats, merge_stats(stats, 1)])
    stats = join([stats] + [merge_stats(stats, k) for k in even_distances()])
    stats = stats.reshape(2, group_rows)
    weights = jnp.exp(scores - stats[0][:, None]) / stats[1][:, None]
    weights3 = weights.reshape(group_rows, orient_count, shift_count)
    orient_mass = jnp.sum(weights3, axis=(0, 2))
    summed = backproject(weights3.astype(bf16), group_images, cosine_table, sine_table)

    blocks = summed.reshape(img_count, sub_rows, coef)
    masses = orient_mass.reshape(img_count, sub_rows, 1)
    outgoing = jnp.concatenate(
        [blocks, jnp.broadcast_to(masses, (img_count, sub_rows, SEGLEN))], axis=2
    ).astype(bf16)
    incoming = [hop(outgoing[m], "img", m).astype(f32) for m in range(1, img_count)]
    own = blocks[0] + sum(value[:, :coef] for value in incoming)
    own_mass = masses[0] + sum(value[:, coef : coef + 1] for value in incoming)
    segments = own.astype(bf16).reshape(-1, SEGLEN)
    seg_mass = jnp.repeat(own_mass[:, 0], segs)[None, :]

    part = jnp.dot(chosen, segments, preferred_element_type=f32)
    part_mass = lax.dot_general(
        seg_mass.astype(bf16), chosen, (((1,), (1,)), ((), ())), preferred_element_type=f32
    )
    mass_rows = max(16, row_count // SEGLEN)
    part_mass = part_mass.reshape(ori_count, row_count)
    part_mass = jnp.pad(part_mass, ((0, 0), (0, mass_rows * SEGLEN - row_count)))
    parcel = jnp.concatenate(
        [part.reshape(ori_count, row_count, SEGLEN), part_mass.reshape(ori_count, -1, SEGLEN)], axis=1
    ).astype(bf16)
    half = ori_count // 2
    parcel = parcel[:half].astype(f32) + hop(parcel[half:], "ori", 1).astype(f32)
    small = parcel.astype(bf16)
    brick = parcel[0] + sum(hop(small[k // 2], "ori", k).astype(f32) for k in even_distances())
    inserted = brick[:row_count]
    weight_sum = brick[row_count:].reshape(-1)[:row_count]
    mapped = jnp.dot(
        inserted, interpolation, precision=lax.Precision.HIGHEST, preferred_element_type=f32
    )
    volume = mapped / (weight_sum + regularizer)[:, None]
    back_values = lax.dot_general(
        volume,
        interpolation,
        (((1,), (1,)), ((), ())),
        precision=lax.Precision.HIGHEST,
        preferred_element_type=f32,
    )
    bricks = gather_plane(back_values.astype(bf16))
    resampled = lax.dot_general(
        chosen, bricks, (((0,), (0,)), ((), ())), preferred_element_type=f32
    )
    return (volume, resampled.reshape(sub_rows, coef))


def iota(shape, axis):
    return lax.broadcasted_iota(jnp.int32, shape, axis)


def distance_of(place, shares):
    half = shares // 2
    if isinstance(place, int):
        return 2 * place if place < half else 2 * (place - half) + 1
    return jnp.where(place < half, 2 * place, 2 * (place - half) + 1)


def gather_pair(value, *after, own=None):
    parts = [value if own is None else own]
    parts += [hop(value, "ori", k) for k in even_distances()]
    (near,) = call(
        functools.partial(stack_kernel, len(parts)),
        (*parts, *after),
        (((len(parts), *value.shape), value.dtype),),
        cost=COST_STACK,
    )
    return near, hop(near, "ori", 1)


def stack_kernel(count, *refs):
    for place in range(count):
        refs[-1][place] = refs[place][...]


def phase_kernel(shifts, place, phases, tables):
    count = shifts.shape[0]
    unit = 2.0 * math.pi / image_side
    moves = unit * shifts[...]

    def angles(start, positions):
        lane = iota((count, positions), 1)
        freq_x = (lane % grid_width).astype(f32)
        freq_y = (lane // grid_width + start).astype(f32) - image_side / 2
        return moves[:, 0:1] * freq_x + moves[:, 1:2] * freq_y

    first = angles(0, CHUNK)
    step = jnp.broadcast_to(moves[:, 1:2] * float(CHUNK // grid_width), (count, CHUNK))
    phases[...] = jnp.zeros(phases.shape, f32)
    for h, angle in enumerate((first, step)):
        phases[0, h, :count, :] = jnp.cos(angle)
        phases[1, h, :count, :] = jnp.sin(angle)
    length = tables.shape[2]
    angle = angles(place[0] * (length // grid_width), length)
    tables[...] = jnp.zeros(tables.shape, f32)
    tables[0, :count, :] = jnp.cos(angle)
    tables[1, :count, :] = jnp.sin(angle)


def turn(phases, now):
    cosine, sine = now[0], now[1]
    cos_step, sin_step = phases[0, 1], phases[1, 1]
    now[0] = cosine * cos_step - sine * sin_step
    now[1] = sine * cos_step + cosine * sin_step


def place_order(ori, shares, group_rows):
    own_images = group_rows // shares
    rows = 16 // own_images * group_rows
    out_row, in_row = iota((rows, 16 * shares), 0), iota((rows, 16 * shares), 1)
    share, part = in_row // 16, in_row % 16
    image = (distance_of(share, shares) ^ ori) * own_images + part % own_images
    return jnp.where(out_row == part // own_images * group_rows + image, 1.0, 0.0).astype(bf16)


def place_images(near, far, ori, out):
    shares, group_rows = 2 * near.shape[0], out.shape[0]
    step = 16 * shares // group_rows
    order = place_order(ori, shares, group_rows)
    for q in range(out.shape[1] // SEGLEN // step):
        rows = slice(16 * q, 16 * q + 16)
        block = jnp.concatenate([near[:, rows, :], far[:, rows, :]], axis=0)
        block = block.reshape(shares * 16, SEGLEN)
        placed = jnp.dot(order, block, preferred_element_type=f32).astype(bf16)
        for jj in range(step):
            lanes = pl.ds((q * step + jj) * SEGLEN, SEGLEN)
            out[:, lanes] = placed[jj * group_rows : (jj + 1) * group_rows]


def score_kernel(
    shift_count,
    near,
    far,
    references,
    phases,
    slots,
    owners,
    regularizer,
    place,
    message,
    piece,
    own,
    now,
):
    group_rows, coef = own.shape
    half_len = coef // 2
    place_images(near, far, place[0], own)
    tiles = piece.shape[0] // group_rows // 2
    for h in range(2):
        for t in range(tiles):
            first = h * half_len + (place[0] * tiles + t) * SEGLEN
            row = (h * tiles + t) * group_rows
            piece[row : row + group_rows, :] = own[:, pl.ds(pl.multiple_of(first, SEGLEN), SEGLEN)]
    now[0] = phases[0, 0]
    now[1] = phases[1, 0]

    def step(t, total):
        re_lanes = pl.ds(pl.multiple_of(t * CHUNK, CHUNK), CHUNK)
        im_lanes = pl.ds(pl.multiple_of(half_len + t * CHUNK, CHUNK), CHUNK)
        real_part = references[:, re_lanes].astype(f32)
        imag_part = references[:, im_lanes].astype(f32)
        rotated_re, rotated_im = [], []
        for s in range(shift_count):
            c, d = now[0, s : s + 1, :], now[1, s : s + 1, :]
            rotated_re.append((real_part * c - imag_part * d).astype(bf16))
            rotated_im.append((real_part * d + imag_part * c).astype(bf16))
        total += lax.dot_general(
            jnp.concatenate(rotated_re, axis=0), own[:, re_lanes], LANES, preferred_element_type=f32
        )
        total += lax.dot_general(
            jnp.concatenate(rotated_im, axis=0), own[:, im_lanes], LANES, preferred_element_type=f32
        )
        turn(phases, now)
        return total

    columns = shift_count * references.shape[0]
    total = lax.fori_loop(
        0, half_len // CHUNK, step, jnp.zeros((columns, group_rows), f32), unroll=True
    )
    message[...] = jnp.zeros(message.shape, f32)
    message[:group_rows, :columns] = jnp.swapaxes(total, 0, 1) * (2.0 / math.sqrt(coef))
    row = group_rows
    for fact in (slots, owners, regularizer):
        message[row : row + fact.shape[0], :SEGLEN] = fact[...].astype(f32)
        row += fact.shape[0]


def in_order(near, far, place, rows, out):
    half = near.shape[0]
    for p in range(2 * half):
        part = near[p, rows, :] if p < half else far[p - half, rows, :]
        out[place[0] ^ distance_of(p, 2 * half)] = part


def weight_kernel(group_rows, columns, near, far, pick, piece, place, *refs):
    *messages, scores, picked = refs
    shares = scores.shape[0]
    half = shares // 2
    in_order(near, far, place, slice(0, group_rows), scores)
    parts = [scores[p, :, :columns] for p in range(shares)]
    peak = jnp.max(parts[0], axis=1, keepdims=True)
    for part in parts[1:]:
        peak = jnp.maximum(peak, jnp.max(part, axis=1, keepdims=True))
    exponents = [jnp.exp(part - peak) for part in parts]
    total = sum(jnp.sum(part, axis=1, keepdims=True) for part in exponents)
    weights = [(part / total).astype(bf16) for part in exponents]
    picked[...] = jnp.dot(
        jnp.concatenate(weights[:half], axis=0), pick[0], preferred_element_type=f32
    ) + jnp.dot(jnp.concatenate(weights[half:], axis=0), pick[1], preferred_element_type=f32)
    for k, message in enumerate(messages):
        lanes = pl.ds(pl.multiple_of((place[1] ^ k) * SEGLEN, SEGLEN), SEGLEN)
        message[: picked.shape[0], :] = picked[:, lanes].astype(bf16)
        message[picked.shape[0] :, :] = piece[...]


def flat_facts(group_rows, sub_rows, near, far, place, reg_rows, ordered, upright, flat):
    shares = ordered.shape[0]
    orients = shares * sub_rows
    blocks = flat.shape[1]
    lot = SEGLEN // orients
    in_order(near, far, place, slice(group_rows, near.shape[1]), ordered)

    def rows_of(first, count):
        return [ordered[p, first : first + count, :SEGLEN] for p in range(shares)]

    facts = rows_of(0, sub_rows) + rows_of(sub_rows, sub_rows)
    for h in range(reg_rows):
        facts += rows_of(2 * sub_rows + h, 1)
    used = 2 * orients + shares * reg_rows
    facts = jnp.concatenate(facts + [jnp.zeros((SEGLEN - used, SEGLEN), f32)], axis=0)
    upright[...] = jnp.swapaxes(facts, 0, 1)
    parts = [upright[pl.ds(b, blocks, stride=lot), :] for b in range(lot)]
    for h in range(2):
        lanes = slice(h * orients, (h + 1) * orients)
        flat[h] = jnp.concatenate([part[:, lanes] for part in parts], axis=1)
    run = blocks // (2 * shares)
    taken = []
    for p in range(shares):
        share = place[0] ^ distance_of(p, shares)
        taken += [h * (blocks // 2) + share * run + i for h in range(2) for i in range(run)]
    slots = jnp.concatenate([flat[0, pl.ds(a, 1), :] for a in taken], axis=0)
    owners = jnp.concatenate([flat[1, pl.ds(a, 1), :] for a in taken], axis=0)
    return slots, owners


def choice_kernel(
    group_rows,
    sub_rows,
    near,
    far,
    after,
    place,
    chosen,
    own_slots,
    own_owner_lanes,
    ordered,
    upright,
    flat,
):
    shares = ordered.shape[0]
    row_count = own_slots.shape[1]
    tiles = SEGLEN
    slots, owners = flat_facts(group_rows, sub_rows, near, far, place, 0, ordered, upright, flat)
    target = (owners.astype(jnp.int32) // 2).astype(f32) * float(row_count) + slots
    pair_row = iota((chosen.shape[0], SEGLEN), 0).astype(f32)
    for a in range(flat.shape[1]):
        block = slice(a * SEGLEN, (a + 1) * SEGLEN)
        chosen[:, block] = jnp.where(pair_row == target[a : a + 1, :], 1.0, 0.0).astype(bf16)
    own = near[0, group_rows : near.shape[1], :SEGLEN]
    own = jnp.concatenate([own, jnp.zeros((SEGLEN - own.shape[0], SEGLEN), f32)], axis=0)
    own = jnp.swapaxes(own, 0, 1)
    slot_lane = iota((tiles, row_count), 1).astype(f32)
    for o in range(sub_rows):
        rows = slice(o * tiles, (o + 1) * tiles)
        own_slots[rows, :] = jnp.where(slot_lane == own[:, o : o + 1], 1.0, 0.0).astype(bf16)
        own_owner_lanes[rows, :] = jnp.broadcast_to(
            own[:, sub_rows + o : sub_rows + o + 1], (tiles, SEGLEN)
        ).astype(bf16)


def count_kernel(
    group_rows,
    sub_rows,
    near,
    far,
    after,
    place,
    parity_lanes,
    counts,
    regularizer,
    ordered,
    upright,
    flat,
):
    shares = ordered.shape[0]
    row_count = regularizer.shape[0]
    reg_rows = row_count // SEGLEN
    orients = shares * sub_rows
    blocks = flat.shape[1]
    slots, owners = flat_facts(
        group_rows, sub_rows, near, far, place, reg_rows, ordered, upright, flat
    )
    for h in range(reg_rows):
        first = 2 * orients + h * shares
        regularizer[h * SEGLEN : (h + 1) * SEGLEN, :] = upright[:, first : first + shares]
    parity = (owners.astype(jnp.int32) % 2).astype(f32)
    columns = jnp.concatenate(
        [owners, parity, jnp.zeros((SEGLEN - 2 * blocks, SEGLEN), f32)], axis=0
    )
    columns = jnp.swapaxes(columns, 0, 1)
    slot_row = iota((row_count, SEGLEN), 0).astype(f32)
    count_lane = iota((SEGLEN, shares * orients), 1)
    lane_owner = (count_lane // orients).astype(f32)
    same = iota((SEGLEN, shares * orients), 0) % orients == count_lane % orients
    total = jnp.zeros((row_count, shares * orients), f32)
    for a in range(0, blocks, 2):
        slot_chosen, owned = [], []
        for b in (a, a + 1):
            block = slice(b * SEGLEN, (b + 1) * SEGLEN)
            parity_lanes[block, :] = jnp.broadcast_to(
                columns[:, blocks + b : blocks + b + 1], (SEGLEN, SEGLEN)
            ).astype(bf16)
            slot_chosen.append(jnp.where(slot_row == slots[b : b + 1, :], 1.0, 0.0).astype(bf16))
            holds = jnp.where(columns[:, b : b + 1] == lane_owner, 1.0, 0.0)
            owned.append(jnp.where(same, holds, 0.0).astype(bf16))
        total += jnp.dot(
            jnp.concatenate(slot_chosen, axis=1),
            jnp.concatenate(owned, axis=0),
            preferred_element_type=f32,
        )
    counts[...] = total.astype(bf16)


def slice_kernel(shift_count, group_rows, *refs):
    *messages, tables, arrange, kernel, after, segments, masses = refs
    length = tables.shape[2]
    half = arrange.shape[1] // SEGLEN
    orients = arrange.shape[0] // shift_count
    lot = CHUNK // SEGLEN

    stacked = jnp.concatenate(
        [
            jnp.concatenate(
                [message[a * group_rows : (a + 1) * group_rows, :] for message in messages], axis=0
            )
            for a in range(half)
        ],
        axis=1,
    )
    weights = lax.dot_general(arrange[...], stacked, LANES, preferred_element_type=f32)
    mass = jnp.sum(weights, axis=1, keepdims=True)
    mass = sum(mass[s * orients : (s + 1) * orients] for s in range(shift_count))
    masses[...] = jnp.broadcast_to(mass, masses.shape)
    weights = weights.astype(bf16)

    def images_at(tile):
        row = (half + tile) * group_rows
        return jnp.concatenate([message[row : row + group_rows, :] for message in messages], axis=0)

    for t in range(length // CHUNK):
        lanes = slice(t * CHUNK, (t + 1) * CHUNK)
        tiles = range(t * lot, (t + 1) * lot)
        real_part = jnp.concatenate([images_at(j) for j in tiles], axis=1)
        imag_part = jnp.concatenate([images_at(length // SEGLEN + j) for j in tiles], axis=1)
        summed_re = jnp.dot(weights, real_part, preferred_element_type=f32)
        summed_im = jnp.dot(weights, imag_part, preferred_element_type=f32)
        total_re = jnp.zeros((orients, CHUNK), f32)
        total_im = jnp.zeros((orients, CHUNK), f32)
        for s in range(shift_count):
            c, d = tables[0, s : s + 1, lanes], tables[1, s : s + 1, lanes]
            part_re = summed_re[s * orients : (s + 1) * orients]
            part_im = summed_im[s * orients : (s + 1) * orients]
            total_re += part_re * c + part_im * d
            total_im += part_im * c - part_re * d
        for h in range(lot):
            lanes = slice(h * SEGLEN, (h + 1) * SEGLEN)
            row = (t * lot + h) * orients
            segments[row : row + orients, :] = total_re[:, lanes].astype(bf16)
            row += length // SEGLEN * orients
            segments[row : row + orients, :] = total_im[:, lanes].astype(bf16)
    segments[2 * (length // SEGLEN) * orients :, :] = kernel[...].astype(bf16)


def insert(shares, first, chosen, parity_lanes, segments):
    rows = segments.shape[0] // shares.shape[0]
    zero = jnp.zeros((rows, SEGLEN), bf16)
    for p in range(shares.shape[0]):
        part = shares[p, :rows, :]
        parity = parity_lanes[(first + p) * rows : (first + p + 1) * rows, :]
        for w in range(2):
            segments[p * rows : (p + 1) * rows, w * SEGLEN : (w + 1) * SEGLEN] = jnp.where(
                parity == float(w), part, zero
            )
    lanes = slice(first * rows, (first + shares.shape[0]) * rows)
    return jnp.dot(chosen[:, lanes], segments[...], preferred_element_type=f32)


def near_kernel(
    near, chosen, parity_lanes, counts, regularizer, masses, inserted, inverse, segments
):
    inserted[...] = insert(near, 0, chosen, parity_lanes, segments)
    shares = regularizer.shape[1]
    mass = masses[...]
    mass_hi = mass.astype(bf16).astype(f32)
    lane = iota(mass.shape, 1)
    both = jnp.where(lane < shares, mass_hi, jnp.where(lane < 2 * shares, mass - mass_hi, 0.0))
    spread = jnp.concatenate([jnp.where(lane % shares == w, both, 0.0) for w in range(shares)], axis=0)
    weight_sum = jnp.dot(counts[...], spread.astype(bf16), preferred_element_type=f32)
    weight_sum = weight_sum[:, :shares] + weight_sum[:, shares : 2 * shares]
    inverse[...] = 1.0 / (weight_sum + regularizer[...])


def volume_kernel(
    near,
    far,
    near_inserted,
    chosen,
    parity_lanes,
    inverse,
    own_slots,
    own_owner_lanes,
    place,
    volume,
    resampled,
    segments,
    mapped,
    result,
):
    half = near.shape[0]
    shares = 2 * half
    rows = segments.shape[0] // half
    row_count = volume.shape[0]
    sub_rows = resampled.shape[0]
    tiles = resampled.shape[1] // SEGLEN
    inserted = insert(far, half, chosen, parity_lanes, segments) + near_inserted[...]
    inserted = inserted.astype(bf16)
    kernels = [near[p, rows:, :] for p in range(half)] + [far[p, rows:, :] for p in range(half)]
    for p in range(shares):
        mapped_at = place[0] ^ distance_of(p, shares)
        mapped[mapped_at] = kernels[p]
    back = []
    for w in range(shares):
        kernel = mapped[w]
        part = inserted[
            w // 2 * row_count : (w // 2 + 1) * row_count, w % 2 * SEGLEN : (w % 2 + 1) * SEGLEN
        ]
        brick = jnp.dot(part, kernel, preferred_element_type=f32) * inverse[:, w : w + 1]

        @pl.when(place[0] == w)
        def _():
            volume[...] = brick

        back.append(
            lax.dot_general(
                brick.astype(bf16), kernel, LANES, preferred_element_type=f32
            ).astype(bf16)
        )
    taken = jnp.dot(own_slots[...], jnp.concatenate(back, axis=1), preferred_element_type=f32)
    owner = own_owner_lanes[...].astype(f32)
    total = jnp.zeros((sub_rows * tiles, SEGLEN), f32)
    for w in range(shares):
        total = jnp.where(owner == float(w), taken[:, w * SEGLEN : (w + 1) * SEGLEN], total)
    result[...] = total
    for j in range(tiles):
        resampled[:, j * SEGLEN : (j + 1) * SEGLEN] = result[pl.ds(j, sub_rows, stride=tiles), :]


def call(kernel, inputs, outputs, scratch=(), cost=1.0, small=(), space=pltpu.VMEM, room=24):
    inside = pl.BlockSpec(memory_space=pltpu.VMEM)
    scalars = pl.BlockSpec(memory_space=pltpu.SMEM)
    return pl.pallas_call(
        kernel,
        out_shape=[jax.ShapeDtypeStruct(shape, dtype) for shape, dtype in outputs],
        in_specs=[pl.BlockSpec(memory_space=space)] * len(inputs) + [scalars] * len(small),
        out_specs=[inside] * len(outputs),
        scratch_shapes=list(scratch),
        compiler_params=pltpu.CompilerParams(vmem_limit_bytes=room * 2**20),
        cost_estimate=pl.CostEstimate(
            flops=int(cost * 1.15e9), bytes_accessed=0, transcendentals=0
        ),
    )(*inputs, *small)


def whole_plane(images, references, shifts, owners, slot_rows, interpolation, regularizer):
    ori_count, img_count = lax.axis_size("ori"), lax.axis_size("img")
    ori, img = lax.axis_index("ori"), lax.axis_index("img")
    shift_count = shifts.shape[0]
    own_images, coef = images.shape
    tiles = coef // SEGLEN
    half = ori_count // 2
    row_count = regularizer.shape[0]
    orient_count = references.shape[0]
    sub_rows = orient_count // img_count
    group_rows = own_images * ori_count
    columns = shift_count * orient_count
    orients = ori_count * sub_rows
    length = coef // 2 // ori_count
    place = jnp.stack([ori, img]).astype(jnp.int32)

    piece = images.reshape(own_images, tiles, SEGLEN).transpose(1, 0, 2).reshape(-1, SEGLEN)
    column = np.arange(columns)
    orient = column % orient_count
    lane = orient // sub_rows * SEGLEN + column // orient_count * sub_rows + orient % sub_rows
    pick = np.stack([lane + h * (SEGLEN // 2) for h in range(2)])[:, :, None]
    pick = jnp.asarray(pick == np.arange(img_count * SEGLEN), bf16)
    row = np.arange(shift_count * orients)
    share = row % orients // sub_rows
    source = share % half * SEGLEN + share // half * (SEGLEN // 2)
    source += row // orients * sub_rows + row % sub_rows
    arrange = jnp.asarray(source[:, None] == np.arange(half * SEGLEN), bf16)
    phases, tables = call(
        phase_kernel,
        (shifts,),
        (((2, 2, -(-shift_count // 8) * 8, CHUNK), f32), ((2, -(-shift_count // 8) * 8, length), f32)),
        small=(place,),
        cost=COST_PHASE,
    )
    near, far = gather_pair(piece, phases)
    message_rows = group_rows + 16
    message_lanes = -(-columns // SEGLEN) * SEGLEN
    scores, part = call(
        functools.partial(score_kernel, shift_count),
        (
            near,
            far,
            references,
            phases,
            slot_rows.reshape(-1, SEGLEN),
            owners.reshape(-1, SEGLEN),
            regularizer.reshape(-1, SEGLEN),
        ),
        (((message_rows, message_lanes), f32), ((2 * length // SEGLEN * group_rows, SEGLEN), bf16)),
        scratch=(pltpu.VMEM((group_rows, coef), bf16), pltpu.VMEM(phases.shape[1:], f32)),
        small=(place,),
        cost=COST_SCORE,
    )
    near, far = gather_pair(scores)

    messages = call(
        functools.partial(weight_kernel, group_rows, columns),
        (near, far, pick, part),
        (((half * group_rows + part.shape[0], SEGLEN), bf16),) * img_count,
        scratch=(
            pltpu.VMEM((ori_count, group_rows, message_lanes), f32),
            pltpu.VMEM((half * group_rows, img_count * SEGLEN), f32),
        ),
        small=(place,),
        cost=COST_WEIGHT,
    )
    arrived = [messages[0]] + [hop(messages[k], "img", k) for k in range(1, img_count)]

    fact_scratch = (
        pltpu.VMEM((ori_count, 16, message_lanes), f32),
        pltpu.VMEM((SEGLEN, SEGLEN), f32),
        pltpu.VMEM((2, orients * tiles // SEGLEN, SEGLEN), f32),
    )
    parity_lanes, counts, regs = call(
        functools.partial(count_kernel, group_rows, sub_rows),
        (near, far, messages[0]),
        (
            ((orients * tiles, SEGLEN), bf16),
            ((row_count, ori_count * orients), bf16),
            ((row_count, ori_count), f32),
        ),
        scratch=fact_scratch,
        small=(place,),
        cost=COST_COUNT,
    )
    rows = 2 * (length // SEGLEN) * orients
    segments, masses = call(
        functools.partial(slice_kernel, shift_count, group_rows),
        (*arrived, tables, arrange, interpolation, regs),
        (((rows + SEGLEN, SEGLEN), bf16), ((orients, SEGLEN), f32)),
        cost=COST_SLICE,
    )
    chosen, own_slots, own_owner_lanes = call(
        functools.partial(choice_kernel, group_rows, sub_rows),
        (near, far, masses),
        (
            ((half * row_count, orients * tiles), bf16),
            ((sub_rows * tiles, row_count), bf16),
            ((sub_rows * tiles, SEGLEN), bf16),
        ),
        scratch=fact_scratch,
        small=(place,),
        cost=COST_CHOICE,
    )

    near, far = gather_pair(segments, own_owner_lanes)
    masked = pltpu.VMEM((half * rows, 2 * SEGLEN), bf16)
    inserted, inverse = call(
        near_kernel,
        (near, chosen, parity_lanes, counts, regs, masses),
        (((half * row_count, 2 * SEGLEN), f32), ((row_count, ori_count), f32)),
        scratch=(masked,),
        cost=COST_NEAR,
    )
    volume, resampled = call(
        volume_kernel,
        (near, far, inserted, chosen, parity_lanes, inverse, own_slots, own_owner_lanes),
        (((row_count, SEGLEN), f32), ((sub_rows, coef), f32)),
        scratch=(
            masked,
            pltpu.VMEM((ori_count, SEGLEN, SEGLEN), bf16),
            pltpu.VMEM((sub_rows * tiles, SEGLEN), f32),
        ),
        small=(place,),
        cost=COST_VOLUME,
    )
    return (volume, resampled)


def shards(images, references, shifts, owners, slot_rows, interpolation, regularizer):
    arguments = (images, references, shifts, owners, slot_rows, interpolation, regularizer)
    whole_bytes = images.size * 2 * lax.axis_size("img") * lax.axis_size("ori")
    if whole_bytes <= 4 * 2**20:
        return whole_plane(*arguments)
    return reduced(*arguments)


def solution(mesh):
    in_specs = (
        P(("img", "ori"), None),
        P("ori", None),
        P(),
        P(("ori", "img"), None),
        P(("ori", "img")),
        P(("ori", "img"), None),
        P(("ori", "img")),
    )
    out_specs = (P(("ori", "img"), None), P(("ori", "img"), None))
    return jax.shard_map(shards, mesh=mesh, in_specs=in_specs, out_specs=out_specs, check_vma=False)
```

```python
import functools
import math

import jax
import jax.numpy as jnp
import numpy as np
from jax import lax
from jax.experimental import pallas as pl
from jax.experimental.pallas import tpu as pltpu
from jax.sharding import PartitionSpec as P

SEGLEN = 128
grid_width = 64
image_side = 128.0
CHUNK = 256
LANES = (((1,), (1,)), ((), ()))
COST_PHASE = 12.0
COST_SCORE = 0.001
COST_WEIGHT = 0.001
COST_STACK = 0.001
COST_FETCH = 0.001
COST_CHOICE = 0.001
COST_COUNT = 0.001
COST_SLICE = 0.001
COST_NEAR = 0.001
COST_VOLUME = 0.001
bf16 = jnp.bfloat16
f32 = jnp.float32


def hop(value, axis, distance):
    pairs = [(place, place ^ distance) for place in range(lax.axis_size(axis))]
    return lax.ppermute(value, axis, pairs)


def even_distances():
    return range(2, lax.axis_size("ori"), 2)


def gather_plane(value):
    near = jnp.concatenate([value] + [hop(value, "ori", k) for k in even_distances()], axis=0)
    return jnp.concatenate([near, hop(near, "ori", 1)], axis=0)


def phase_tables(shifts, coef):
    half_len = coef // 2
    positions = jnp.arange(half_len, dtype=jnp.int32)
    freq_x = (positions % grid_width).astype(f32)
    freq_y = (positions // grid_width - half_len // grid_width // 2).astype(f32)
    angles = (
        2.0
        * math.pi
        / image_side
        * (shifts[:, 0:1] * freq_x[None, :] + shifts[:, 1:2] * freq_y[None, :])
    )
    return (jnp.cos(angles), jnp.sin(angles))


def rotate(real_part, imag_part, cosine_row, sine_row):
    rotated_re = real_part * cosine_row[None, :] - imag_part * sine_row[None, :]
    rotated_im = real_part * sine_row[None, :] + imag_part * cosine_row[None, :]
    return jnp.concatenate([rotated_re, rotated_im], axis=1).astype(bf16)


def backproject(weights_b, group_images, cosine_table, sine_table):
    half_len = group_images.shape[1] // 2
    orient_count = weights_b.shape[1]
    total_re = jnp.zeros((orient_count, half_len), f32)
    total_im = jnp.zeros((orient_count, half_len), f32)
    for s in range(cosine_table.shape[0]):
        summed = lax.dot_general(
            weights_b[:, :, s],
            group_images,
            (((0,), (0,)), ((), ())),
            preferred_element_type=f32,
        )
        sum_re = summed[:, :half_len]
        sum_im = summed[:, half_len:]
        total_re = total_re + sum_re * cosine_table[s] + sum_im * sine_table[s]
        total_im = total_im - sum_re * sine_table[s] + sum_im * cosine_table[s]
    return jnp.concatenate([total_re, total_im], axis=1)


def merge_stats(stats, distance):
    far = hop(stats, "ori", distance)
    if distance == 1:
        return far[:, ::-1]
    half = distance // 2
    return jnp.stack([far[:, :, e ^ half] for e in range(far.shape[2])], axis=2)


def join(pairs):
    peak = pairs[0][0]
    for pair in pairs[1:]:
        peak = jnp.maximum(peak, pair[0])
    total = sum(pair[1] * jnp.exp(pair[0] - peak) for pair in pairs)
    return jnp.stack([peak, total])


def reduced(images, references, shifts, owners, slot_rows, interpolation, regularizer):
    ori_count, img_count = lax.axis_size("ori"), lax.axis_size("img")
    ori, img = lax.axis_index("ori"), lax.axis_index("img")
    shift_count = shifts.shape[0]
    coef = images.shape[1]
    own_images = images.shape[0]
    segs = coef // SEGLEN
    row_count = regularizer.shape[0]
    orient_count = references.shape[0]
    sub_rows = orient_count // img_count
    half_len = coef // 2

    group_images = gather_plane(images)
    group_rows = group_images.shape[0]
    cosine_table, sine_table = phase_tables(shifts, coef)
    references = jnp.concatenate(
        [
            lax.dynamic_slice_in_dim(references, (img ^ m) * sub_rows, sub_rows, 0)
            for m in range(img_count)
        ],
        axis=0,
    )
    real_part = references[:, :half_len].astype(f32)
    imag_part = references[:, half_len:].astype(f32)
    distance = owners[:, 0] ^ ori
    place = (distance >> 1) + (distance & 1) * (ori_count // 2)
    target = place * row_count + slot_rows
    all_rows = ori_count * row_count
    chosen = (jnp.arange(all_rows, dtype=jnp.int32)[:, None] == target[None, :]).astype(bf16)

    score_list = []
    for s in range(shift_count):
        rotated = rotate(real_part, imag_part, cosine_table[s], sine_table[s])
        score_list.append(
            lax.dot_general(
                group_images, rotated, (((1,), (1,)), ((), ())), preferred_element_type=f32
            )
        )
    scores = jnp.stack(score_list, axis=2).reshape(group_rows, -1) * (2.0 / math.sqrt(coef))
    local_peak = jnp.max(scores, axis=1)
    local_total = jnp.sum(jnp.exp(scores - local_peak[:, None]), axis=1)
    stats = jnp.stack([local_peak, local_total]).reshape(2, 2, ori_count // 2, own_images)
    stats = join([stats, merge_stats(stats, 1)])
    stats = join([stats] + [merge_stats(stats, k) for k in even_distances()])
    stats = stats.reshape(2, group_rows)
    weights = jnp.exp(scores - stats[0][:, None]) / stats[1][:, None]
    weights3 = weights.reshape(group_rows, orient_count, shift_count)
    orient_mass = jnp.sum(weights3, axis=(0, 2))
    summed = backproject(weights3.astype(bf16), group_images, cosine_table, sine_table)

    blocks = summed.reshape(img_count, sub_rows, coef)
    masses = orient_mass.reshape(img_count, sub_rows, 1)
    outgoing = jnp.concatenate(
        [blocks, jnp.broadcast_to(masses, (img_count, sub_rows, SEGLEN))], axis=2
    ).astype(bf16)
    incoming = [hop(outgoing[m], "img", m).astype(f32) for m in range(1, img_count)]
    own = blocks[0] + sum(value[:, :coef] for value in incoming)
    own_mass = masses[0] + sum(value[:, coef : coef + 1] for value in incoming)
    segments = own.astype(bf16).reshape(-1, SEGLEN)
    seg_mass = jnp.repeat(own_mass[:, 0], segs)[None, :]

    part = jnp.dot(chosen, segments, preferred_element_type=f32)
    part_mass = lax.dot_general(
        seg_mass.astype(bf16), chosen, (((1,), (1,)), ((), ())), preferred_element_type=f32
    )
    mass_rows = max(16, row_count // SEGLEN)
    part_mass = part_mass.reshape(ori_count, row_count)
    part_mass = jnp.pad(part_mass, ((0, 0), (0, mass_rows * SEGLEN - row_count)))
    parcel = jnp.concatenate(
        [part.reshape(ori_count, row_count, SEGLEN), part_mass.reshape(ori_count, -1, SEGLEN)], axis=1
    ).astype(bf16)
    half = ori_count // 2
    parcel = parcel[:half].astype(f32) + hop(parcel[half:], "ori", 1).astype(f32)
    small = parcel.astype(bf16)
    brick = parcel[0] + sum(hop(small[k // 2], "ori", k).astype(f32) for k in even_distances())
    inserted = brick[:row_count]
    weight_sum = brick[row_count:].reshape(-1)[:row_count]
    mapped = jnp.dot(
        inserted, interpolation, precision=lax.Precision.HIGHEST, preferred_element_type=f32
    )
    volume = mapped / (weight_sum + regularizer)[:, None]
    back_values = lax.dot_general(
        volume,
        interpolation,
        (((1,), (1,)), ((), ())),
        precision=lax.Precision.HIGHEST,
        preferred_element_type=f32,
    )
    bricks = gather_plane(back_values.astype(bf16))
    resampled = lax.dot_general(
        chosen, bricks, (((0,), (0,)), ((), ())), preferred_element_type=f32
    )
    return (volume, resampled.reshape(sub_rows, coef))


def iota(shape, axis):
    return lax.broadcasted_iota(jnp.int32, shape, axis)


def distance_of(place, shares):
    half = shares // 2
    if isinstance(place, int):
        return 2 * place if place < half else 2 * (place - half) + 1
    return jnp.where(place < half, 2 * place, 2 * (place - half) + 1)


def gather_pair(value, *after, own=None):
    parts = [value if own is None else own]
    parts += [hop(value, "ori", k) for k in even_distances()]
    (near,) = call(
        functools.partial(stack_kernel, len(parts)),
        (*parts, *after),
        (((len(parts), *value.shape), value.dtype),),
        cost=COST_STACK,
    )
    return near, hop(near, "ori", 1)


def stack_kernel(count, *refs):
    for place in range(count):
        refs[-1][place] = refs[place][...]


def phase_kernel(shifts, place, phases, tables):
    count = shifts.shape[0]
    unit = 2.0 * math.pi / image_side
    moves = unit * shifts[...]

    def angles(start, positions):
        lane = iota((count, positions), 1)
        freq_x = (lane % grid_width).astype(f32)
        freq_y = (lane // grid_width + start).astype(f32) - image_side / 2
        return moves[:, 0:1] * freq_x + moves[:, 1:2] * freq_y

    first = angles(0, CHUNK)
    step = jnp.broadcast_to(moves[:, 1:2] * float(CHUNK // grid_width), (count, CHUNK))
    phases[...] = jnp.zeros(phases.shape, f32)
    for h, angle in enumerate((first, step)):
        phases[0, h, :count, :] = jnp.cos(angle)
        phases[1, h, :count, :] = jnp.sin(angle)
    length = tables.shape[2]
    angle = angles(place[0] * (length // grid_width), length)
    tables[...] = jnp.zeros(tables.shape, f32)
    tables[0, :count, :] = jnp.cos(angle)
    tables[1, :count, :] = jnp.sin(angle)


def turn(phases, now):
    cosine, sine = now[0], now[1]
    cos_step, sin_step = phases[0, 1], phases[1, 1]
    now[0] = cosine * cos_step - sine * sin_step
    now[1] = sine * cos_step + cosine * sin_step


def place_order(ori, shares, group_rows):
    own_images = group_rows // shares
    rows = 16 // own_images * group_rows
    out_row, in_row = iota((rows, 16 * shares), 0), iota((rows, 16 * shares), 1)
    share, part = in_row // 16, in_row % 16
    image = (distance_of(share, shares) ^ ori) * own_images + part % own_images
    return jnp.where(out_row == part // own_images * group_rows + image, 1.0, 0.0).astype(bf16)


def place_images(near, far, ori, out):
    shares, group_rows = 2 * near.shape[0], out.shape[0]
    step = 16 * shares // group_rows
    order = place_order(ori, shares, group_rows)
    for q in range(out.shape[1] // SEGLEN // step):
        rows = slice(16 * q, 16 * q + 16)
        block = jnp.concatenate([near[:, rows, :], far[:, rows, :]], axis=0)
        block = block.reshape(shares * 16, SEGLEN)
        placed = jnp.dot(order, block, preferred_element_type=f32).astype(bf16)
        for jj in range(step):
            lanes = pl.ds((q * step + jj) * SEGLEN, SEGLEN)
            out[:, lanes] = placed[jj * group_rows : (jj + 1) * group_rows]


def score_kernel(
    shift_count,
    near,
    far,
    references,
    phases,
    slots,
    owners,
    regularizer,
    place,
    message,
    piece,
    own,
    now,
):
    group_rows, coef = own.shape
    half_len = coef // 2
    place_images(near, far, place[0], own)
    tiles = piece.shape[0] // group_rows // 2
    for h in range(2):
        for t in range(tiles):
            first = h * half_len + (place[0] * tiles + t) * SEGLEN
            row = (h * tiles + t) * group_rows
            piece[row : row + group_rows, :] = own[:, pl.ds(pl.multiple_of(first, SEGLEN), SEGLEN)]
    now[0] = phases[0, 0]
    now[1] = phases[1, 0]

    def step(t, total):
        re_lanes = pl.ds(pl.multiple_of(t * CHUNK, CHUNK), CHUNK)
        im_lanes = pl.ds(pl.multiple_of(half_len + t * CHUNK, CHUNK), CHUNK)
        real_part = references[:, re_lanes].astype(f32)
        imag_part = references[:, im_lanes].astype(f32)
        rotated_re, rotated_im = [], []
        for s in range(shift_count):
            c, d = now[0, s : s + 1, :], now[1, s : s + 1, :]
            rotated_re.append((real_part * c - imag_part * d).astype(bf16))
            rotated_im.append((real_part * d + imag_part * c).astype(bf16))
        total += lax.dot_general(
            jnp.concatenate(rotated_re, axis=0), own[:, re_lanes], LANES, preferred_element_type=f32
        )
        total += lax.dot_general(
            jnp.concatenate(rotated_im, axis=0), own[:, im_lanes], LANES, preferred_element_type=f32
        )
        turn(phases, now)
        return total

    columns = shift_count * references.shape[0]
    total = lax.fori_loop(
        0, half_len // CHUNK, step, jnp.zeros((columns, group_rows), f32), unroll=True
    )
    message[...] = jnp.zeros(message.shape, f32)
    message[:group_rows, :columns] = jnp.swapaxes(total, 0, 1) * (2.0 / math.sqrt(coef))
    row = group_rows
    for fact in (slots, owners, regularizer):
        message[row : row + fact.shape[0], :SEGLEN] = fact[...].astype(f32)
        row += fact.shape[0]


def in_order(near, far, place, rows, out):
    half = near.shape[0]
    for p in range(2 * half):
        part = near[p, rows, :] if p < half else far[p - half, rows, :]
        out[place[0] ^ distance_of(p, 2 * half)] = part


def weight_kernel(group_rows, columns, near, far, pick, piece, place, *refs):
    *messages, scores, picked = refs
    shares = scores.shape[0]
    half = shares // 2
    in_order(near, far, place, slice(0, group_rows), scores)
    parts = [scores[p, :, :columns] for p in range(shares)]
    peak = jnp.max(parts[0], axis=1, keepdims=True)
    for part in parts[1:]:
        peak = jnp.maximum(peak, jnp.max(part, axis=1, keepdims=True))
    exponents = [jnp.exp(part - peak) for part in parts]
    total = sum(jnp.sum(part, axis=1, keepdims=True) for part in exponents)
    weights = [(part / total).astype(bf16) for part in exponents]
    picked[...] = jnp.dot(
        jnp.concatenate(weights[:half], axis=0), pick[0], preferred_element_type=f32
    ) + jnp.dot(jnp.concatenate(weights[half:], axis=0), pick[1], preferred_element_type=f32)
    for k, message in enumerate(messages):
        lanes = pl.ds(pl.multiple_of((place[1] ^ k) * SEGLEN, SEGLEN), SEGLEN)
        message[: picked.shape[0], :] = picked[:, lanes].astype(bf16)
        message[picked.shape[0] :, :] = piece[...]


def flat_facts(group_rows, sub_rows, near, far, place, reg_rows, ordered, upright, flat):
    shares = ordered.shape[0]
    orients = shares * sub_rows
    blocks = flat.shape[1]
    lot = SEGLEN // orients
    in_order(near, far, place, slice(group_rows, near.shape[1]), ordered)

    def rows_of(first, count):
        return [ordered[p, first : first + count, :SEGLEN] for p in range(shares)]

    facts = rows_of(0, sub_rows) + rows_of(sub_rows, sub_rows)
    for h in range(reg_rows):
        facts += rows_of(2 * sub_rows + h, 1)
    used = 2 * orients + shares * reg_rows
    facts = jnp.concatenate(facts + [jnp.zeros((SEGLEN - used, SEGLEN), f32)], axis=0)
    upright[...] = jnp.swapaxes(facts, 0, 1)
    parts = [upright[pl.ds(b, blocks, stride=lot), :] for b in range(lot)]
    for h in range(2):
        lanes = slice(h * orients, (h + 1) * orients)
        flat[h] = jnp.concatenate([part[:, lanes] for part in parts], axis=1)
    run = blocks // (2 * shares)
    taken = []
    for p in range(shares):
        share = place[0] ^ distance_of(p, shares)
        taken += [h * (blocks // 2) + share * run + i for h in range(2) for i in range(run)]
    slots = jnp.concatenate([flat[0, pl.ds(a, 1), :] for a in taken], axis=0)
    owners = jnp.concatenate([flat[1, pl.ds(a, 1), :] for a in taken], axis=0)
    return slots, owners


def choice_kernel(
    group_rows,
    sub_rows,
    near,
    far,
    after,
    place,
    chosen,
    own_slots,
    own_owner_lanes,
    ordered,
    upright,
    flat,
):
    shares = ordered.shape[0]
    row_count = own_slots.shape[1]
    tiles = SEGLEN
    slots, owners = flat_facts(group_rows, sub_rows, near, far, place, 0, ordered, upright, flat)
    target = (owners.astype(jnp.int32) // 2).astype(f32) * float(row_count) + slots
    pair_row = iota((chosen.shape[0], SEGLEN), 0).astype(f32)
    for a in range(flat.shape[1]):
        block = slice(a * SEGLEN, (a + 1) * SEGLEN)
        chosen[:, block] = jnp.where(pair_row == target[a : a + 1, :], 1.0, 0.0).astype(bf16)
    own = near[0, group_rows : near.shape[1], :SEGLEN]
    own = jnp.concatenate([own, jnp.zeros((SEGLEN - own.shape[0], SEGLEN), f32)], axis=0)
    own = jnp.swapaxes(own, 0, 1)
    slot_lane = iota((tiles, row_count), 1).astype(f32)
    for o in range(sub_rows):
        rows = slice(o * tiles, (o + 1) * tiles)
        own_slots[rows, :] = jnp.where(slot_lane == own[:, o : o + 1], 1.0, 0.0).astype(bf16)
        own_owner_lanes[rows, :] = jnp.broadcast_to(
            own[:, sub_rows + o : sub_rows + o + 1], (tiles, SEGLEN)
        ).astype(bf16)


def count_kernel(
    group_rows,
    sub_rows,
    near,
    far,
    after,
    place,
    parity_lanes,
    counts,
    regularizer,
    ordered,
    upright,
    flat,
):
    shares = ordered.shape[0]
    row_count = regularizer.shape[0]
    reg_rows = row_count // SEGLEN
    orients = shares * sub_rows
    blocks = flat.shape[1]
    slots, owners = flat_facts(
        group_rows, sub_rows, near, far, place, reg_rows, ordered, upright, flat
    )
    for h in range(reg_rows):
        first = 2 * orients + h * shares
        regularizer[h * SEGLEN : (h + 1) * SEGLEN, :] = upright[:, first : first + shares]
    parity = (owners.astype(jnp.int32) % 2).astype(f32)
    columns = jnp.concatenate(
        [owners, parity, jnp.zeros((SEGLEN - 2 * blocks, SEGLEN), f32)], axis=0
    )
    columns = jnp.swapaxes(columns, 0, 1)
    slot_row = iota((row_count, SEGLEN), 0).astype(f32)
    count_lane = iota((SEGLEN, shares * orients), 1)
    lane_owner = (count_lane // orients).astype(f32)
    same = iota((SEGLEN, shares * orients), 0) % orients == count_lane % orients
    total = jnp.zeros((row_count, shares * orients), f32)
    for a in range(0, blocks, 2):
        slot_chosen, owned = [], []
        for b in (a, a + 1):
            block = slice(b * SEGLEN, (b + 1) * SEGLEN)
            parity_lanes[block, :] = jnp.broadcast_to(
                columns[:, blocks + b : blocks + b + 1], (SEGLEN, SEGLEN)
            ).astype(bf16)
            slot_chosen.append(jnp.where(slot_row == slots[b : b + 1, :], 1.0, 0.0).astype(bf16))
            holds = jnp.where(columns[:, b : b + 1] == lane_owner, 1.0, 0.0)
            owned.append(jnp.where(same, holds, 0.0).astype(bf16))
        total += jnp.dot(
            jnp.concatenate(slot_chosen, axis=1),
            jnp.concatenate(owned, axis=0),
            preferred_element_type=f32,
        )
    counts[...] = total.astype(bf16)


def slice_kernel(shift_count, group_rows, *refs):
    *messages, tables, arrange, kernel, after, segments, masses = refs
    length = tables.shape[2]
    half = arrange.shape[1] // SEGLEN
    orients = arrange.shape[0] // shift_count
    lot = CHUNK // SEGLEN

    stacked = jnp.concatenate(
        [
            jnp.concatenate(
                [message[a * group_rows : (a + 1) * group_rows, :] for message in messages], axis=0
            )
            for a in range(half)
        ],
        axis=1,
    )
    weights = lax.dot_general(arrange[...], stacked, LANES, preferred_element_type=f32)
    mass = jnp.sum(weights, axis=1, keepdims=True)
    mass = sum(mass[s * orients : (s + 1) * orients] for s in range(shift_count))
    masses[...] = jnp.broadcast_to(mass, masses.shape)
    weights = weights.astype(bf16)

    def images_at(tile):
        row = (half + tile) * group_rows
        return jnp.concatenate([message[row : row + group_rows, :] for message in messages], axis=0)

    for t in range(length // CHUNK):
        lanes = slice(t * CHUNK, (t + 1) * CHUNK)
        tiles = range(t * lot, (t + 1) * lot)
        real_part = jnp.concatenate([images_at(j) for j in tiles], axis=1)
        imag_part = jnp.concatenate([images_at(length // SEGLEN + j) for j in tiles], axis=1)
        summed_re = jnp.dot(weights, real_part, preferred_element_type=f32)
        summed_im = jnp.dot(weights, imag_part, preferred_element_type=f32)
        total_re = jnp.zeros((orients, CHUNK), f32)
        total_im = jnp.zeros((orients, CHUNK), f32)
        for s in range(shift_count):
            c, d = tables[0, s : s + 1, lanes], tables[1, s : s + 1, lanes]
            part_re = summed_re[s * orients : (s + 1) * orients]
            part_im = summed_im[s * orients : (s + 1) * orients]
            total_re += part_re * c + part_im * d
            total_im += part_im * c - part_re * d
        for h in range(lot):
            lanes = slice(h * SEGLEN, (h + 1) * SEGLEN)
            row = (t * lot + h) * orients
            segments[row : row + orients, :] = total_re[:, lanes].astype(bf16)
            row += length // SEGLEN * orients
            segments[row : row + orients, :] = total_im[:, lanes].astype(bf16)
    segments[2 * (length // SEGLEN) * orients :, :] = kernel[...].astype(bf16)


def insert(shares, first, chosen, parity_lanes, segments):
    rows = segments.shape[0] // shares.shape[0]
    zero = jnp.zeros((rows, SEGLEN), bf16)
    for p in range(shares.shape[0]):
        part = shares[p, :rows, :]
        parity = parity_lanes[(first + p) * rows : (first + p + 1) * rows, :]
        for w in range(2):
            segments[p * rows : (p + 1) * rows, w * SEGLEN : (w + 1) * SEGLEN] = jnp.where(
                parity == float(w), part, zero
            )
    lanes = slice(first * rows, (first + shares.shape[0]) * rows)
    return jnp.dot(chosen[:, lanes], segments[...], preferred_element_type=f32)


def near_kernel(
    near, chosen, parity_lanes, counts, regularizer, masses, inserted, inverse, segments
):
    inserted[...] = insert(near, 0, chosen, parity_lanes, segments)
    shares = regularizer.shape[1]
    mass = masses[...]
    mass_hi = mass.astype(bf16).astype(f32)
    lane = iota(mass.shape, 1)
    both = jnp.where(lane < shares, mass_hi, jnp.where(lane < 2 * shares, mass - mass_hi, 0.0))
    spread = jnp.concatenate([jnp.where(lane % shares == w, both, 0.0) for w in range(shares)], axis=0)
    weight_sum = jnp.dot(counts[...], spread.astype(bf16), preferred_element_type=f32)
    weight_sum = weight_sum[:, :shares] + weight_sum[:, shares : 2 * shares]
    inverse[...] = 1.0 / (weight_sum + regularizer[...])


def volume_kernel(
    near,
    far,
    near_inserted,
    chosen,
    parity_lanes,
    inverse,
    own_slots,
    own_owner_lanes,
    place,
    volume,
    resampled,
    segments,
    kernels,
    bricks,
    result,
    rows_out,
    signals,
):
    half = near.shape[0]
    shares = 2 * half
    rows = segments.shape[0] // half
    row_count = bricks.shape[1]
    sub_rows, coef = rows_out.shape
    tiles = coef // SEGLEN
    kernels[...] = jnp.zeros(kernels.shape, bf16)
    for p in range(shares):
        w = place[0] ^ distance_of(p, shares)
        at = pl.ds(pl.multiple_of(w % 2 * SEGLEN, SEGLEN), SEGLEN)
        kernels[w // 2, at, at] = near[p, rows:, :] if p < half else far[p - half, rows:, :]
    inserted = insert(far, half, chosen, parity_lanes, segments) + near_inserted[...]
    inserted = inserted.astype(bf16)
    mapped = []
    for a in range(half):
        pair = jnp.dot(
            inserted[a * row_count : (a + 1) * row_count, :],
            kernels[a],
            preferred_element_type=f32,
        )
        sides = []
        for w in (2 * a, 2 * a + 1):
            side = pair[:, w % 2 * SEGLEN : (w % 2 + 1) * SEGLEN] * inverse[:, w : w + 1]
            bricks[w] = side
            sides.append(side.astype(bf16))
        mapped.append(jnp.concatenate(sides, axis=1))
    own = pltpu.make_async_copy(bricks.at[place[0]], volume, signals.at[0])
    own.start()
    back = [
        lax.dot_general(pair, kernels[a], LANES, preferred_element_type=f32).astype(bf16)
        for a, pair in enumerate(mapped)
    ]
    taken = jnp.dot(own_slots[...], jnp.concatenate(back, axis=1), preferred_element_type=f32)
    owner = own_owner_lanes[...].astype(f32)
    total = jnp.zeros((sub_rows * tiles, SEGLEN), f32)
    for w in range(shares):
        total = jnp.where(owner == float(w), taken[:, w * SEGLEN : (w + 1) * SEGLEN], total)
    result[...] = total
    for j in range(tiles):
        rows_out[:, j * SEGLEN : (j + 1) * SEGLEN] = result[pl.ds(j, sub_rows, stride=tiles), :]
    back_again = pltpu.make_async_copy(rows_out, resampled, signals.at[1])
    back_again.start()
    own.wait()
    back_again.wait()


def call(kernel, inputs, outputs, scratch=(), cost=1.0, small=(), out_space=pltpu.VMEM):
    inside = pl.BlockSpec(memory_space=pltpu.VMEM)
    scalars = pl.BlockSpec(memory_space=pltpu.SMEM)
    return pl.pallas_call(
        kernel,
        out_shape=[jax.ShapeDtypeStruct(shape, dtype) for shape, dtype in outputs],
        in_specs=[inside] * len(inputs) + [scalars] * len(small),
        out_specs=[pl.BlockSpec(memory_space=out_space)] * len(outputs),
        scratch_shapes=list(scratch),
        compiler_params=pltpu.CompilerParams(vmem_limit_bytes=24 * 2**20),
        cost_estimate=pl.CostEstimate(
            flops=int(cost * 1.15e9), bytes_accessed=0, transcendentals=0
        ),
    )(*inputs, *small)


def whole_plane(images, references, shifts, owners, slot_rows, interpolation, regularizer):
    ori_count, img_count = lax.axis_size("ori"), lax.axis_size("img")
    ori, img = lax.axis_index("ori"), lax.axis_index("img")
    shift_count = shifts.shape[0]
    own_images, coef = images.shape
    tiles = coef // SEGLEN
    half = ori_count // 2
    row_count = regularizer.shape[0]
    orient_count = references.shape[0]
    sub_rows = orient_count // img_count
    group_rows = own_images * ori_count
    columns = shift_count * orient_count
    orients = ori_count * sub_rows
    length = coef // 2 // ori_count
    place = jnp.stack([ori, img]).astype(jnp.int32)

    piece = images.reshape(own_images, tiles, SEGLEN).transpose(1, 0, 2).reshape(-1, SEGLEN)
    column = np.arange(columns)
    orient = column % orient_count
    lane = orient // sub_rows * SEGLEN + column // orient_count * sub_rows + orient % sub_rows
    pick = np.stack([lane + h * (SEGLEN // 2) for h in range(2)])[:, :, None]
    pick = jnp.asarray(pick == np.arange(img_count * SEGLEN), bf16)
    row = np.arange(shift_count * orients)
    share = row % orients // sub_rows
    source = share % half * SEGLEN + share // half * (SEGLEN // 2)
    source += row // orients * sub_rows + row % sub_rows
    arrange = jnp.asarray(source[:, None] == np.arange(half * SEGLEN), bf16)
    phases, tables = call(
        phase_kernel,
        (shifts,),
        (((2, 2, -(-shift_count // 8) * 8, CHUNK), f32), ((2, -(-shift_count // 8) * 8, length), f32)),
        small=(place,),
        cost=COST_PHASE,
    )
    near, far = gather_pair(piece, phases)
    message_rows = group_rows + 16
    message_lanes = -(-columns // SEGLEN) * SEGLEN
    scores, part = call(
        functools.partial(score_kernel, shift_count),
        (
            near,
            far,
            references,
            phases,
            slot_rows.reshape(-1, SEGLEN),
            owners.reshape(-1, SEGLEN),
            regularizer.reshape(-1, SEGLEN),
        ),
        (((message_rows, message_lanes), f32), ((2 * length // SEGLEN * group_rows, SEGLEN), bf16)),
        scratch=(pltpu.VMEM((group_rows, coef), bf16), pltpu.VMEM(phases.shape[1:], f32)),
        small=(place,),
        cost=COST_SCORE,
    )
    near, far = gather_pair(scores)

    messages = call(
        functools.partial(weight_kernel, group_rows, columns),
        (near, far, pick, part),
        (((half * group_rows + part.shape[0], SEGLEN), bf16),) * img_count,
        scratch=(
            pltpu.VMEM((ori_count, group_rows, message_lanes), f32),
            pltpu.VMEM((half * group_rows, img_count * SEGLEN), f32),
        ),
        small=(place,),
        cost=COST_WEIGHT,
    )
    arrived = [messages[0]] + [hop(messages[k], "img", k) for k in range(1, img_count)]

    fact_scratch = (
        pltpu.VMEM((ori_count, 16, message_lanes), f32),
        pltpu.VMEM((SEGLEN, SEGLEN), f32),
        pltpu.VMEM((2, orients * tiles // SEGLEN, SEGLEN), f32),
    )
    parity_lanes, counts, regs = call(
        functools.partial(count_kernel, group_rows, sub_rows),
        (near, far, messages[0]),
        (
            ((orients * tiles, SEGLEN), bf16),
            ((row_count, ori_count * orients), bf16),
            ((row_count, ori_count), f32),
        ),
        scratch=fact_scratch,
        small=(place,),
        cost=COST_COUNT,
    )
    rows = 2 * (length // SEGLEN) * orients
    segments, masses = call(
        functools.partial(slice_kernel, shift_count, group_rows),
        (*arrived, tables, arrange, interpolation, regs),
        (((rows + SEGLEN, SEGLEN), bf16), ((orients, SEGLEN), f32)),
        cost=COST_SLICE,
    )
    chosen, own_slots, own_owner_lanes = call(
        functools.partial(choice_kernel, group_rows, sub_rows),
        (near, far, masses),
        (
            ((half * row_count, orients * tiles), bf16),
            ((sub_rows * tiles, row_count), bf16),
            ((sub_rows * tiles, SEGLEN), bf16),
        ),
        scratch=fact_scratch,
        small=(place,),
        cost=COST_CHOICE,
    )

    near, far = gather_pair(segments, own_owner_lanes)
    masked = pltpu.VMEM((half * rows, 2 * SEGLEN), bf16)
    inserted, inverse = call(
        near_kernel,
        (near, chosen, parity_lanes, counts, regs, masses),
        (((half * row_count, 2 * SEGLEN), f32), ((row_count, ori_count), f32)),
        scratch=(masked,),
        cost=COST_NEAR,
    )
    volume, resampled = call(
        volume_kernel,
        (near, far, inserted, chosen, parity_lanes, inverse, own_slots, own_owner_lanes),
        (((row_count, SEGLEN), f32), ((sub_rows, coef), f32)),
        scratch=(
            masked,
            pltpu.VMEM((half, 2 * SEGLEN, 2 * SEGLEN), bf16),
            pltpu.VMEM((ori_count, row_count, SEGLEN), f32),
            pltpu.VMEM((sub_rows * tiles, SEGLEN), f32),
            pltpu.VMEM((sub_rows, coef), f32),
            pltpu.SemaphoreType.DMA((2,)),
        ),
        small=(place,),
        cost=COST_VOLUME,
        out_space=pl.ANY,
    )
    return (volume, resampled)


def shards(images, references, shifts, owners, slot_rows, interpolation, regularizer):
    arguments = (images, references, shifts, owners, slot_rows, interpolation, regularizer)
    whole_bytes = images.size * 2 * lax.axis_size("img") * lax.axis_size("ori")
    if whole_bytes <= 4 * 2**20:
        return whole_plane(*arguments)
    return reduced(*arguments)


def solution(mesh):
    in_specs = (
        P(("img", "ori"), None),
        P("ori", None),
        P(),
        P(("ori", "img"), None),
        P(("ori", "img")),
        P(("ori", "img"), None),
        P(("ori", "img")),
    )
    out_specs = (P(("ori", "img"), None), P(("ori", "img"), None))
    return jax.shard_map(shards, mesh=mesh, in_specs=in_specs, out_specs=out_specs, check_vma=False)
```

```python
import functools
import math

import jax
import jax.numpy as jnp
import numpy as np
from jax import lax
from jax.experimental import pallas as pl
from jax.experimental.pallas import tpu as pltpu
from jax.sharding import PartitionSpec as P

SEGLEN = 128
grid_width = 64
image_side = 128.0
CHUNK = 256
LANES = (((1,), (1,)), ((), ()))
COST_PHASE = 12.0
COST_SCORE = 0.001
COST_WEIGHT = 0.001
COST_STACK = 0.001
COST_BESIDE = 30.0
COST_FACT = 0.001
COST_SLICE = 0.001
COST_NEAR = 0.001
COST_VOLUME = 0.001
bf16 = jnp.bfloat16
f32 = jnp.float32


def hop(value, axis, distance):
    pairs = [(place, place ^ distance) for place in range(lax.axis_size(axis))]
    return lax.ppermute(value, axis, pairs)


def even_distances():
    return range(2, lax.axis_size("ori"), 2)


def gather_plane(value):
    near = jnp.concatenate([value] + [hop(value, "ori", k) for k in even_distances()], axis=0)
    return jnp.concatenate([near, hop(near, "ori", 1)], axis=0)


def phase_tables(shifts, coef):
    half_len = coef // 2
    positions = jnp.arange(half_len, dtype=jnp.int32)
    freq_x = (positions % grid_width).astype(f32)
    freq_y = (positions // grid_width - half_len // grid_width // 2).astype(f32)
    angles = (
        2.0
        * math.pi
        / image_side
        * (shifts[:, 0:1] * freq_x[None, :] + shifts[:, 1:2] * freq_y[None, :])
    )
    return (jnp.cos(angles), jnp.sin(angles))


def rotate(real_part, imag_part, cosine_row, sine_row):
    rotated_re = real_part * cosine_row[None, :] - imag_part * sine_row[None, :]
    rotated_im = real_part * sine_row[None, :] + imag_part * cosine_row[None, :]
    return jnp.concatenate([rotated_re, rotated_im], axis=1).astype(bf16)


def backproject(weights_b, group_images, cosine_table, sine_table):
    half_len = group_images.shape[1] // 2
    orient_count = weights_b.shape[1]
    total_re = jnp.zeros((orient_count, half_len), f32)
    total_im = jnp.zeros((orient_count, half_len), f32)
    for s in range(cosine_table.shape[0]):
        summed = lax.dot_general(
            weights_b[:, :, s],
            group_images,
            (((0,), (0,)), ((), ())),
            preferred_element_type=f32,
        )
        sum_re = summed[:, :half_len]
        sum_im = summed[:, half_len:]
        total_re = total_re + sum_re * cosine_table[s] + sum_im * sine_table[s]
        total_im = total_im - sum_re * sine_table[s] + sum_im * cosine_table[s]
    return jnp.concatenate([total_re, total_im], axis=1)


def merge_stats(stats, distance):
    far = hop(stats, "ori", distance)
    if distance == 1:
        return far[:, ::-1]
    half = distance // 2
    return jnp.stack([far[:, :, e ^ half] for e in range(far.shape[2])], axis=2)


def join(pairs):
    peak = pairs[0][0]
    for pair in pairs[1:]:
        peak = jnp.maximum(peak, pair[0])
    total = sum(pair[1] * jnp.exp(pair[0] - peak) for pair in pairs)
    return jnp.stack([peak, total])


def reduced(images, references, shifts, owners, slot_rows, interpolation, regularizer):
    ori_count, img_count = lax.axis_size("ori"), lax.axis_size("img")
    ori, img = lax.axis_index("ori"), lax.axis_index("img")
    shift_count = shifts.shape[0]
    coef = images.shape[1]
    own_images = images.shape[0]
    segs = coef // SEGLEN
    row_count = regularizer.shape[0]
    orient_count = references.shape[0]
    sub_rows = orient_count // img_count
    half_len = coef // 2

    group_images = gather_plane(images)
    group_rows = group_images.shape[0]
    cosine_table, sine_table = phase_tables(shifts, coef)
    references = jnp.concatenate(
        [
            lax.dynamic_slice_in_dim(references, (img ^ m) * sub_rows, sub_rows, 0)
            for m in range(img_count)
        ],
        axis=0,
    )
    real_part = references[:, :half_len].astype(f32)
    imag_part = references[:, half_len:].astype(f32)
    distance = owners[:, 0] ^ ori
    place = (distance >> 1) + (distance & 1) * (ori_count // 2)
    target = place * row_count + slot_rows
    all_rows = ori_count * row_count
    chosen = (jnp.arange(all_rows, dtype=jnp.int32)[:, None] == target[None, :]).astype(bf16)

    score_list = []
    for s in range(shift_count):
        rotated = rotate(real_part, imag_part, cosine_table[s], sine_table[s])
        score_list.append(
            lax.dot_general(
                group_images, rotated, (((1,), (1,)), ((), ())), preferred_element_type=f32
            )
        )
    scores = jnp.stack(score_list, axis=2).reshape(group_rows, -1) * (2.0 / math.sqrt(coef))
    local_peak = jnp.max(scores, axis=1)
    local_total = jnp.sum(jnp.exp(scores - local_peak[:, None]), axis=1)
    stats = jnp.stack([local_peak, local_total]).reshape(2, 2, ori_count // 2, own_images)
    stats = join([stats, merge_stats(stats, 1)])
    stats = join([stats] + [merge_stats(stats, k) for k in even_distances()])
    stats = stats.reshape(2, group_rows)
    weights = jnp.exp(scores - stats[0][:, None]) / stats[1][:, None]
    weights3 = weights.reshape(group_rows, orient_count, shift_count)
    orient_mass = jnp.sum(weights3, axis=(0, 2))
    summed = backproject(weights3.astype(bf16), group_images, cosine_table, sine_table)

    blocks = summed.reshape(img_count, sub_rows, coef)
    masses = orient_mass.reshape(img_count, sub_rows, 1)
    outgoing = jnp.concatenate(
        [blocks, jnp.broadcast_to(masses, (img_count, sub_rows, SEGLEN))], axis=2
    ).astype(bf16)
    incoming = [hop(outgoing[m], "img", m).astype(f32) for m in range(1, img_count)]
    own = blocks[0] + sum(value[:, :coef] for value in incoming)
    own_mass = masses[0] + sum(value[:, coef : coef + 1] for value in incoming)
    segments = own.astype(bf16).reshape(-1, SEGLEN)
    seg_mass = jnp.repeat(own_mass[:, 0], segs)[None, :]

    part = jnp.dot(chosen, segments, preferred_element_type=f32)
    part_mass = lax.dot_general(
        seg_mass.astype(bf16), chosen, (((1,), (1,)), ((), ())), preferred_element_type=f32
    )
    mass_rows = max(16, row_count // SEGLEN)
    part_mass = part_mass.reshape(ori_count, row_count)
    part_mass = jnp.pad(part_mass, ((0, 0), (0, mass_rows * SEGLEN - row_count)))
    parcel = jnp.concatenate(
        [part.reshape(ori_count, row_count, SEGLEN), part_mass.reshape(ori_count, -1, SEGLEN)], axis=1
    ).astype(bf16)
    half = ori_count // 2
    parcel = parcel[:half].astype(f32) + hop(parcel[half:], "ori", 1).astype(f32)
    small = parcel.astype(bf16)
    brick = parcel[0] + sum(hop(small[k // 2], "ori", k).astype(f32) for k in even_distances())
    inserted = brick[:row_count]
    weight_sum = brick[row_count:].reshape(-1)[:row_count]
    mapped = jnp.dot(
        inserted, interpolation, precision=lax.Precision.HIGHEST, preferred_element_type=f32
    )
    volume = mapped / (weight_sum + regularizer)[:, None]
    back_values = lax.dot_general(
        volume,
        interpolation,
        (((1,), (1,)), ((), ())),
        precision=lax.Precision.HIGHEST,
        preferred_element_type=f32,
    )
    bricks = gather_plane(back_values.astype(bf16))
    resampled = lax.dot_general(
        chosen, bricks, (((0,), (0,)), ((), ())), preferred_element_type=f32
    )
    return (volume, resampled.reshape(sub_rows, coef))


def iota(shape, axis):
    return lax.broadcasted_iota(jnp.int32, shape, axis)


def distance_of(place, shares):
    half = shares // 2
    if isinstance(place, int):
        return 2 * place if place < half else 2 * (place - half) + 1
    return jnp.where(place < half, 2 * place, 2 * (place - half) + 1)


def gather_pair(value, *after, own=None):
    parts = [value if own is None else own]
    parts += [hop(value, "ori", k) for k in even_distances()]
    (near,) = call(
        functools.partial(stack_kernel, len(parts)),
        (*reversed(parts), *after),
        (((len(parts), *value.shape), value.dtype),),
        cost=COST_STACK,
    )
    return near, hop(near, "ori", 1)


def stack_kernel(count, *refs):
    for place in range(count):
        refs[-1][count - 1 - place] = refs[place][...]


def phase_kernel(shifts, place, phases, tables):
    count = shifts.shape[0]
    unit = 2.0 * math.pi / image_side
    moves = unit * shifts[...]

    def angles(start, positions):
        lane = iota((count, positions), 1)
        freq_x = (lane % grid_width).astype(f32)
        freq_y = (lane // grid_width + start).astype(f32) - image_side / 2
        return moves[:, 0:1] * freq_x + moves[:, 1:2] * freq_y

    first = angles(0, CHUNK)
    step = jnp.broadcast_to(moves[:, 1:2] * float(CHUNK // grid_width), (count, CHUNK))
    phases[...] = jnp.zeros(phases.shape, f32)
    for h, angle in enumerate((first, step)):
        phases[0, h, :count, :] = jnp.cos(angle)
        phases[1, h, :count, :] = jnp.sin(angle)
    length = tables.shape[2]
    angle = angles(place[0] * (length // grid_width), length)
    tables[...] = jnp.zeros(tables.shape, f32)
    tables[0, :count, :] = jnp.cos(angle)
    tables[1, :count, :] = jnp.sin(angle)


def turn(phases, now):
    cosine, sine = now[0], now[1]
    cos_step, sin_step = phases[0, 1], phases[1, 1]
    now[0] = cosine * cos_step - sine * sin_step
    now[1] = sine * cos_step + cosine * sin_step


def place_order(ori, shares, group_rows):
    own_images = group_rows // shares
    rows = 16 // own_images * group_rows
    out_row, in_row = iota((rows, 16 * shares), 0), iota((rows, 16 * shares), 1)
    share, part = in_row // 16, in_row % 16
    image = (distance_of(share, shares) ^ ori) * own_images + part % own_images
    return jnp.where(out_row == part // own_images * group_rows + image, 1.0, 0.0).astype(bf16)


def place_images(near, far, ori, out):
    shares, group_rows = 2 * near.shape[0], out.shape[0]
    step = 16 * shares // group_rows
    order = place_order(ori, shares, group_rows)
    for q in range(out.shape[1] // SEGLEN // step):
        rows = slice(16 * q, 16 * q + 16)
        block = jnp.concatenate([near[:, rows, :], far[:, rows, :]], axis=0)
        block = block.reshape(shares * 16, SEGLEN)
        placed = jnp.dot(order, block, preferred_element_type=f32).astype(bf16)
        for jj in range(step):
            lanes = pl.ds((q * step + jj) * SEGLEN, SEGLEN)
            out[:, lanes] = placed[jj * group_rows : (jj + 1) * group_rows]


def score_kernel(
    shift_count,
    near,
    far,
    references,
    phases,
    pick,
    slots,
    owners,
    place,
    message,
    piece,
    own,
    now,
):
    group_rows, coef = own.shape
    half_len = coef // 2
    place_images(near, far, place[0], own)
    tiles = piece.shape[0] // group_rows // 2
    for h in range(2):
        for t in range(tiles):
            first = h * half_len + (place[0] * tiles + t) * SEGLEN
            row = (h * tiles + t) * group_rows
            piece[row : row + group_rows, :] = own[:, pl.ds(pl.multiple_of(first, SEGLEN), SEGLEN)]
    now[0] = phases[0, 0]
    now[1] = phases[1, 0]

    def step(t, total):
        re_lanes = pl.ds(pl.multiple_of(t * CHUNK, CHUNK), CHUNK)
        im_lanes = pl.ds(pl.multiple_of(half_len + t * CHUNK, CHUNK), CHUNK)
        real_part = references[:, re_lanes].astype(f32)
        imag_part = references[:, im_lanes].astype(f32)
        rotated_re, rotated_im = [], []
        for s in range(shift_count):
            c, d = now[0, s : s + 1, :], now[1, s : s + 1, :]
            rotated_re.append((real_part * c - imag_part * d).astype(bf16))
            rotated_im.append((real_part * d + imag_part * c).astype(bf16))
        total += lax.dot_general(
            jnp.concatenate(rotated_re, axis=0), own[:, re_lanes], LANES, preferred_element_type=f32
        )
        total += lax.dot_general(
            jnp.concatenate(rotated_im, axis=0), own[:, im_lanes], LANES, preferred_element_type=f32
        )
        turn(phases, now)
        return total

    columns = shift_count * references.shape[0]
    total = lax.fori_loop(
        0, half_len // CHUNK, step, jnp.zeros((columns, group_rows), f32), unroll=True
    )
    scores = jnp.swapaxes(total, 0, 1) * (2.0 / math.sqrt(coef))
    peak = jnp.max(scores, axis=1, keepdims=True)
    exponents = jnp.exp(scores - peak)
    total = jnp.sum(exponents, axis=1, keepdims=True)
    picked = jnp.dot(exponents.astype(bf16), pick[...], preferred_element_type=f32)
    blocks = pick.shape[1] // SEGLEN
    shares = message.shape[0] // blocks
    valid = columns // blocks
    lane = iota((group_rows, SEGLEN), 1)
    rest = jnp.concatenate(
        [
            part
            for fact in (slots, owners)
            for part in (
                pltpu.roll(fact[...].astype(f32), SEGLEN // 2, 1),
                fact[...].astype(f32),
            )
        ],
        axis=0,
    )
    at = valid
    for value in (peak, total):
        for _ in range(3):
            part = value.astype(bf16).astype(f32)
            rest = jnp.where(lane == at, part, rest)
            value = value - part
            at += 1
    for b in range(blocks):
        block = picked[:, b * SEGLEN : (b + 1) * SEGLEN]
        block = jnp.where(lane < valid, block, rest).astype(bf16)
        for p in range(shares):
            message[b * shares + p] = block


def beside_kernel(rows, *refs):
    *parts, kernel, regularizer, out, brick = refs
    brick[:SEGLEN, :] = kernel[...].astype(bf16)
    high = regularizer[...].astype(bf16).astype(f32)
    spare = jnp.zeros((brick.shape[0] - SEGLEN - 2 * high.shape[0], SEGLEN), f32)
    brick[SEGLEN:, :] = jnp.concatenate([high, regularizer[...] - high, spare], axis=0).astype(bf16)
    count = len(parts)
    for tile in range(parts[0].shape[0] // rows):
        for k, part in enumerate(parts):
            row = (tile * count + k) * rows
            out[row : row + rows, :] = part[tile * rows : (tile + 1) * rows, :]


def facts_of(got, share, sub_rows):
    part = got[share].astype(f32)
    rolled = pltpu.roll(part, SEGLEN // 2, 1)
    lane = iota((sub_rows, SEGLEN), 1)

    def rows(first):
        return jnp.where(
            lane < SEGLEN // 2,
            rolled[first : first + sub_rows],
            part[first + sub_rows : first + 2 * sub_rows],
        )

    return rows(0), rows(2 * sub_rows)


def flat_facts(sub_rows, shares, got, place, upright, flat):
    orients = shares * sub_rows
    blocks = flat.shape[1]
    lot = SEGLEN // orients
    pairs = [facts_of(got, place[1] * shares + p, sub_rows) for p in range(shares)]
    facts = [pair[h] for h in range(2) for pair in pairs]
    facts = jnp.concatenate(facts + [jnp.zeros((SEGLEN - 2 * orients, SEGLEN), f32)], axis=0)
    upright[...] = jnp.swapaxes(facts, 0, 1)
    parts = [upright[pl.ds(b, blocks, stride=lot), :] for b in range(lot)]
    for h in range(2):
        lanes = slice(h * orients, (h + 1) * orients)
        flat[h] = jnp.concatenate([part[:, lanes] for part in parts], axis=1)
    run = blocks // (2 * shares)
    taken = []
    for p in range(shares):
        share = place[0] ^ distance_of(p, shares)
        taken += [h * (blocks // 2) + share * run + i for h in range(2) for i in range(run)]
    slots = jnp.concatenate([flat[0, pl.ds(a, 1), :] for a in taken], axis=0)
    owners = jnp.concatenate([flat[1, pl.ds(a, 1), :] for a in taken], axis=0)
    return slots, owners


def fact_kernel(
    sub_rows,
    shares,
    got,
    after,
    place,
    chosen,
    parity_lanes,
    counts,
    own_slots,
    own_owner_lanes,
    upright,
    flat,
):
    row_count = own_slots.shape[1]
    orients = shares * sub_rows
    blocks = flat.shape[1]
    tiles = SEGLEN
    pairs = shares // 2
    slots, owners = flat_facts(sub_rows, shares, got, place, upright, flat)
    pair = (owners.astype(jnp.int32) // 2).astype(f32)
    parity = owners - 2.0 * pair
    columns = jnp.concatenate(
        [owners, parity, jnp.zeros((SEGLEN - 2 * blocks, SEGLEN), f32)], axis=0
    )
    columns = jnp.swapaxes(columns, 0, 1)
    groups = row_count // 16
    slot_row = iota((row_count, SEGLEN), 0).astype(f32).astype(bf16).reshape(groups, 16, SEGLEN)
    zeros = jnp.zeros((groups, 16, SEGLEN), bf16)
    ones = jnp.ones((groups, 16, SEGLEN), bf16)
    count_lane = iota((SEGLEN, shares * orients), 1)
    lane_owner = (count_lane // orients).astype(f32)
    same = iota((SEGLEN, shares * orients), 0) % orients == count_lane % orients
    lane_owner = jnp.where(same, lane_owner, -1.0)
    total = jnp.zeros((row_count, shares * orients), f32)
    for a in range(0, blocks, 2):
        slot_chosen, owned = [], []
        for b in (a, a + 1):
            block = slice(b * SEGLEN, (b + 1) * SEGLEN)
            slot = jnp.broadcast_to(slots[b : b + 1, :], (16, SEGLEN)).astype(bf16)
            match = slot_row == slot[None]
            for q in range(pairs):
                held = jnp.broadcast_to(pair[b : b + 1, :], (16, SEGLEN))
                held = jnp.where(held == float(q), 1.0, 0.0).astype(bf16)
                part = jnp.where(match, jnp.broadcast_to(held[None], zeros.shape), zeros)
                chosen[q * row_count : (q + 1) * row_count, block] = part.reshape(row_count, SEGLEN)
            slot_chosen.append(jnp.where(match, ones, zeros).reshape(row_count, SEGLEN))
            parity_lanes[block, :] = jnp.broadcast_to(
                columns[:, blocks + b : blocks + b + 1], (SEGLEN, SEGLEN)
            ).astype(bf16)
            owned.append(jnp.where(columns[:, b : b + 1] == lane_owner, 1.0, 0.0).astype(bf16))
        total += jnp.dot(
            jnp.concatenate(slot_chosen, axis=1),
            jnp.concatenate(owned, axis=0),
            preferred_element_type=f32,
        )
    counts[...] = total.astype(bf16)
    own = jnp.concatenate(facts_of(got, place[1] * shares + place[0], sub_rows), axis=0)
    own = jnp.concatenate([own, jnp.zeros((SEGLEN - own.shape[0], SEGLEN), f32)], axis=0)
    own = jnp.swapaxes(own, 0, 1)
    slot_lane = iota((tiles, row_count), 1).astype(f32)
    for o in range(sub_rows):
        rows = slice(o * tiles, (o + 1) * tiles)
        own_slots[rows, :] = jnp.where(slot_lane == own[:, o : o + 1], 1.0, 0.0).astype(bf16)
        own_owner_lanes[rows, :] = jnp.broadcast_to(
            own[:, sub_rows + o : sub_rows + o + 1], (tiles, SEGLEN)
        ).astype(bf16)


def slice_kernel(shift_count, group_rows, *refs):
    got, images, tables, arrange, after, place, segments, masses = refs
    length = tables.shape[2]
    shares = 2 * arrange.shape[1] // SEGLEN
    orients = arrange.shape[0] // shift_count
    lot = CHUNK // SEGLEN
    valid = shift_count * orients // shares
    img_count = got.shape[0] // shares
    image_rows = img_count * group_rows
    everything = jnp.concatenate(
        [got[(place[1] ^ k) * shares + p] for p in range(shares) for k in range(img_count)], axis=0
    )
    row, lane = iota((SEGLEN, 2 * SEGLEN), 0), iota((SEGLEN, 2 * SEGLEN), 1)
    first = jnp.where(lane < SEGLEN, valid, valid + 3)
    spread = jnp.where((row >= first) & (row < first + 3), 1.0, 0.0).astype(bf16)
    values = jnp.dot(everything, spread, preferred_element_type=f32)
    parts = [slice(p * image_rows, (p + 1) * image_rows) for p in range(shares)]
    peak = functools.reduce(jnp.maximum, [values[part, :SEGLEN] for part in parts])
    factors = [jnp.exp(values[part, :SEGLEN] - peak) for part in parts]
    total = sum(values[part, SEGLEN:] * factor for part, factor in zip(parts, factors, strict=True))
    inverse = 1.0 / total
    lane = iota((image_rows, SEGLEN), 1)
    weighted = [
        jnp.where(lane < valid, everything[part].astype(f32) * (factor * inverse), 0.0)
        for part, factor in zip(parts, factors, strict=True)
    ]
    stacked = jnp.concatenate(
        [
            (weighted[p] + pltpu.roll(weighted[p + 1], SEGLEN // 2, 1)).astype(bf16)
            for p in range(0, shares, 2)
        ],
        axis=1,
    )
    weights = lax.dot_general(arrange[...], stacked, LANES, preferred_element_type=f32)
    mass = jnp.sum(weights, axis=1, keepdims=True)
    mass = sum(mass[s * orients : (s + 1) * orients] for s in range(shift_count))
    masses[...] = jnp.broadcast_to(mass, masses.shape)
    weights = weights.astype(bf16)

    def images_at(tile):
        return images[tile * image_rows : (tile + 1) * image_rows, :]

    for t in range(length // CHUNK):
        lanes = slice(t * CHUNK, (t + 1) * CHUNK)
        tiles = range(t * lot, (t + 1) * lot)
        real_part = jnp.concatenate([images_at(j) for j in tiles], axis=1)
        imag_part = jnp.concatenate([images_at(length // SEGLEN + j) for j in tiles], axis=1)
        summed_re = jnp.dot(weights, real_part, preferred_element_type=f32)
        summed_im = jnp.dot(weights, imag_part, preferred_element_type=f32)
        total_re = jnp.zeros((orients, CHUNK), f32)
        total_im = jnp.zeros((orients, CHUNK), f32)
        for s in range(shift_count):
            c, d = tables[0, s : s + 1, lanes], tables[1, s : s + 1, lanes]
            part_re = summed_re[s * orients : (s + 1) * orients]
            part_im = summed_im[s * orients : (s + 1) * orients]
            total_re += part_re * c + part_im * d
            total_im += part_im * c - part_re * d
        for h in range(lot):
            lanes = slice(h * SEGLEN, (h + 1) * SEGLEN)
            row = (t * lot + h) * orients
            segments[row : row + orients, :] = total_re[:, lanes].astype(bf16)
            row += length // SEGLEN * orients
            segments[row : row + orients, :] = total_im[:, lanes].astype(bf16)


def insert(shares, first, chosen, parity_lanes, segments):
    rows = segments.shape[0] // shares.shape[0]
    zero = jnp.zeros((rows, SEGLEN), bf16)
    for p in range(shares.shape[0]):
        part = shares[p, :rows, :]
        parity = parity_lanes[(first + p) * rows : (first + p + 1) * rows, :]
        for w in range(2):
            segments[p * rows : (p + 1) * rows, w * SEGLEN : (w + 1) * SEGLEN] = jnp.where(
                parity == float(w), part, zero
            )
    lanes = slice(first * rows, (first + shares.shape[0]) * rows)
    return jnp.dot(chosen[:, lanes], segments[...], preferred_element_type=f32)


def near_kernel(near, chosen, parity_lanes, counts, masses, inserted, weight_sum, segments):
    inserted[...] = insert(near, 0, chosen, parity_lanes, segments)
    shares = weight_sum.shape[1]
    mass = masses[...]
    mass_hi = mass.astype(bf16).astype(f32)
    lane = iota(mass.shape, 1)
    both = jnp.where(lane < shares, mass_hi, jnp.where(lane < 2 * shares, mass - mass_hi, 0.0))
    spread = jnp.concatenate([jnp.where(lane % shares == w, both, 0.0) for w in range(shares)], axis=0)
    total = jnp.dot(counts[...], spread.astype(bf16), preferred_element_type=f32)
    weight_sum[...] = total[:, :shares] + total[:, shares : 2 * shares]


def volume_kernel(
    far,
    near_bricks,
    far_bricks,
    near_inserted,
    chosen,
    parity_lanes,
    weight_sum,
    own_slots,
    own_owner_lanes,
    place,
    volume,
    resampled,
    segments,
    kernels,
    bricks,
    result,
    rows_out,
    regularizer,
    signals,
):
    half = far.shape[0]
    shares = 2 * half
    rows = segments.shape[0] // half
    row_count = bricks.shape[1]
    sub_rows, coef = rows_out.shape
    tiles = coef // SEGLEN
    reg_rows = row_count // SEGLEN
    kernels[...] = jnp.zeros(kernels.shape, bf16)
    regularizer[...] = jnp.zeros(regularizer.shape, f32)
    for p in range(shares):
        w = place[0] ^ distance_of(p, shares)
        at = pl.ds(pl.multiple_of(w % 2 * SEGLEN, SEGLEN), SEGLEN)
        brick = near_bricks[p] if p < half else far_bricks[p - half]
        kernels[w // 2, at, at] = brick[:SEGLEN]
        parts = brick[SEGLEN:].astype(f32)
        for h in range(reg_rows):
            regularizer[pl.ds(h * shares + w, 1), :] = (
                parts[h : h + 1, :] + parts[reg_rows + h : reg_rows + h + 1, :]
            )
    columns = jnp.swapaxes(regularizer[...], 0, 1)
    columns = [columns[:, h * shares : (h + 1) * shares] for h in range(reg_rows)]
    inverse = 1.0 / (weight_sum[...] + jnp.concatenate(columns, axis=0))
    inserted = insert(far, half, chosen, parity_lanes, segments) + near_inserted[...]
    inserted = inserted.astype(bf16)
    mapped = []
    for a in range(half):
        pair = jnp.dot(
            inserted[a * row_count : (a + 1) * row_count, :],
            kernels[a],
            preferred_element_type=f32,
        )
        sides = []
        for w in (2 * a, 2 * a + 1):
            side = pair[:, w % 2 * SEGLEN : (w % 2 + 1) * SEGLEN] * inverse[:, w : w + 1]
            bricks[w] = side
            sides.append(side.astype(bf16))
        mapped.append(jnp.concatenate(sides, axis=1))
    own = pltpu.make_async_copy(bricks.at[place[0]], volume, signals.at[0])
    own.start()
    back = [
        lax.dot_general(pair, kernels[a], LANES, preferred_element_type=f32).astype(bf16)
        for a, pair in enumerate(mapped)
    ]
    taken = jnp.dot(own_slots[...], jnp.concatenate(back, axis=1), preferred_element_type=f32)
    owner = own_owner_lanes[...].astype(f32)
    total = jnp.zeros((sub_rows * tiles, SEGLEN), f32)
    for w in range(shares):
        total = jnp.where(owner == float(w), taken[:, w * SEGLEN : (w + 1) * SEGLEN], total)
    result[...] = total
    for j in range(tiles):
        rows_out[:, j * SEGLEN : (j + 1) * SEGLEN] = result[pl.ds(j, sub_rows, stride=tiles), :]
    back_again = pltpu.make_async_copy(rows_out, resampled, signals.at[1])
    back_again.start()
    own.wait()
    back_again.wait()


def call(kernel, inputs, outputs, scratch=(), cost=1.0, small=(), out_space=pltpu.VMEM):
    inside = pl.BlockSpec(memory_space=pltpu.VMEM)
    scalars = pl.BlockSpec(memory_space=pltpu.SMEM)
    return pl.pallas_call(
        kernel,
        out_shape=[jax.ShapeDtypeStruct(shape, dtype) for shape, dtype in outputs],
        in_specs=[inside] * len(inputs) + [scalars] * len(small),
        out_specs=[pl.BlockSpec(memory_space=out_space)] * len(outputs),
        scratch_shapes=list(scratch),
        compiler_params=pltpu.CompilerParams(vmem_limit_bytes=24 * 2**20),
        cost_estimate=pl.CostEstimate(
            flops=int(cost * 1.15e9), bytes_accessed=0, transcendentals=0
        ),
    )(*inputs, *small)


def whole_plane(images, references, shifts, owners, slot_rows, interpolation, regularizer):
    ori_count, img_count = lax.axis_size("ori"), lax.axis_size("img")
    ori, img = lax.axis_index("ori"), lax.axis_index("img")
    shift_count = shifts.shape[0]
    own_images, coef = images.shape
    tiles = coef // SEGLEN
    half = ori_count // 2
    row_count = regularizer.shape[0]
    orient_count = references.shape[0]
    sub_rows = orient_count // img_count
    group_rows = own_images * ori_count
    columns = shift_count * orient_count
    orients = ori_count * sub_rows
    length = coef // 2 // ori_count
    place = jnp.stack([ori, img]).astype(jnp.int32)

    piece = images.reshape(own_images, tiles, SEGLEN).transpose(1, 0, 2).reshape(-1, SEGLEN)
    column = np.arange(columns)
    orient = column % orient_count
    lane = orient // sub_rows * SEGLEN + column // orient_count * sub_rows + orient % sub_rows
    pick = jnp.asarray(lane[:, None] == np.arange(img_count * SEGLEN), bf16)
    row = np.arange(shift_count * orients)
    source = row % orients // sub_rows * (SEGLEN // 2) + row // orients * sub_rows + row % sub_rows
    arrange = jnp.asarray(source[:, None] == np.arange(half * SEGLEN), bf16)
    phases, tables = call(
        phase_kernel,
        (shifts,),
        (((2, 2, -(-shift_count // 8) * 8, CHUNK), f32), ((2, -(-shift_count // 8) * 8, length), f32)),
        small=(place,),
        cost=COST_PHASE,
    )
    near, far = gather_pair(piece, phases)
    message, part = call(
        functools.partial(score_kernel, shift_count),
        (
            near,
            far,
            references,
            phases,
            pick,
            slot_rows.reshape(-1, SEGLEN),
            owners.reshape(-1, SEGLEN),
        ),
        (
            ((img_count * ori_count, group_rows, SEGLEN), bf16),
            ((2 * length // SEGLEN * group_rows, SEGLEN), bf16),
        ),
        scratch=(pltpu.VMEM((group_rows, coef), bf16), pltpu.VMEM(phases.shape[1:], f32)),
        small=(place,),
        cost=COST_SCORE,
    )
    got = lax.all_to_all(message, ("img", "ori"), split_axis=0, concat_axis=0, tiled=True)
    pieces = [part] + [hop(part, "img", k) for k in range(1, img_count)]
    beside, brick = call(
        functools.partial(beside_kernel, group_rows),
        (*pieces, interpolation, regularizer.reshape(-1, SEGLEN)),
        (((img_count * part.shape[0], SEGLEN), bf16), ((SEGLEN + 16, SEGLEN), bf16)),
        cost=COST_BESIDE,
    )
    near_bricks, far_bricks = gather_pair(brick)

    rows = 2 * (length // SEGLEN) * orients
    segments, masses = call(
        functools.partial(slice_kernel, shift_count, group_rows),
        (got, beside, tables, arrange, near_bricks),
        (((rows, SEGLEN), bf16), ((orients, SEGLEN), f32)),
        small=(place,),
        cost=COST_SLICE,
    )
    chosen, parity_lanes, counts, own_slots, own_owner_lanes = call(
        functools.partial(fact_kernel, sub_rows, ori_count),
        (got, masses),
        (
            ((half * row_count, orients * tiles), bf16),
            ((orients * tiles, SEGLEN), bf16),
            ((row_count, ori_count * orients), bf16),
            ((sub_rows * tiles, row_count), bf16),
            ((sub_rows * tiles, SEGLEN), bf16),
        ),
        scratch=(
            pltpu.VMEM((SEGLEN, SEGLEN), f32),
            pltpu.VMEM((2, orients * tiles // SEGLEN, SEGLEN), f32),
        ),
        small=(place,),
        cost=COST_FACT,
    )

    near, far = gather_pair(segments, counts)
    masked = pltpu.VMEM((half * rows, 2 * SEGLEN), bf16)
    inserted, weight_sum = call(
        near_kernel,
        (near, chosen, parity_lanes, counts, masses),
        (((half * row_count, 2 * SEGLEN), f32), ((row_count, ori_count), f32)),
        scratch=(masked,),
        cost=COST_NEAR,
    )
    volume, resampled = call(
        volume_kernel,
        (
            far,
            near_bricks,
            far_bricks,
            inserted,
            chosen,
            parity_lanes,
            weight_sum,
            own_slots,
            own_owner_lanes,
        ),
        (((row_count, SEGLEN), f32), ((sub_rows, coef), f32)),
        scratch=(
            masked,
            pltpu.VMEM((half, 2 * SEGLEN, 2 * SEGLEN), bf16),
            pltpu.VMEM((ori_count, row_count, SEGLEN), f32),
            pltpu.VMEM((sub_rows * tiles, SEGLEN), f32),
            pltpu.VMEM((sub_rows, coef), f32),
            pltpu.VMEM((SEGLEN, SEGLEN), f32),
            pltpu.SemaphoreType.DMA((2,)),
        ),
        small=(place,),
        cost=COST_VOLUME,
        out_space=pl.ANY,
    )
    return (volume, resampled)


def shards(images, references, shifts, owners, slot_rows, interpolation, regularizer):
    arguments = (images, references, shifts, owners, slot_rows, interpolation, regularizer)
    whole_bytes = images.size * 2 * lax.axis_size("img") * lax.axis_size("ori")
    if whole_bytes <= 4 * 2**20:
        return whole_plane(*arguments)
    return reduced(*arguments)


def solution(mesh):
    in_specs = (
        P(("img", "ori"), None),
        P("ori", None),
        P(),
        P(("ori", "img"), None),
        P(("ori", "img")),
        P(("ori", "img"), None),
        P(("ori", "img")),
    )
    out_specs = (P(("ori", "img"), None), P(("ori", "img"), None))
    return jax.shard_map(shards, mesh=mesh, in_specs=in_specs, out_specs=out_specs, check_vma=False)
```

```python
import functools
import math

import jax
import jax.numpy as jnp
import numpy as np
from jax import lax
from jax.experimental import pallas as pl
from jax.experimental.pallas import tpu as pltpu
from jax.sharding import PartitionSpec as P

SEGLEN = 128
grid_width = 64
image_side = 128.0
CHUNK = 256
LANES = (((1,), (1,)), ((), ()))
COST_PHASE = 12.0
COST_SCORE = 0.001
COST_WEIGHT = 0.001
COST_STACK = 0.001
COST_BESIDE = 30.0
COST_FACT = 0.001
COST_SLICE = 0.001
COST_NEAR = 0.001
COST_VOLUME = 0.001
bf16 = jnp.bfloat16
f32 = jnp.float32


def hop(value, axis, distance):
    pairs = [(place, place ^ distance) for place in range(lax.axis_size(axis))]
    return lax.ppermute(value, axis, pairs)


def even_distances():
    return range(2, lax.axis_size("ori"), 2)


def gather_plane(value):
    near = jnp.concatenate([value] + [hop(value, "ori", k) for k in even_distances()], axis=0)
    return jnp.concatenate([near, hop(near, "ori", 1)], axis=0)


def phase_tables(shifts, coef):
    half_len = coef // 2
    positions = jnp.arange(half_len, dtype=jnp.int32)
    freq_x = (positions % grid_width).astype(f32)
    freq_y = (positions // grid_width - half_len // grid_width // 2).astype(f32)
    angles = (
        2.0
        * math.pi
        / image_side
        * (shifts[:, 0:1] * freq_x[None, :] + shifts[:, 1:2] * freq_y[None, :])
    )
    return (jnp.cos(angles), jnp.sin(angles))


def rotate(real_part, imag_part, cosine_row, sine_row):
    rotated_re = real_part * cosine_row[None, :] - imag_part * sine_row[None, :]
    rotated_im = real_part * sine_row[None, :] + imag_part * cosine_row[None, :]
    return jnp.concatenate([rotated_re, rotated_im], axis=1).astype(bf16)


def backproject(weights_b, group_images, cosine_table, sine_table):
    half_len = group_images.shape[1] // 2
    orient_count = weights_b.shape[1]
    total_re = jnp.zeros((orient_count, half_len), f32)
    total_im = jnp.zeros((orient_count, half_len), f32)
    for s in range(cosine_table.shape[0]):
        summed = lax.dot_general(
            weights_b[:, :, s],
            group_images,
            (((0,), (0,)), ((), ())),
            preferred_element_type=f32,
        )
        sum_re = summed[:, :half_len]
        sum_im = summed[:, half_len:]
        total_re = total_re + sum_re * cosine_table[s] + sum_im * sine_table[s]
        total_im = total_im - sum_re * sine_table[s] + sum_im * cosine_table[s]
    return jnp.concatenate([total_re, total_im], axis=1)


def merge_stats(stats, distance):
    far = hop(stats, "ori", distance)
    if distance == 1:
        return far[:, ::-1]
    half = distance // 2
    return jnp.stack([far[:, :, e ^ half] for e in range(far.shape[2])], axis=2)


def join(pairs):
    peak = pairs[0][0]
    for pair in pairs[1:]:
        peak = jnp.maximum(peak, pair[0])
    total = sum(pair[1] * jnp.exp(pair[0] - peak) for pair in pairs)
    return jnp.stack([peak, total])


def reduced(images, references, shifts, owners, slot_rows, interpolation, regularizer):
    ori_count, img_count = lax.axis_size("ori"), lax.axis_size("img")
    ori, img = lax.axis_index("ori"), lax.axis_index("img")
    shift_count = shifts.shape[0]
    coef = images.shape[1]
    own_images = images.shape[0]
    segs = coef // SEGLEN
    row_count = regularizer.shape[0]
    orient_count = references.shape[0]
    sub_rows = orient_count // img_count
    half_len = coef // 2

    group_images = gather_plane(images)
    group_rows = group_images.shape[0]
    cosine_table, sine_table = phase_tables(shifts, coef)
    references = jnp.concatenate(
        [
            lax.dynamic_slice_in_dim(references, (img ^ m) * sub_rows, sub_rows, 0)
            for m in range(img_count)
        ],
        axis=0,
    )
    real_part = references[:, :half_len].astype(f32)
    imag_part = references[:, half_len:].astype(f32)
    distance = owners[:, 0] ^ ori
    place = (distance >> 1) + (distance & 1) * (ori_count // 2)
    target = place * row_count + slot_rows
    all_rows = ori_count * row_count
    chosen = (jnp.arange(all_rows, dtype=jnp.int32)[:, None] == target[None, :]).astype(bf16)

    score_list = []
    for s in range(shift_count):
        rotated = rotate(real_part, imag_part, cosine_table[s], sine_table[s])
        score_list.append(
            lax.dot_general(
                group_images, rotated, (((1,), (1,)), ((), ())), preferred_element_type=f32
            )
        )
    scores = jnp.stack(score_list, axis=2).reshape(group_rows, -1) * (2.0 / math.sqrt(coef))
    local_peak = jnp.max(scores, axis=1)
    local_total = jnp.sum(jnp.exp(scores - local_peak[:, None]), axis=1)
    stats = jnp.stack([local_peak, local_total]).reshape(2, 2, ori_count // 2, own_images)
    stats = join([stats, merge_stats(stats, 1)])
    stats = join([stats] + [merge_stats(stats, k) for k in even_distances()])
    stats = stats.reshape(2, group_rows)
    weights = jnp.exp(scores - stats[0][:, None]) / stats[1][:, None]
    weights3 = weights.reshape(group_rows, orient_count, shift_count)
    orient_mass = jnp.sum(weights3, axis=(0, 2))
    summed = backproject(weights3.astype(bf16), group_images, cosine_table, sine_table)

    blocks = summed.reshape(img_count, sub_rows, coef)
    masses = orient_mass.reshape(img_count, sub_rows, 1)
    outgoing = jnp.concatenate(
        [blocks, jnp.broadcast_to(masses, (img_count, sub_rows, SEGLEN))], axis=2
    ).astype(bf16)
    incoming = [hop(outgoing[m], "img", m).astype(f32) for m in range(1, img_count)]
    own = blocks[0] + sum(value[:, :coef] for value in incoming)
    own_mass = masses[0] + sum(value[:, coef : coef + 1] for value in incoming)
    segments = own.astype(bf16).reshape(-1, SEGLEN)
    seg_mass = jnp.repeat(own_mass[:, 0], segs)[None, :]

    part = jnp.dot(chosen, segments, preferred_element_type=f32)
    part_mass = lax.dot_general(
        seg_mass.astype(bf16), chosen, (((1,), (1,)), ((), ())), preferred_element_type=f32
    )
    mass_rows = max(16, row_count // SEGLEN)
    part_mass = part_mass.reshape(ori_count, row_count)
    part_mass = jnp.pad(part_mass, ((0, 0), (0, mass_rows * SEGLEN - row_count)))
    parcel = jnp.concatenate(
        [part.reshape(ori_count, row_count, SEGLEN), part_mass.reshape(ori_count, -1, SEGLEN)], axis=1
    ).astype(bf16)
    half = ori_count // 2
    parcel = parcel[:half].astype(f32) + hop(parcel[half:], "ori", 1).astype(f32)
    small = parcel.astype(bf16)
    brick = parcel[0] + sum(hop(small[k // 2], "ori", k).astype(f32) for k in even_distances())
    inserted = brick[:row_count]
    weight_sum = brick[row_count:].reshape(-1)[:row_count]
    mapped = jnp.dot(
        inserted, interpolation, precision=lax.Precision.HIGHEST, preferred_element_type=f32
    )
    volume = mapped / (weight_sum + regularizer)[:, None]
    back_values = lax.dot_general(
        volume,
        interpolation,
        (((1,), (1,)), ((), ())),
        precision=lax.Precision.HIGHEST,
        preferred_element_type=f32,
    )
    bricks = gather_plane(back_values.astype(bf16))
    resampled = lax.dot_general(
        chosen, bricks, (((0,), (0,)), ((), ())), preferred_element_type=f32
    )
    return (volume, resampled.reshape(sub_rows, coef))


def iota(shape, axis):
    return lax.broadcasted_iota(jnp.int32, shape, axis)


def distance_of(place, shares):
    even = (shares - 2 * place) & (shares - 1)
    return even ^ (place // (shares // 2))


def hops_in_plane(value):
    count = lax.axis_size("ori")
    return [hop(value, "ori", distance) for distance in range(count - 2, 0, -2)]


def stacks(value, others, *after):
    count = len(others) + 1
    (near,) = call(
        functools.partial(stack_kernel, count),
        (*others, value, *after),
        (((count, *value.shape), value.dtype),),
        cost=COST_STACK,
    )
    return near, hop(near, "ori", 1)


def gather_pair(value, *after):
    return stacks(value, hops_in_plane(value), *after)


def stack_kernel(count, *refs):
    for place in range(count):
        refs[-1][(place + 1) % count] = refs[place][...]


def phase_kernel(shifts, place, phases, tables):
    count = shifts.shape[0]
    unit = 2.0 * math.pi / image_side
    moves = unit * shifts[...]

    def angles(start, positions):
        lane = iota((count, positions), 1)
        freq_x = (lane % grid_width).astype(f32)
        freq_y = (lane // grid_width + start).astype(f32) - image_side / 2
        return moves[:, 0:1] * freq_x + moves[:, 1:2] * freq_y

    first = angles(0, CHUNK)
    step = jnp.broadcast_to(moves[:, 1:2] * float(CHUNK // grid_width), (count, CHUNK))
    phases[...] = jnp.zeros(phases.shape, f32)
    for h, angle in enumerate((first, step)):
        phases[0, h, :count, :] = jnp.cos(angle)
        phases[1, h, :count, :] = jnp.sin(angle)
    length = tables.shape[2]
    angle = angles(place[0] * (length // grid_width), length)
    tables[...] = jnp.zeros(tables.shape, f32)
    tables[0, :count, :] = jnp.cos(angle)
    tables[1, :count, :] = jnp.sin(angle)


def turn(phases, now):
    cosine, sine = now[0], now[1]
    cos_step, sin_step = phases[0, 1], phases[1, 1]
    now[0] = cosine * cos_step - sine * sin_step
    now[1] = sine * cos_step + cosine * sin_step


def place_order(ori, shares, group_rows):
    own_images = group_rows // shares
    rows = 16 // own_images * group_rows
    out_row, in_row = iota((rows, 16 * shares), 0), iota((rows, 16 * shares), 1)
    share, part = in_row // 16, in_row % 16
    image = (distance_of(share, shares) ^ ori) * own_images + part % own_images
    return jnp.where(out_row == part // own_images * group_rows + image, 1.0, 0.0).astype(bf16)


def place_images(near, far, ori, out):
    shares, group_rows = 2 * near.shape[0], out.shape[0]
    step = 16 * shares // group_rows
    order = place_order(ori, shares, group_rows)
    for q in range(out.shape[1] // SEGLEN // step):
        rows = slice(16 * q, 16 * q + 16)
        block = jnp.concatenate([near[:, rows, :], far[:, rows, :]], axis=0)
        block = block.reshape(shares * 16, SEGLEN)
        placed = jnp.dot(order, block, preferred_element_type=f32).astype(bf16)
        for jj in range(step):
            lanes = pl.ds((q * step + jj) * SEGLEN, SEGLEN)
            out[:, lanes] = placed[jj * group_rows : (jj + 1) * group_rows]


def score_kernel(
    shift_count,
    near,
    far,
    references,
    phases,
    pick,
    slots,
    owners,
    place,
    message,
    piece,
    own,
    now,
):
    group_rows, coef = own.shape
    half_len = coef // 2
    place_images(near, far, place[0], own)
    tiles = piece.shape[0] // group_rows // 2
    for h in range(2):
        for t in range(tiles):
            first = h * half_len + (place[0] * tiles + t) * SEGLEN
            row = (h * tiles + t) * group_rows
            piece[row : row + group_rows, :] = own[:, pl.ds(pl.multiple_of(first, SEGLEN), SEGLEN)]
    now[0] = phases[0, 0]
    now[1] = phases[1, 0]

    def step(t, total):
        re_lanes = pl.ds(pl.multiple_of(t * CHUNK, CHUNK), CHUNK)
        im_lanes = pl.ds(pl.multiple_of(half_len + t * CHUNK, CHUNK), CHUNK)
        real_part = references[:, re_lanes].astype(f32)
        imag_part = references[:, im_lanes].astype(f32)
        rotated_re, rotated_im = [], []
        for s in range(shift_count):
            c, d = now[0, s : s + 1, :], now[1, s : s + 1, :]
            rotated_re.append((real_part * c - imag_part * d).astype(bf16))
            rotated_im.append((real_part * d + imag_part * c).astype(bf16))
        total += lax.dot_general(
            jnp.concatenate(rotated_re, axis=0), own[:, re_lanes], LANES, preferred_element_type=f32
        )
        total += lax.dot_general(
            jnp.concatenate(rotated_im, axis=0), own[:, im_lanes], LANES, preferred_element_type=f32
        )
        turn(phases, now)
        return total

    columns = shift_count * references.shape[0]
    total = lax.fori_loop(
        0, half_len // CHUNK, step, jnp.zeros((columns, group_rows), f32), unroll=True
    )
    scores = jnp.swapaxes(total, 0, 1) * (2.0 / math.sqrt(coef))
    peak = jnp.max(scores, axis=1, keepdims=True)
    exponents = jnp.exp(scores - peak)
    total = jnp.sum(exponents, axis=1, keepdims=True)
    picked = jnp.dot(exponents.astype(bf16), pick[...], preferred_element_type=f32)
    blocks = pick.shape[1] // SEGLEN
    shares = message.shape[0] // blocks
    valid = columns // blocks
    lane = iota((group_rows, SEGLEN), 1)
    rest = jnp.concatenate(
        [
            part
            for fact in (slots, owners)
            for part in (
                pltpu.roll(fact[...].astype(f32), SEGLEN // 2, 1),
                fact[...].astype(f32),
            )
        ],
        axis=0,
    )
    at = valid
    for value in (peak, total):
        for _ in range(3):
            part = value.astype(bf16).astype(f32)
            rest = jnp.where(lane == at, part, rest)
            value = value - part
            at += 1
    for b in range(blocks):
        block = picked[:, b * SEGLEN : (b + 1) * SEGLEN]
        block = jnp.where(lane < valid, block, rest).astype(bf16)
        for p in range(shares):
            message[b * shares + p] = block


def beside_kernel(rows, *refs):
    *parts, kernel, regularizer, out, brick = refs
    brick[:SEGLEN, :] = kernel[...].astype(bf16)
    high = regularizer[...].astype(bf16).astype(f32)
    spare = jnp.zeros((brick.shape[0] - SEGLEN - 2 * high.shape[0], SEGLEN), f32)
    brick[SEGLEN:, :] = jnp.concatenate([high, regularizer[...] - high, spare], axis=0).astype(bf16)
    count = len(parts)
    for tile in range(parts[0].shape[0] // rows):
        for k, part in enumerate(parts):
            row = (tile * count + k) * rows
            out[row : row + rows, :] = part[tile * rows : (tile + 1) * rows, :]


def facts_of(got, share, sub_rows):
    part = got[share].astype(f32)
    rolled = pltpu.roll(part, SEGLEN // 2, 1)
    lane = iota((sub_rows, SEGLEN), 1)

    def rows(first):
        return jnp.where(
            lane < SEGLEN // 2,
            rolled[first : first + sub_rows],
            part[first + sub_rows : first + 2 * sub_rows],
        )

    return rows(0), rows(2 * sub_rows)


def flat_facts(sub_rows, shares, got, place, upright, flat):
    orients = shares * sub_rows
    blocks = flat.shape[1]
    lot = SEGLEN // orients
    pairs = [facts_of(got, place[1] * shares + p, sub_rows) for p in range(shares)]
    facts = [pair[h] for h in range(2) for pair in pairs]
    facts = jnp.concatenate(facts + [jnp.zeros((SEGLEN - 2 * orients, SEGLEN), f32)], axis=0)
    upright[...] = jnp.swapaxes(facts, 0, 1)
    parts = [upright[pl.ds(b, blocks, stride=lot), :] for b in range(lot)]
    for h in range(2):
        lanes = slice(h * orients, (h + 1) * orients)
        flat[h] = jnp.concatenate([part[:, lanes] for part in parts], axis=1)
    run = blocks // (2 * shares)
    taken = []
    for p in range(shares):
        share = place[0] ^ distance_of(p, shares)
        taken += [h * (blocks // 2) + share * run + i for h in range(2) for i in range(run)]
    slots = jnp.concatenate([flat[0, pl.ds(a, 1), :] for a in taken], axis=0)
    owners = jnp.concatenate([flat[1, pl.ds(a, 1), :] for a in taken], axis=0)
    return slots, owners


def fact_kernel(
    sub_rows,
    shares,
    got,
    after,
    place,
    chosen,
    parity_lanes,
    counts,
    own_slots,
    own_owner_lanes,
    upright,
    flat,
):
    row_count = own_slots.shape[1]
    orients = shares * sub_rows
    blocks = flat.shape[1]
    tiles = SEGLEN
    pairs = shares // 2
    slots, owners = flat_facts(sub_rows, shares, got, place, upright, flat)
    pair = (owners.astype(jnp.int32) // 2).astype(f32)
    parity = owners - 2.0 * pair
    columns = jnp.concatenate(
        [owners, parity, jnp.zeros((SEGLEN - 2 * blocks, SEGLEN), f32)], axis=0
    )
    columns = jnp.swapaxes(columns, 0, 1)
    groups = row_count // 16
    slot_row = iota((row_count, SEGLEN), 0).astype(f32).astype(bf16).reshape(groups, 16, SEGLEN)
    zeros = jnp.zeros((groups, 16, SEGLEN), bf16)
    ones = jnp.ones((groups, 16, SEGLEN), bf16)
    count_lane = iota((SEGLEN, shares * orients), 1)
    lane_owner = (count_lane // orients).astype(f32)
    same = iota((SEGLEN, shares * orients), 0) % orients == count_lane % orients
    lane_owner = jnp.where(same, lane_owner, -1.0)
    total = jnp.zeros((row_count, shares * orients), f32)
    for a in range(0, blocks, 2):
        slot_chosen, owned = [], []
        for b in (a, a + 1):
            block = slice(b * SEGLEN, (b + 1) * SEGLEN)
            slot = jnp.broadcast_to(slots[b : b + 1, :], (16, SEGLEN)).astype(bf16)
            match = slot_row == slot[None]
            for q in range(pairs):
                held = jnp.broadcast_to(pair[b : b + 1, :], (16, SEGLEN))
                held = jnp.where(held == float(q), 1.0, 0.0).astype(bf16)
                part = jnp.where(match, jnp.broadcast_to(held[None], zeros.shape), zeros)
                chosen[q * row_count : (q + 1) * row_count, block] = part.reshape(row_count, SEGLEN)
            slot_chosen.append(jnp.where(match, ones, zeros).reshape(row_count, SEGLEN))
            parity_lanes[block, :] = jnp.broadcast_to(
                columns[:, blocks + b : blocks + b + 1], (SEGLEN, SEGLEN)
            ).astype(bf16)
            owned.append(jnp.where(columns[:, b : b + 1] == lane_owner, 1.0, 0.0).astype(bf16))
        total += jnp.dot(
            jnp.concatenate(slot_chosen, axis=1),
            jnp.concatenate(owned, axis=0),
            preferred_element_type=f32,
        )
    counts[...] = total.astype(bf16)
    own = jnp.concatenate(facts_of(got, place[1] * shares + place[0], sub_rows), axis=0)
    own = jnp.concatenate([own, jnp.zeros((SEGLEN - own.shape[0], SEGLEN), f32)], axis=0)
    own = jnp.swapaxes(own, 0, 1)
    slot_lane = iota((tiles, row_count), 1).astype(f32)
    for o in range(sub_rows):
        rows = slice(o * tiles, (o + 1) * tiles)
        own_slots[rows, :] = jnp.where(slot_lane == own[:, o : o + 1], 1.0, 0.0).astype(bf16)
        own_owner_lanes[rows, :] = jnp.broadcast_to(
            own[:, sub_rows + o : sub_rows + o + 1], (tiles, SEGLEN)
        ).astype(bf16)


def slice_kernel(shift_count, group_rows, *refs):
    got, images, tables, arrange, after, place, segments, masses = refs
    length = tables.shape[2]
    shares = 2 * arrange.shape[1] // SEGLEN
    orients = arrange.shape[0] // shift_count
    lot = CHUNK // SEGLEN
    valid = shift_count * orients // shares
    img_count = got.shape[0] // shares
    image_rows = img_count * group_rows
    everything = jnp.concatenate(
        [got[(place[1] ^ k) * shares + p] for p in range(shares) for k in range(img_count)], axis=0
    )
    row, lane = iota((SEGLEN, 2 * SEGLEN), 0), iota((SEGLEN, 2 * SEGLEN), 1)
    first = jnp.where(lane < SEGLEN, valid, valid + 3)
    spread = jnp.where((row >= first) & (row < first + 3), 1.0, 0.0).astype(bf16)
    values = jnp.dot(everything, spread, preferred_element_type=f32)
    parts = [slice(p * image_rows, (p + 1) * image_rows) for p in range(shares)]
    peak = functools.reduce(jnp.maximum, [values[part, :SEGLEN] for part in parts])
    factors = [jnp.exp(values[part, :SEGLEN] - peak) for part in parts]
    total = sum(values[part, SEGLEN:] * factor for part, factor in zip(parts, factors, strict=True))
    inverse = 1.0 / total
    lane = iota((image_rows, SEGLEN), 1)
    weighted = [
        jnp.where(lane < valid, everything[part].astype(f32) * (factor * inverse), 0.0)
        for part, factor in zip(parts, factors, strict=True)
    ]
    stacked = jnp.concatenate(
        [
            (weighted[p] + pltpu.roll(weighted[p + 1], SEGLEN // 2, 1)).astype(bf16)
            for p in range(0, shares, 2)
        ],
        axis=1,
    )
    weights = lax.dot_general(arrange[...], stacked, LANES, preferred_element_type=f32)
    mass = jnp.sum(weights, axis=1, keepdims=True)
    mass = sum(mass[s * orients : (s + 1) * orients] for s in range(shift_count))
    masses[...] = jnp.broadcast_to(mass, masses.shape)
    weights = weights.astype(bf16)

    def images_at(tile):
        return images[tile * image_rows : (tile + 1) * image_rows, :]

    for t in range(length // CHUNK):
        lanes = slice(t * CHUNK, (t + 1) * CHUNK)
        tiles = range(t * lot, (t + 1) * lot)
        real_part = jnp.concatenate([images_at(j) for j in tiles], axis=1)
        imag_part = jnp.concatenate([images_at(length // SEGLEN + j) for j in tiles], axis=1)
        summed_re = jnp.dot(weights, real_part, preferred_element_type=f32)
        summed_im = jnp.dot(weights, imag_part, preferred_element_type=f32)
        total_re = jnp.zeros((orients, CHUNK), f32)
        total_im = jnp.zeros((orients, CHUNK), f32)
        for s in range(shift_count):
            c, d = tables[0, s : s + 1, lanes], tables[1, s : s + 1, lanes]
            part_re = summed_re[s * orients : (s + 1) * orients]
            part_im = summed_im[s * orients : (s + 1) * orients]
            total_re += part_re * c + part_im * d
            total_im += part_im * c - part_re * d
        for h in range(lot):
            lanes = slice(h * SEGLEN, (h + 1) * SEGLEN)
            row = (t * lot + h) * orients
            segments[row : row + orients, :] = total_re[:, lanes].astype(bf16)
            row += length // SEGLEN * orients
            segments[row : row + orients, :] = total_im[:, lanes].astype(bf16)


def insert(shares, first, chosen, parity_lanes, segments):
    rows = segments.shape[0] // len(shares)
    zero = jnp.zeros((rows, SEGLEN), bf16)
    for p in range(len(shares)):
        part = shares[p][:rows, :]
        parity = parity_lanes[(first + p) * rows : (first + p + 1) * rows, :]
        for w in range(2):
            segments[p * rows : (p + 1) * rows, w * SEGLEN : (w + 1) * SEGLEN] = jnp.where(
                parity == float(w), part, zero
            )
    lanes = slice(first * rows, (first + len(shares)) * rows)
    return jnp.dot(chosen[:, lanes], segments[...], preferred_element_type=f32)


def next_kernel(first, *refs):
    *shares, chosen, parity_lanes, before, inserted, segments = refs
    inserted[...] = before[...] + insert(shares, first, chosen, parity_lanes, segments)


def near_kernel(
    own, other, chosen, parity_lanes, counts, masses, inserted, weight_sum, sent, segments
):
    sent[...] = own[...]
    inserted[...] = insert([own, other], 0, chosen, parity_lanes, segments)
    shares = weight_sum.shape[1]
    mass = masses[...]
    mass_hi = mass.astype(bf16).astype(f32)
    lane = iota(mass.shape, 1)
    both = jnp.where(lane < shares, mass_hi, jnp.where(lane < 2 * shares, mass - mass_hi, 0.0))
    spread = jnp.concatenate([jnp.where(lane % shares == w, both, 0.0) for w in range(shares)], axis=0)
    total = jnp.dot(counts[...], spread.astype(bf16), preferred_element_type=f32)
    weight_sum[...] = total[:, :shares] + total[:, shares : 2 * shares]


def volume_kernel(half, *refs):
    far, refs = refs[:half], refs[half:]
    (
        near_bricks,
        far_bricks,
        near_inserted,
        chosen,
        parity_lanes,
        weight_sum,
        own_slots,
        own_owner_lanes,
        place,
        volume,
        resampled,
        segments,
        kernels,
        bricks,
        result,
        rows_out,
        regularizer,
        signals,
    ) = refs
    shares = 2 * half
    rows = segments.shape[0] // half
    row_count = bricks.shape[1]
    sub_rows, coef = rows_out.shape
    tiles = coef // SEGLEN
    reg_rows = row_count // SEGLEN
    kernels[...] = jnp.zeros(kernels.shape, bf16)
    regularizer[...] = jnp.zeros(regularizer.shape, f32)
    for p in range(shares):
        w = place[0] ^ distance_of(p, shares)
        at = pl.ds(pl.multiple_of(w % 2 * SEGLEN, SEGLEN), SEGLEN)
        brick = near_bricks[p] if p < half else far_bricks[p - half]
        kernels[w // 2, at, at] = brick[:SEGLEN]
        parts = brick[SEGLEN:].astype(f32)
        for h in range(reg_rows):
            regularizer[pl.ds(h * shares + w, 1), :] = (
                parts[h : h + 1, :] + parts[reg_rows + h : reg_rows + h + 1, :]
            )
    columns = jnp.swapaxes(regularizer[...], 0, 1)
    columns = [columns[:, h * shares : (h + 1) * shares] for h in range(reg_rows)]
    inverse = 1.0 / (weight_sum[...] + jnp.concatenate(columns, axis=0))
    inserted = insert(far, half, chosen, parity_lanes, segments) + near_inserted[...]
    inserted = inserted.astype(bf16)
    mapped = []
    for a in range(half):
        pair = jnp.dot(
            inserted[a * row_count : (a + 1) * row_count, :],
            kernels[a],
            preferred_element_type=f32,
        )
        sides = []
        for w in (2 * a, 2 * a + 1):
            side = pair[:, w % 2 * SEGLEN : (w % 2 + 1) * SEGLEN] * inverse[:, w : w + 1]
            bricks[w] = side
            sides.append(side.astype(bf16))
        mapped.append(jnp.concatenate(sides, axis=1))
    own = pltpu.make_async_copy(bricks.at[place[0]], volume, signals.at[0])
    own.start()
    back = [
        lax.dot_general(pair, kernels[a], LANES, preferred_element_type=f32).astype(bf16)
        for a, pair in enumerate(mapped)
    ]
    taken = jnp.dot(own_slots[...], jnp.concatenate(back, axis=1), preferred_element_type=f32)
    owner = own_owner_lanes[...].astype(f32)
    total = jnp.zeros((sub_rows * tiles, SEGLEN), f32)
    for w in range(shares):
        total = jnp.where(owner == float(w), taken[:, w * SEGLEN : (w + 1) * SEGLEN], total)
    result[...] = total
    for j in range(tiles):
        rows_out[:, j * SEGLEN : (j + 1) * SEGLEN] = result[pl.ds(j, sub_rows, stride=tiles), :]
    back_again = pltpu.make_async_copy(rows_out, resampled, signals.at[1])
    back_again.start()
    own.wait()
    back_again.wait()


def call(kernel, inputs, outputs, scratch=(), cost=1.0, small=(), out_space=pltpu.VMEM):
    inside = pl.BlockSpec(memory_space=pltpu.VMEM)
    scalars = pl.BlockSpec(memory_space=pltpu.SMEM)
    return pl.pallas_call(
        kernel,
        out_shape=[jax.ShapeDtypeStruct(shape, dtype) for shape, dtype in outputs],
        in_specs=[inside] * len(inputs) + [scalars] * len(small),
        out_specs=[pl.BlockSpec(memory_space=out_space)] * len(outputs),
        scratch_shapes=list(scratch),
        compiler_params=pltpu.CompilerParams(vmem_limit_bytes=24 * 2**20),
        cost_estimate=pl.CostEstimate(
            flops=int(cost * 1.15e9), bytes_accessed=0, transcendentals=0
        ),
    )(*inputs, *small)


def whole_plane(images, references, shifts, owners, slot_rows, interpolation, regularizer):
    ori_count, img_count = lax.axis_size("ori"), lax.axis_size("img")
    ori, img = lax.axis_index("ori"), lax.axis_index("img")
    shift_count = shifts.shape[0]
    own_images, coef = images.shape
    tiles = coef // SEGLEN
    half = ori_count // 2
    row_count = regularizer.shape[0]
    orient_count = references.shape[0]
    sub_rows = orient_count // img_count
    group_rows = own_images * ori_count
    columns = shift_count * orient_count
    orients = ori_count * sub_rows
    length = coef // 2 // ori_count
    place = jnp.stack([ori, img]).astype(jnp.int32)

    piece = images.reshape(own_images, tiles, SEGLEN).transpose(1, 0, 2).reshape(-1, SEGLEN)
    column = np.arange(columns)
    orient = column % orient_count
    lane = orient // sub_rows * SEGLEN + column // orient_count * sub_rows + orient % sub_rows
    pick = jnp.asarray(lane[:, None] == np.arange(img_count * SEGLEN), bf16)
    row = np.arange(shift_count * orients)
    source = row % orients // sub_rows * (SEGLEN // 2) + row // orients * sub_rows + row % sub_rows
    arrange = jnp.asarray(source[:, None] == np.arange(half * SEGLEN), bf16)
    phases, tables = call(
        phase_kernel,
        (shifts,),
        (((2, 2, -(-shift_count // 8) * 8, CHUNK), f32), ((2, -(-shift_count // 8) * 8, length), f32)),
        small=(place,),
        cost=COST_PHASE,
    )
    near, far = gather_pair(piece, phases)
    message, part = call(
        functools.partial(score_kernel, shift_count),
        (
            near,
            far,
            references,
            phases,
            pick,
            slot_rows.reshape(-1, SEGLEN),
            owners.reshape(-1, SEGLEN),
        ),
        (
            ((img_count * ori_count, group_rows, SEGLEN), bf16),
            ((2 * length // SEGLEN * group_rows, SEGLEN), bf16),
        ),
        scratch=(pltpu.VMEM((group_rows, coef), bf16), pltpu.VMEM(phases.shape[1:], f32)),
        small=(place,),
        cost=COST_SCORE,
    )
    got = lax.all_to_all(message, ("img", "ori"), split_axis=0, concat_axis=0, tiled=True)
    pieces = [part] + [hop(part, "img", k) for k in range(1, img_count)]
    beside, brick = call(
        functools.partial(beside_kernel, group_rows),
        (*pieces, interpolation, regularizer.reshape(-1, SEGLEN)),
        (((img_count * part.shape[0], SEGLEN), bf16), ((SEGLEN + 16, SEGLEN), bf16)),
        cost=COST_BESIDE,
    )
    near_bricks, far_bricks = gather_pair(brick)

    rows = 2 * (length // SEGLEN) * orients
    segments, masses = call(
        functools.partial(slice_kernel, shift_count, group_rows),
        (got, beside, tables, arrange, near_bricks),
        (((rows, SEGLEN), bf16), ((orients, SEGLEN), f32)),
        small=(place,),
        cost=COST_SLICE,
    )
    chosen, parity_lanes, counts, own_slots, own_owner_lanes = call(
        functools.partial(fact_kernel, sub_rows, ori_count),
        (got, masses),
        (
            ((half * row_count, orients * tiles), bf16),
            ((orients * tiles, SEGLEN), bf16),
            ((row_count, ori_count * orients), bf16),
            ((sub_rows * tiles, row_count), bf16),
            ((sub_rows * tiles, SEGLEN), bf16),
        ),
        scratch=(
            pltpu.VMEM((SEGLEN, SEGLEN), f32),
            pltpu.VMEM((2, orients * tiles // SEGLEN, SEGLEN), f32),
        ),
        small=(place,),
        cost=COST_FACT,
    )

    others = hops_in_plane(segments)

    def masked(count):
        return pltpu.VMEM((count * rows, 2 * SEGLEN), bf16)

    shape = ((half * row_count, 2 * SEGLEN), f32)
    inserted, weight_sum, sent = call(
        near_kernel,
        (segments, others[0], chosen, parity_lanes, counts, masses),
        (shape, ((row_count, ori_count), f32), (segments.shape, bf16)),
        scratch=(masked(2),),
        cost=COST_NEAR,
    )
    far = [hop(part, "ori", 1) for part in [sent, *others]]
    (inserted,) = call(
        functools.partial(next_kernel, 2),
        (*others[1:], chosen, parity_lanes, inserted),
        (shape,),
        scratch=(masked(half - 2),),
        cost=COST_NEAR,
    )
    volume, resampled = call(
        functools.partial(volume_kernel, half),
        (
            *far,
            near_bricks,
            far_bricks,
            inserted,
            chosen,
            parity_lanes,
            weight_sum,
            own_slots,
            own_owner_lanes,
        ),
        (((row_count, SEGLEN), f32), ((sub_rows, coef), f32)),
        scratch=(
            masked(half),
            pltpu.VMEM((half, 2 * SEGLEN, 2 * SEGLEN), bf16),
            pltpu.VMEM((ori_count, row_count, SEGLEN), f32),
            pltpu.VMEM((sub_rows * tiles, SEGLEN), f32),
            pltpu.VMEM((sub_rows, coef), f32),
            pltpu.VMEM((SEGLEN, SEGLEN), f32),
            pltpu.SemaphoreType.DMA((2,)),
        ),
        small=(place,),
        cost=COST_VOLUME,
        out_space=pl.ANY,
    )
    return (volume, resampled)


def shards(images, references, shifts, owners, slot_rows, interpolation, regularizer):
    arguments = (images, references, shifts, owners, slot_rows, interpolation, regularizer)
    whole_bytes = images.size * 2 * lax.axis_size("img") * lax.axis_size("ori")
    if whole_bytes <= 4 * 2**20:
        return whole_plane(*arguments)
    return reduced(*arguments)


def solution(mesh):
    in_specs = (
        P(("img", "ori"), None),
        P("ori", None),
        P(),
        P(("ori", "img"), None),
        P(("ori", "img")),
        P(("ori", "img"), None),
        P(("ori", "img")),
    )
    out_specs = (P(("ori", "img"), None), P(("ori", "img"), None))
    return jax.shard_map(shards, mesh=mesh, in_specs=in_specs, out_specs=out_specs, check_vma=False)
```

```python
import functools
import math

import jax
import jax.numpy as jnp
import numpy as np
from jax import lax
from jax.experimental import pallas as pl
from jax.experimental.pallas import tpu as pltpu
from jax.sharding import PartitionSpec as P

SEGLEN = 128
grid_width = 64
image_side = 128.0
CHUNK = 256
LANES = (((1,), (1,)), ((), ()))
COST_PHASE = 12.0
COST_SCORE = 0.001
COST_WEIGHT = 0.001
COST_STACK = 0.001
COST_BESIDE = 30.0
COST_FACT = 0.001
COST_SLICE = 0.001
COST_NEAR = 0.001
COST_VOLUME = 0.001
bf16 = jnp.bfloat16
f32 = jnp.float32


def hop(value, axis, distance):
    pairs = [(place, place ^ distance) for place in range(lax.axis_size(axis))]
    return lax.ppermute(value, axis, pairs)


def even_distances():
    return range(2, lax.axis_size("ori"), 2)


def gather_plane(value):
    near = jnp.concatenate([value] + [hop(value, "ori", k) for k in even_distances()], axis=0)
    return jnp.concatenate([near, hop(near, "ori", 1)], axis=0)


def phase_tables(shifts, coef):
    half_len = coef // 2
    positions = jnp.arange(half_len, dtype=jnp.int32)
    freq_x = (positions % grid_width).astype(f32)
    freq_y = (positions // grid_width - half_len // grid_width // 2).astype(f32)
    angles = (
        2.0
        * math.pi
        / image_side
        * (shifts[:, 0:1] * freq_x[None, :] + shifts[:, 1:2] * freq_y[None, :])
    )
    return (jnp.cos(angles), jnp.sin(angles))


def rotate(real_part, imag_part, cosine_row, sine_row):
    rotated_re = real_part * cosine_row[None, :] - imag_part * sine_row[None, :]
    rotated_im = real_part * sine_row[None, :] + imag_part * cosine_row[None, :]
    return jnp.concatenate([rotated_re, rotated_im], axis=1).astype(bf16)


def backproject(weights_b, group_images, cosine_table, sine_table):
    half_len = group_images.shape[1] // 2
    orient_count = weights_b.shape[1]
    total_re = jnp.zeros((orient_count, half_len), f32)
    total_im = jnp.zeros((orient_count, half_len), f32)
    for s in range(cosine_table.shape[0]):
        summed = lax.dot_general(
            weights_b[:, :, s],
            group_images,
            (((0,), (0,)), ((), ())),
            preferred_element_type=f32,
        )
        sum_re = summed[:, :half_len]
        sum_im = summed[:, half_len:]
        total_re = total_re + sum_re * cosine_table[s] + sum_im * sine_table[s]
        total_im = total_im - sum_re * sine_table[s] + sum_im * cosine_table[s]
    return jnp.concatenate([total_re, total_im], axis=1)


def merge_stats(stats, distance):
    far = hop(stats, "ori", distance)
    if distance == 1:
        return far[:, ::-1]
    half = distance // 2
    return jnp.stack([far[:, :, e ^ half] for e in range(far.shape[2])], axis=2)


def join(pairs):
    peak = pairs[0][0]
    for pair in pairs[1:]:
        peak = jnp.maximum(peak, pair[0])
    total = sum(pair[1] * jnp.exp(pair[0] - peak) for pair in pairs)
    return jnp.stack([peak, total])


def reduced(images, references, shifts, owners, slot_rows, interpolation, regularizer):
    ori_count, img_count = lax.axis_size("ori"), lax.axis_size("img")
    ori, img = lax.axis_index("ori"), lax.axis_index("img")
    shift_count = shifts.shape[0]
    coef = images.shape[1]
    own_images = images.shape[0]
    segs = coef // SEGLEN
    row_count = regularizer.shape[0]
    orient_count = references.shape[0]
    sub_rows = orient_count // img_count
    half_len = coef // 2

    group_images = gather_plane(images)
    group_rows = group_images.shape[0]
    cosine_table, sine_table = phase_tables(shifts, coef)
    references = jnp.concatenate(
        [
            lax.dynamic_slice_in_dim(references, (img ^ m) * sub_rows, sub_rows, 0)
            for m in range(img_count)
        ],
        axis=0,
    )
    real_part = references[:, :half_len].astype(f32)
    imag_part = references[:, half_len:].astype(f32)
    distance = owners[:, 0] ^ ori
    place = (distance >> 1) + (distance & 1) * (ori_count // 2)
    target = place * row_count + slot_rows
    all_rows = ori_count * row_count
    chosen = (jnp.arange(all_rows, dtype=jnp.int32)[:, None] == target[None, :]).astype(bf16)

    score_list = []
    for s in range(shift_count):
        rotated = rotate(real_part, imag_part, cosine_table[s], sine_table[s])
        score_list.append(
            lax.dot_general(
                group_images, rotated, (((1,), (1,)), ((), ())), preferred_element_type=f32
            )
        )
    scores = jnp.stack(score_list, axis=2).reshape(group_rows, -1) * (2.0 / math.sqrt(coef))
    local_peak = jnp.max(scores, axis=1)
    local_total = jnp.sum(jnp.exp(scores - local_peak[:, None]), axis=1)
    stats = jnp.stack([local_peak, local_total]).reshape(2, 2, ori_count // 2, own_images)
    stats = join([stats, merge_stats(stats, 1)])
    stats = join([stats] + [merge_stats(stats, k) for k in even_distances()])
    stats = stats.reshape(2, group_rows)
    weights = jnp.exp(scores - stats[0][:, None]) / stats[1][:, None]
    weights3 = weights.reshape(group_rows, orient_count, shift_count)
    orient_mass = jnp.sum(weights3, axis=(0, 2))
    summed = backproject(weights3.astype(bf16), group_images, cosine_table, sine_table)

    blocks = summed.reshape(img_count, sub_rows, coef)
    masses = orient_mass.reshape(img_count, sub_rows, 1)
    outgoing = jnp.concatenate(
        [blocks, jnp.broadcast_to(masses, (img_count, sub_rows, SEGLEN))], axis=2
    ).astype(bf16)
    incoming = [hop(outgoing[m], "img", m).astype(f32) for m in range(1, img_count)]
    own = blocks[0] + sum(value[:, :coef] for value in incoming)
    own_mass = masses[0] + sum(value[:, coef : coef + 1] for value in incoming)
    segments = own.astype(bf16).reshape(-1, SEGLEN)
    seg_mass = jnp.repeat(own_mass[:, 0], segs)[None, :]

    part = jnp.dot(chosen, segments, preferred_element_type=f32)
    part_mass = lax.dot_general(
        seg_mass.astype(bf16), chosen, (((1,), (1,)), ((), ())), preferred_element_type=f32
    )
    mass_rows = max(16, row_count // SEGLEN)
    part_mass = part_mass.reshape(ori_count, row_count)
    part_mass = jnp.pad(part_mass, ((0, 0), (0, mass_rows * SEGLEN - row_count)))
    parcel = jnp.concatenate(
        [part.reshape(ori_count, row_count, SEGLEN), part_mass.reshape(ori_count, -1, SEGLEN)], axis=1
    ).astype(bf16)
    half = ori_count // 2
    parcel = parcel[:half].astype(f32) + hop(parcel[half:], "ori", 1).astype(f32)
    small = parcel.astype(bf16)
    brick = parcel[0] + sum(hop(small[k // 2], "ori", k).astype(f32) for k in even_distances())
    inserted = brick[:row_count]
    weight_sum = brick[row_count:].reshape(-1)[:row_count]
    mapped = jnp.dot(
        inserted, interpolation, precision=lax.Precision.HIGHEST, preferred_element_type=f32
    )
    volume = mapped / (weight_sum + regularizer)[:, None]
    back_values = lax.dot_general(
        volume,
        interpolation,
        (((1,), (1,)), ((), ())),
        precision=lax.Precision.HIGHEST,
        preferred_element_type=f32,
    )
    bricks = gather_plane(back_values.astype(bf16))
    resampled = lax.dot_general(
        chosen, bricks, (((0,), (0,)), ((), ())), preferred_element_type=f32
    )
    return (volume, resampled.reshape(sub_rows, coef))


def iota(shape, axis):
    return lax.broadcasted_iota(jnp.int32, shape, axis)


def distance_of(place, shares):
    even = (shares - 2 * place) & (shares - 1)
    return even ^ (place // (shares // 2))


def hops_in_plane(value):
    count = lax.axis_size("ori")
    return [hop(value, "ori", distance) for distance in range(count - 2, 0, -2)]


def stacks(value, others, *after):
    count = len(others) + 1
    (near,) = call(
        functools.partial(stack_kernel, count),
        (*others, value, *after),
        (((count, *value.shape), value.dtype),),
        cost=COST_STACK,
    )
    return near, hop(near, "ori", 1)


def gather_pair(value, *after):
    return stacks(value, hops_in_plane(value), *after)


def stack_kernel(count, *refs):
    for place in range(count):
        refs[-1][(place + 1) % count] = refs[place][...]


def phase_kernel(shifts, place, phases, tables):
    count = shifts.shape[0]
    unit = 2.0 * math.pi / image_side
    moves = unit * shifts[...]

    def angles(start, positions):
        lane = iota((count, positions), 1)
        freq_x = (lane % grid_width).astype(f32)
        freq_y = (lane // grid_width + start).astype(f32) - image_side / 2
        return moves[:, 0:1] * freq_x + moves[:, 1:2] * freq_y

    first = angles(0, CHUNK)
    step = jnp.broadcast_to(moves[:, 1:2] * float(CHUNK // grid_width), (count, CHUNK))
    phases[...] = jnp.zeros(phases.shape, f32)
    for h, angle in enumerate((first, step)):
        phases[0, h, :count, :] = jnp.cos(angle)
        phases[1, h, :count, :] = jnp.sin(angle)
    length = tables.shape[2]
    angle = angles(place[0] * (length // grid_width), length)
    tables[...] = jnp.zeros(tables.shape, f32)
    tables[0, :count, :] = jnp.cos(angle)
    tables[1, :count, :] = jnp.sin(angle)


def turn(phases, now):
    cosine, sine = now[0], now[1]
    cos_step, sin_step = phases[0, 1], phases[1, 1]
    now[0] = cosine * cos_step - sine * sin_step
    now[1] = sine * cos_step + cosine * sin_step


def place_order(ori, shares, group_rows):
    own_images = group_rows // shares
    rows = 16 // own_images * group_rows
    out_row, in_row = iota((rows, 16 * shares), 0), iota((rows, 16 * shares), 1)
    share, part = in_row // 16, in_row % 16
    image = (distance_of(share, shares) ^ ori) * own_images + part % own_images
    return jnp.where(out_row == part // own_images * group_rows + image, 1.0, 0.0).astype(bf16)


def place_images(near, far, ori, out):
    shares, group_rows = 2 * near.shape[0], out.shape[0]
    step = 16 * shares // group_rows
    order = place_order(ori, shares, group_rows)
    for q in range(out.shape[1] // SEGLEN // step):
        rows = slice(16 * q, 16 * q + 16)
        block = jnp.concatenate([near[:, rows, :], far[:, rows, :]], axis=0)
        block = block.reshape(shares * 16, SEGLEN)
        placed = jnp.dot(order, block, preferred_element_type=f32).astype(bf16)
        for jj in range(step):
            lanes = pl.ds((q * step + jj) * SEGLEN, SEGLEN)
            out[:, lanes] = placed[jj * group_rows : (jj + 1) * group_rows]


def score_kernel(
    shift_count,
    near,
    far,
    references,
    phases,
    pick,
    slots,
    owners,
    place,
    message,
    piece,
    own,
    now,
):
    group_rows, coef = own.shape
    half_len = coef // 2
    place_images(near, far, place[0], own)
    tiles = piece.shape[0] // group_rows // 2
    for h in range(2):
        for t in range(tiles):
            first = h * half_len + (place[0] * tiles + t) * SEGLEN
            row = (h * tiles + t) * group_rows
            piece[row : row + group_rows, :] = own[:, pl.ds(pl.multiple_of(first, SEGLEN), SEGLEN)]
    now[0] = phases[0, 0]
    now[1] = phases[1, 0]

    def step(t, total):
        re_lanes = pl.ds(pl.multiple_of(t * CHUNK, CHUNK), CHUNK)
        im_lanes = pl.ds(pl.multiple_of(half_len + t * CHUNK, CHUNK), CHUNK)
        real_part = references[:, re_lanes].astype(f32)
        imag_part = references[:, im_lanes].astype(f32)
        rotated_re, rotated_im = [], []
        for s in range(shift_count):
            c, d = now[0, s : s + 1, :], now[1, s : s + 1, :]
            rotated_re.append((real_part * c - imag_part * d).astype(bf16))
            rotated_im.append((real_part * d + imag_part * c).astype(bf16))
        total += lax.dot_general(
            own[:, re_lanes], jnp.concatenate(rotated_re, axis=0), LANES, preferred_element_type=f32
        )
        total += lax.dot_general(
            own[:, im_lanes], jnp.concatenate(rotated_im, axis=0), LANES, preferred_element_type=f32
        )
        turn(phases, now)
        return total

    columns = shift_count * references.shape[0]
    total = lax.fori_loop(
        0, half_len // CHUNK, step, jnp.zeros((group_rows, columns), f32), unroll=True
    )
    scores = total * (2.0 / math.sqrt(coef))
    peak = jnp.max(scores, axis=1, keepdims=True)
    exponents = jnp.exp(scores - peak)
    total = jnp.sum(exponents, axis=1, keepdims=True)
    picked = jnp.dot(exponents.astype(bf16), pick[...], preferred_element_type=f32)
    blocks = pick.shape[1] // SEGLEN
    shares = message.shape[0] // blocks
    valid = columns // blocks
    lane = iota((group_rows, SEGLEN), 1)
    rest = jnp.concatenate(
        [
            part
            for fact in (slots, owners)
            for part in (
                pltpu.roll(fact[...].astype(f32), SEGLEN // 2, 1),
                fact[...].astype(f32),
            )
        ],
        axis=0,
    )
    at = valid
    for value in (peak, total):
        for _ in range(3):
            part = value.astype(bf16).astype(f32)
            rest = jnp.where(lane == at, part, rest)
            value = value - part
            at += 1
    for b in range(blocks):
        block = picked[:, b * SEGLEN : (b + 1) * SEGLEN]
        block = jnp.where(lane < valid, block, rest).astype(bf16)
        for p in range(shares):
            message[b * shares + p] = block


def beside_kernel(rows, *refs):
    *parts, kernel, regularizer, out, brick = refs
    brick[:SEGLEN, :] = kernel[...].astype(bf16)
    high = regularizer[...].astype(bf16).astype(f32)
    spare = jnp.zeros((brick.shape[0] - SEGLEN - 2 * high.shape[0], SEGLEN), f32)
    brick[SEGLEN:, :] = jnp.concatenate([high, regularizer[...] - high, spare], axis=0).astype(bf16)
    count = len(parts)
    for tile in range(parts[0].shape[0] // rows):
        for k, part in enumerate(parts):
            row = (tile * count + k) * rows
            out[row : row + rows, :] = part[tile * rows : (tile + 1) * rows, :]


def facts_of(got, share, sub_rows):
    part = got[share].astype(f32)
    rolled = pltpu.roll(part, SEGLEN // 2, 1)
    lane = iota((sub_rows, SEGLEN), 1)

    def rows(first):
        return jnp.where(
            lane < SEGLEN // 2,
            rolled[first : first + sub_rows],
            part[first + sub_rows : first + 2 * sub_rows],
        )

    return rows(0), rows(2 * sub_rows)


def flat_facts(sub_rows, shares, got, place, upright, flat):
    orients = shares * sub_rows
    blocks = flat.shape[1]
    lot = SEGLEN // orients
    pairs = [facts_of(got, place[1] * shares + p, sub_rows) for p in range(shares)]
    facts = [pair[h] for h in range(2) for pair in pairs]
    facts = jnp.concatenate(facts + [jnp.zeros((SEGLEN - 2 * orients, SEGLEN), f32)], axis=0)
    upright[...] = jnp.swapaxes(facts, 0, 1)
    parts = [upright[pl.ds(b, blocks, stride=lot), :] for b in range(lot)]
    for h in range(2):
        lanes = slice(h * orients, (h + 1) * orients)
        flat[h] = jnp.concatenate([part[:, lanes] for part in parts], axis=1)
    run = blocks // (2 * shares)
    taken = []
    for p in range(shares):
        share = place[0] ^ distance_of(p, shares)
        taken += [h * (blocks // 2) + share * run + i for h in range(2) for i in range(run)]
    slots = jnp.concatenate([flat[0, pl.ds(a, 1), :] for a in taken], axis=0)
    owners = jnp.concatenate([flat[1, pl.ds(a, 1), :] for a in taken], axis=0)
    return slots, owners


def fact_kernel(
    sub_rows,
    shares,
    got,
    after,
    place,
    chosen,
    parity_lanes,
    counts,
    own_slots,
    own_owner_lanes,
    upright,
    flat,
):
    row_count = own_slots.shape[1]
    orients = shares * sub_rows
    blocks = flat.shape[1]
    tiles = SEGLEN
    pairs = shares // 2
    slots, owners = flat_facts(sub_rows, shares, got, place, upright, flat)
    pair = (owners.astype(jnp.int32) // 2).astype(f32)
    parity = owners - 2.0 * pair
    columns = jnp.concatenate(
        [owners, parity, jnp.zeros((SEGLEN - 2 * blocks, SEGLEN), f32)], axis=0
    )
    columns = jnp.swapaxes(columns, 0, 1)
    groups = row_count // 16
    slot_row = iota((row_count, SEGLEN), 0).astype(f32).astype(bf16).reshape(groups, 16, SEGLEN)
    zeros = jnp.zeros((groups, 16, SEGLEN), bf16)
    ones = jnp.ones((groups, 16, SEGLEN), bf16)
    count_lane = iota((SEGLEN, shares * orients), 1)
    lane_owner = (count_lane // orients).astype(f32)
    same = iota((SEGLEN, shares * orients), 0) % orients == count_lane % orients
    lane_owner = jnp.where(same, lane_owner, -1.0)
    total = jnp.zeros((row_count, shares * orients), f32)
    for a in range(0, blocks, 2):
        slot_chosen, owned = [], []
        for b in (a, a + 1):
            block = slice(b * SEGLEN, (b + 1) * SEGLEN)
            slot = jnp.broadcast_to(slots[b : b + 1, :], (16, SEGLEN)).astype(bf16)
            match = slot_row == slot[None]
            for q in range(pairs):
                held = jnp.broadcast_to(pair[b : b + 1, :], (16, SEGLEN))
                held = jnp.where(held == float(q), 1.0, 0.0).astype(bf16)
                part = jnp.where(match, jnp.broadcast_to(held[None], zeros.shape), zeros)
                chosen[q * row_count : (q + 1) * row_count, block] = part.reshape(row_count, SEGLEN)
            slot_chosen.append(jnp.where(match, ones, zeros).reshape(row_count, SEGLEN))
            parity_lanes[block, :] = jnp.broadcast_to(
                columns[:, blocks + b : blocks + b + 1], (SEGLEN, SEGLEN)
            ).astype(bf16)
            owned.append(jnp.where(columns[:, b : b + 1] == lane_owner, 1.0, 0.0).astype(bf16))
        total += jnp.dot(
            jnp.concatenate(slot_chosen, axis=1),
            jnp.concatenate(owned, axis=0),
            preferred_element_type=f32,
        )
    counts[...] = total.astype(bf16)
    own = jnp.concatenate(facts_of(got, place[1] * shares + place[0], sub_rows), axis=0)
    own = jnp.concatenate([own, jnp.zeros((SEGLEN - own.shape[0], SEGLEN), f32)], axis=0)
    own = jnp.swapaxes(own, 0, 1)
    slot_lane = iota((tiles, row_count), 1).astype(f32)
    for o in range(sub_rows):
        rows = slice(o * tiles, (o + 1) * tiles)
        own_slots[rows, :] = jnp.where(slot_lane == own[:, o : o + 1], 1.0, 0.0).astype(bf16)
        own_owner_lanes[rows, :] = jnp.broadcast_to(
            own[:, sub_rows + o : sub_rows + o + 1], (tiles, SEGLEN)
        ).astype(bf16)


def slice_kernel(shift_count, group_rows, *refs):
    got, images, tables, arrange, after, place, segments, masses = refs
    length = tables.shape[2]
    shares = 2 * arrange.shape[1] // SEGLEN
    orients = arrange.shape[0] // shift_count
    lot = CHUNK // SEGLEN
    valid = shift_count * orients // shares
    img_count = got.shape[0] // shares
    image_rows = img_count * group_rows
    everything = jnp.concatenate(
        [got[(place[1] ^ k) * shares + p] for p in range(shares) for k in range(img_count)], axis=0
    )
    row, lane = iota((SEGLEN, 2 * SEGLEN), 0), iota((SEGLEN, 2 * SEGLEN), 1)
    first = jnp.where(lane < SEGLEN, valid, valid + 3)
    spread = jnp.where((row >= first) & (row < first + 3), 1.0, 0.0).astype(bf16)
    values = jnp.dot(everything, spread, preferred_element_type=f32)
    parts = [slice(p * image_rows, (p + 1) * image_rows) for p in range(shares)]
    peak = functools.reduce(jnp.maximum, [values[part, :SEGLEN] for part in parts])
    factors = [jnp.exp(values[part, :SEGLEN] - peak) for part in parts]
    total = sum(values[part, SEGLEN:] * factor for part, factor in zip(parts, factors, strict=True))
    inverse = 1.0 / total
    lane = iota((image_rows, SEGLEN), 1)
    weighted = [
        jnp.where(lane < valid, everything[part].astype(f32) * (factor * inverse), 0.0)
        for part, factor in zip(parts, factors, strict=True)
    ]
    stacked = jnp.concatenate(
        [
            (weighted[p] + pltpu.roll(weighted[p + 1], SEGLEN // 2, 1)).astype(bf16)
            for p in range(0, shares, 2)
        ],
        axis=1,
    )
    weights = lax.dot_general(arrange[...], stacked, LANES, preferred_element_type=f32)
    mass = jnp.sum(weights, axis=1, keepdims=True)
    mass = sum(mass[s * orients : (s + 1) * orients] for s in range(shift_count))
    masses[...] = jnp.broadcast_to(mass, masses.shape)
    weights = weights.astype(bf16)

    def images_at(tile):
        return images[tile * image_rows : (tile + 1) * image_rows, :]

    for t in range(length // CHUNK):
        lanes = slice(t * CHUNK, (t + 1) * CHUNK)
        tiles = range(t * lot, (t + 1) * lot)
        real_part = jnp.concatenate([images_at(j) for j in tiles], axis=1)
        imag_part = jnp.concatenate([images_at(length // SEGLEN + j) for j in tiles], axis=1)
        summed_re = jnp.dot(weights, real_part, preferred_element_type=f32)
        summed_im = jnp.dot(weights, imag_part, preferred_element_type=f32)
        total_re = jnp.zeros((orients, CHUNK), f32)
        total_im = jnp.zeros((orients, CHUNK), f32)
        for s in range(shift_count):
            c, d = tables[0, s : s + 1, lanes], tables[1, s : s + 1, lanes]
            part_re = summed_re[s * orients : (s + 1) * orients]
            part_im = summed_im[s * orients : (s + 1) * orients]
            total_re += part_re * c + part_im * d
            total_im += part_im * c - part_re * d
        for h in range(lot):
            lanes = slice(h * SEGLEN, (h + 1) * SEGLEN)
            row = (t * lot + h) * orients
            segments[row : row + orients, :] = total_re[:, lanes].astype(bf16)
            row += length // SEGLEN * orients
            segments[row : row + orients, :] = total_im[:, lanes].astype(bf16)


def insert(shares, first, chosen, parity_lanes, segments):
    rows = segments.shape[0] // len(shares)
    zero = jnp.zeros((rows, SEGLEN), bf16)
    for p in range(len(shares)):
        part = shares[p][:rows, :]
        parity = parity_lanes[(first + p) * rows : (first + p + 1) * rows, :]
        for w in range(2):
            segments[p * rows : (p + 1) * rows, w * SEGLEN : (w + 1) * SEGLEN] = jnp.where(
                parity == float(w), part, zero
            )
    lanes = slice(first * rows, (first + len(shares)) * rows)
    return jnp.dot(chosen[:, lanes], segments[...], preferred_element_type=f32)


def next_kernel(first, *refs):
    *shares, chosen, parity_lanes, before, inserted, segments = refs
    inserted[...] = before[...] + insert(shares, first, chosen, parity_lanes, segments)


def near_kernel(
    own, other, chosen, parity_lanes, counts, masses, inserted, weight_sum, sent, segments
):
    sent[...] = own[...]
    inserted[...] = insert([own, other], 0, chosen, parity_lanes, segments)
    shares = weight_sum.shape[1]
    mass = masses[...]
    mass_hi = mass.astype(bf16).astype(f32)
    lane = iota(mass.shape, 1)
    both = jnp.where(lane < shares, mass_hi, jnp.where(lane < 2 * shares, mass - mass_hi, 0.0))
    spread = jnp.concatenate([jnp.where(lane % shares == w, both, 0.0) for w in range(shares)], axis=0)
    total = jnp.dot(counts[...], spread.astype(bf16), preferred_element_type=f32)
    weight_sum[...] = total[:, :shares] + total[:, shares : 2 * shares]


def volume_kernel(half, *refs):
    far, refs = refs[:half], refs[half:]
    (
        near_bricks,
        far_bricks,
        near_inserted,
        chosen,
        parity_lanes,
        weight_sum,
        own_slots,
        own_owner_lanes,
        place,
        volume,
        resampled,
        segments,
        kernels,
        bricks,
        result,
        rows_out,
        regularizer,
        signals,
    ) = refs
    shares = 2 * half
    rows = segments.shape[0] // half
    row_count = bricks.shape[1]
    sub_rows, coef = rows_out.shape
    tiles = coef // SEGLEN
    reg_rows = row_count // SEGLEN
    kernels[...] = jnp.zeros(kernels.shape, bf16)
    regularizer[...] = jnp.zeros(regularizer.shape, f32)
    for p in range(shares):
        w = place[0] ^ distance_of(p, shares)
        at = pl.ds(pl.multiple_of(w % 2 * SEGLEN, SEGLEN), SEGLEN)
        brick = near_bricks[p] if p < half else far_bricks[p - half]
        kernels[w // 2, at, at] = brick[:SEGLEN]
        parts = brick[SEGLEN:].astype(f32)
        for h in range(reg_rows):
            regularizer[pl.ds(h * shares + w, 1), :] = (
                parts[h : h + 1, :] + parts[reg_rows + h : reg_rows + h + 1, :]
            )
    columns = jnp.swapaxes(regularizer[...], 0, 1)
    columns = [columns[:, h * shares : (h + 1) * shares] for h in range(reg_rows)]
    inverse = 1.0 / (weight_sum[...] + jnp.concatenate(columns, axis=0))
    inserted = insert(far, half, chosen, parity_lanes, segments) + near_inserted[...]
    inserted = inserted.astype(bf16)
    mapped = []
    for a in range(half):
        pair = jnp.dot(
            inserted[a * row_count : (a + 1) * row_count, :],
            kernels[a],
            preferred_element_type=f32,
        )
        sides = []
        for w in (2 * a, 2 * a + 1):
            side = pair[:, w % 2 * SEGLEN : (w % 2 + 1) * SEGLEN] * inverse[:, w : w + 1]
            bricks[w] = side
            sides.append(side.astype(bf16))
        mapped.append(jnp.concatenate(sides, axis=1))
    own = pltpu.make_async_copy(bricks.at[place[0]], volume, signals.at[0])
    own.start()
    back = [
        lax.dot_general(pair, kernels[a], LANES, preferred_element_type=f32).astype(bf16)
        for a, pair in enumerate(mapped)
    ]
    taken = jnp.dot(own_slots[...], jnp.concatenate(back, axis=1), preferred_element_type=f32)
    owner = own_owner_lanes[...].astype(f32)
    total = jnp.zeros((sub_rows * tiles, SEGLEN), f32)
    for w in range(shares):
        total = jnp.where(owner == float(w), taken[:, w * SEGLEN : (w + 1) * SEGLEN], total)
    result[...] = total
    for j in range(tiles):
        rows_out[:, j * SEGLEN : (j + 1) * SEGLEN] = result[pl.ds(j, sub_rows, stride=tiles), :]
    back_again = pltpu.make_async_copy(rows_out, resampled, signals.at[1])
    back_again.start()
    own.wait()
    back_again.wait()


def call(kernel, inputs, outputs, scratch=(), cost=1.0, small=(), out_space=pltpu.VMEM):
    inside = pl.BlockSpec(memory_space=pltpu.VMEM)
    scalars = pl.BlockSpec(memory_space=pltpu.SMEM)
    return pl.pallas_call(
        kernel,
        out_shape=[jax.ShapeDtypeStruct(shape, dtype) for shape, dtype in outputs],
        in_specs=[inside] * len(inputs) + [scalars] * len(small),
        out_specs=[pl.BlockSpec(memory_space=out_space)] * len(outputs),
        scratch_shapes=list(scratch),
        compiler_params=pltpu.CompilerParams(vmem_limit_bytes=24 * 2**20),
        cost_estimate=pl.CostEstimate(
            flops=int(cost * 1.15e9), bytes_accessed=0, transcendentals=0
        ),
    )(*inputs, *small)


def whole_plane(images, references, shifts, owners, slot_rows, interpolation, regularizer):
    ori_count, img_count = lax.axis_size("ori"), lax.axis_size("img")
    ori, img = lax.axis_index("ori"), lax.axis_index("img")
    shift_count = shifts.shape[0]
    own_images, coef = images.shape
    tiles = coef // SEGLEN
    half = ori_count // 2
    row_count = regularizer.shape[0]
    orient_count = references.shape[0]
    sub_rows = orient_count // img_count
    group_rows = own_images * ori_count
    columns = shift_count * orient_count
    orients = ori_count * sub_rows
    length = coef // 2 // ori_count
    place = jnp.stack([ori, img]).astype(jnp.int32)

    piece = images.reshape(own_images, tiles, SEGLEN).transpose(1, 0, 2).reshape(-1, SEGLEN)
    column = np.arange(columns)
    orient = column % orient_count
    lane = orient // sub_rows * SEGLEN + column // orient_count * sub_rows + orient % sub_rows
    pick = jnp.asarray(lane[:, None] == np.arange(img_count * SEGLEN), bf16)
    row = np.arange(shift_count * orients)
    source = row % orients // sub_rows * (SEGLEN // 2) + row // orients * sub_rows + row % sub_rows
    arrange = jnp.asarray(source[:, None] == np.arange(half * SEGLEN), bf16)
    phases, tables = call(
        phase_kernel,
        (shifts,),
        (((2, 2, -(-shift_count // 8) * 8, CHUNK), f32), ((2, -(-shift_count // 8) * 8, length), f32)),
        small=(place,),
        cost=COST_PHASE,
    )
    near, far = gather_pair(piece, phases)
    message, part = call(
        functools.partial(score_kernel, shift_count),
        (
            near,
            far,
            references,
            phases,
            pick,
            slot_rows.reshape(-1, SEGLEN),
            owners.reshape(-1, SEGLEN),
        ),
        (
            ((img_count * ori_count, group_rows, SEGLEN), bf16),
            ((2 * length // SEGLEN * group_rows, SEGLEN), bf16),
        ),
        scratch=(pltpu.VMEM((group_rows, coef), bf16), pltpu.VMEM(phases.shape[1:], f32)),
        small=(place,),
        cost=COST_SCORE,
    )
    got = lax.all_to_all(message, ("img", "ori"), split_axis=0, concat_axis=0, tiled=True)
    pieces = [part] + [hop(part, "img", k) for k in range(1, img_count)]
    beside, brick = call(
        functools.partial(beside_kernel, group_rows),
        (*pieces, interpolation, regularizer.reshape(-1, SEGLEN)),
        (((img_count * part.shape[0], SEGLEN), bf16), ((SEGLEN + 16, SEGLEN), bf16)),
        cost=COST_BESIDE,
    )
    near_bricks, far_bricks = gather_pair(brick)

    rows = 2 * (length // SEGLEN) * orients
    segments, masses = call(
        functools.partial(slice_kernel, shift_count, group_rows),
        (got, beside, tables, arrange, near_bricks),
        (((rows, SEGLEN), bf16), ((orients, SEGLEN), f32)),
        small=(place,),
        cost=COST_SLICE,
    )
    chosen, parity_lanes, counts, own_slots, own_owner_lanes = call(
        functools.partial(fact_kernel, sub_rows, ori_count),
        (got, masses),
        (
            ((half * row_count, orients * tiles), bf16),
            ((orients * tiles, SEGLEN), bf16),
            ((row_count, ori_count * orients), bf16),
            ((sub_rows * tiles, row_count), bf16),
            ((sub_rows * tiles, SEGLEN), bf16),
        ),
        scratch=(
            pltpu.VMEM((SEGLEN, SEGLEN), f32),
            pltpu.VMEM((2, orients * tiles // SEGLEN, SEGLEN), f32),
        ),
        small=(place,),
        cost=COST_FACT,
    )

    others = hops_in_plane(segments)

    def masked(count):
        return pltpu.VMEM((count * rows, 2 * SEGLEN), bf16)

    shape = ((half * row_count, 2 * SEGLEN), f32)
    inserted, weight_sum, sent = call(
        near_kernel,
        (segments, others[0], chosen, parity_lanes, counts, masses),
        (shape, ((row_count, ori_count), f32), (segments.shape, bf16)),
        scratch=(masked(2),),
        cost=COST_NEAR,
    )
    far = [hop(part, "ori", 1) for part in [sent, *others]]
    (inserted,) = call(
        functools.partial(next_kernel, 2),
        (*others[1:], chosen, parity_lanes, inserted),
        (shape,),
        scratch=(masked(half - 2),),
        cost=COST_NEAR,
    )
    volume, resampled = call(
        functools.partial(volume_kernel, half),
        (
            *far,
            near_bricks,
            far_bricks,
            inserted,
            chosen,
            parity_lanes,
            weight_sum,
            own_slots,
            own_owner_lanes,
        ),
        (((row_count, SEGLEN), f32), ((sub_rows, coef), f32)),
        scratch=(
            masked(half),
            pltpu.VMEM((half, 2 * SEGLEN, 2 * SEGLEN), bf16),
            pltpu.VMEM((ori_count, row_count, SEGLEN), f32),
            pltpu.VMEM((sub_rows * tiles, SEGLEN), f32),
            pltpu.VMEM((sub_rows, coef), f32),
            pltpu.VMEM((SEGLEN, SEGLEN), f32),
            pltpu.SemaphoreType.DMA((2,)),
        ),
        small=(place,),
        cost=COST_VOLUME,
        out_space=pl.ANY,
    )
    return (volume, resampled)


def shards(images, references, shifts, owners, slot_rows, interpolation, regularizer):
    arguments = (images, references, shifts, owners, slot_rows, interpolation, regularizer)
    whole_bytes = images.size * 2 * lax.axis_size("img") * lax.axis_size("ori")
    if whole_bytes <= 4 * 2**20:
        return whole_plane(*arguments)
    return reduced(*arguments)


def solution(mesh):
    in_specs = (
        P(("img", "ori"), None),
        P("ori", None),
        P(),
        P(("ori", "img"), None),
        P(("ori", "img")),
        P(("ori", "img"), None),
        P(("ori", "img")),
    )
    out_specs = (P(("ori", "img"), None), P(("ori", "img"), None))
    return jax.shard_map(shards, mesh=mesh, in_specs=in_specs, out_specs=out_specs, check_vma=False)
```

```python
import functools
import math

import jax
import jax.numpy as jnp
import numpy as np
from jax import lax
from jax.experimental import pallas as pl
from jax.experimental.pallas import tpu as pltpu
from jax.sharding import PartitionSpec as P

SEGLEN = 128
grid_width = 64
image_side = 128.0
CHUNK = 256
LANES = (((1,), (1,)), ((), ()))
COST_PHASE = 12.0
COST_SCORE = 0.001
COST_WEIGHT = 0.001
COST_STACK = 0.001
COST_BESIDE = 30.0
COST_FACT = 0.001
COST_SLICE = 0.001
COST_NEAR = 0.001
COST_VOLUME = 0.001
bf16 = jnp.bfloat16
f32 = jnp.float32


def hop(value, axis, distance):
    pairs = [(place, place ^ distance) for place in range(lax.axis_size(axis))]
    return lax.ppermute(value, axis, pairs)


def even_distances():
    return range(2, lax.axis_size("ori"), 2)


def gather_plane(value):
    near = jnp.concatenate([value] + [hop(value, "ori", k) for k in even_distances()], axis=0)
    return jnp.concatenate([near, hop(near, "ori", 1)], axis=0)


def phase_tables(shifts, coef):
    half_len = coef // 2
    positions = jnp.arange(half_len, dtype=jnp.int32)
    freq_x = (positions % grid_width).astype(f32)
    freq_y = (positions // grid_width - half_len // grid_width // 2).astype(f32)
    angles = (
        2.0
        * math.pi
        / image_side
        * (shifts[:, 0:1] * freq_x[None, :] + shifts[:, 1:2] * freq_y[None, :])
    )
    return (jnp.cos(angles), jnp.sin(angles))


def rotate(real_part, imag_part, cosine_row, sine_row):
    rotated_re = real_part * cosine_row[None, :] - imag_part * sine_row[None, :]
    rotated_im = real_part * sine_row[None, :] + imag_part * cosine_row[None, :]
    return jnp.concatenate([rotated_re, rotated_im], axis=1).astype(bf16)


def backproject(weights_b, group_images, cosine_table, sine_table):
    half_len = group_images.shape[1] // 2
    orient_count = weights_b.shape[1]
    total_re = jnp.zeros((orient_count, half_len), f32)
    total_im = jnp.zeros((orient_count, half_len), f32)
    for s in range(cosine_table.shape[0]):
        summed = lax.dot_general(
            weights_b[:, :, s],
            group_images,
            (((0,), (0,)), ((), ())),
            preferred_element_type=f32,
        )
        sum_re = summed[:, :half_len]
        sum_im = summed[:, half_len:]
        total_re = total_re + sum_re * cosine_table[s] + sum_im * sine_table[s]
        total_im = total_im - sum_re * sine_table[s] + sum_im * cosine_table[s]
    return jnp.concatenate([total_re, total_im], axis=1)


def merge_stats(stats, distance):
    far = hop(stats, "ori", distance)
    if distance == 1:
        return far[:, ::-1]
    half = distance // 2
    return jnp.stack([far[:, :, e ^ half] for e in range(far.shape[2])], axis=2)


def join(pairs):
    peak = pairs[0][0]
    for pair in pairs[1:]:
        peak = jnp.maximum(peak, pair[0])
    total = sum(pair[1] * jnp.exp(pair[0] - peak) for pair in pairs)
    return jnp.stack([peak, total])


def reduced(images, references, shifts, owners, slot_rows, interpolation, regularizer):
    ori_count, img_count = lax.axis_size("ori"), lax.axis_size("img")
    ori, img = lax.axis_index("ori"), lax.axis_index("img")
    shift_count = shifts.shape[0]
    coef = images.shape[1]
    own_images = images.shape[0]
    segs = coef // SEGLEN
    row_count = regularizer.shape[0]
    orient_count = references.shape[0]
    sub_rows = orient_count // img_count
    half_len = coef // 2

    group_images = gather_plane(images)
    group_rows = group_images.shape[0]
    cosine_table, sine_table = phase_tables(shifts, coef)
    references = jnp.concatenate(
        [
            lax.dynamic_slice_in_dim(references, (img ^ m) * sub_rows, sub_rows, 0)
            for m in range(img_count)
        ],
        axis=0,
    )
    real_part = references[:, :half_len].astype(f32)
    imag_part = references[:, half_len:].astype(f32)
    distance = owners[:, 0] ^ ori
    place = (distance >> 1) + (distance & 1) * (ori_count // 2)
    target = place * row_count + slot_rows
    all_rows = ori_count * row_count
    chosen = (jnp.arange(all_rows, dtype=jnp.int32)[:, None] == target[None, :]).astype(bf16)

    score_list = []
    for s in range(shift_count):
        rotated = rotate(real_part, imag_part, cosine_table[s], sine_table[s])
        score_list.append(
            lax.dot_general(
                group_images, rotated, (((1,), (1,)), ((), ())), preferred_element_type=f32
            )
        )
    scores = jnp.stack(score_list, axis=2).reshape(group_rows, -1) * (2.0 / math.sqrt(coef))
    local_peak = jnp.max(scores, axis=1)
    local_total = jnp.sum(jnp.exp(scores - local_peak[:, None]), axis=1)
    stats = jnp.stack([local_peak, local_total]).reshape(2, 2, ori_count // 2, own_images)
    stats = join([stats, merge_stats(stats, 1)])
    stats = join([stats] + [merge_stats(stats, k) for k in even_distances()])
    stats = stats.reshape(2, group_rows)
    weights = jnp.exp(scores - stats[0][:, None]) / stats[1][:, None]
    weights3 = weights.reshape(group_rows, orient_count, shift_count)
    orient_mass = jnp.sum(weights3, axis=(0, 2))
    summed = backproject(weights3.astype(bf16), group_images, cosine_table, sine_table)

    blocks = summed.reshape(img_count, sub_rows, coef)
    masses = orient_mass.reshape(img_count, sub_rows, 1)
    outgoing = jnp.concatenate(
        [blocks, jnp.broadcast_to(masses, (img_count, sub_rows, SEGLEN))], axis=2
    ).astype(bf16)
    incoming = [hop(outgoing[m], "img", m).astype(f32) for m in range(1, img_count)]
    own = blocks[0] + sum(value[:, :coef] for value in incoming)
    own_mass = masses[0] + sum(value[:, coef : coef + 1] for value in incoming)
    segments = own.astype(bf16).reshape(-1, SEGLEN)
    seg_mass = jnp.repeat(own_mass[:, 0], segs)[None, :]

    part = jnp.dot(chosen, segments, preferred_element_type=f32)
    part_mass = lax.dot_general(
        seg_mass.astype(bf16), chosen, (((1,), (1,)), ((), ())), preferred_element_type=f32
    )
    mass_rows = max(16, row_count // SEGLEN)
    part_mass = part_mass.reshape(ori_count, row_count)
    part_mass = jnp.pad(part_mass, ((0, 0), (0, mass_rows * SEGLEN - row_count)))
    parcel = jnp.concatenate(
        [part.reshape(ori_count, row_count, SEGLEN), part_mass.reshape(ori_count, -1, SEGLEN)], axis=1
    ).astype(bf16)
    half = ori_count // 2
    parcel = parcel[:half].astype(f32) + hop(parcel[half:], "ori", 1).astype(f32)
    small = parcel.astype(bf16)
    brick = parcel[0] + sum(hop(small[k // 2], "ori", k).astype(f32) for k in even_distances())
    inserted = brick[:row_count]
    weight_sum = brick[row_count:].reshape(-1)[:row_count]
    mapped = jnp.dot(
        inserted, interpolation, precision=lax.Precision.HIGHEST, preferred_element_type=f32
    )
    volume = mapped / (weight_sum + regularizer)[:, None]
    back_values = lax.dot_general(
        volume,
        interpolation,
        (((1,), (1,)), ((), ())),
        precision=lax.Precision.HIGHEST,
        preferred_element_type=f32,
    )
    bricks = gather_plane(back_values.astype(bf16))
    resampled = lax.dot_general(
        chosen, bricks, (((0,), (0,)), ((), ())), preferred_element_type=f32
    )
    return (volume, resampled.reshape(sub_rows, coef))


def iota(shape, axis):
    return lax.broadcasted_iota(jnp.int32, shape, axis)


def distance_of(place, shares):
    even = (shares - 2 * place) & (shares - 1)
    return even ^ (place // (shares // 2))


def hops_in_plane(value):
    count = lax.axis_size("ori")
    return [hop(value, "ori", distance) for distance in range(count - 2, 0, -2)]


def stacks(value, others, *after):
    count = len(others) + 1
    (near,) = call(
        functools.partial(stack_kernel, count),
        (*others, value, *after),
        (((count, *value.shape), value.dtype),),
        cost=COST_STACK,
    )
    return near, hop(near, "ori", 1)


def gather_pair(value, *after):
    return stacks(value, hops_in_plane(value), *after)


def stack_kernel(count, *refs):
    for place in range(count):
        refs[-1][(place + 1) % count] = refs[place][...]


def phase_kernel(shifts, place, phases, tables):
    count = shifts.shape[0]
    unit = 2.0 * math.pi / image_side
    moves = unit * shifts[...]

    def angles(start, positions):
        lane = iota((count, positions), 1)
        freq_x = (lane % grid_width).astype(f32)
        freq_y = (lane // grid_width + start).astype(f32) - image_side / 2
        return moves[:, 0:1] * freq_x + moves[:, 1:2] * freq_y

    first = angles(0, CHUNK)
    step = jnp.broadcast_to(moves[:, 1:2] * float(CHUNK // grid_width), (count, CHUNK))
    phases[...] = jnp.zeros(phases.shape, f32)
    for h, angle in enumerate((first, step)):
        phases[0, h, :count, :] = jnp.cos(angle)
        phases[1, h, :count, :] = jnp.sin(angle)
    length = tables.shape[2]
    angle = angles(place[0] * (length // grid_width), length)
    tables[...] = jnp.zeros(tables.shape, f32)
    tables[0, :count, :] = jnp.cos(angle)
    tables[1, :count, :] = jnp.sin(angle)


def turn(phases, now):
    cosine, sine = now[0], now[1]
    cos_step, sin_step = phases[0, 1], phases[1, 1]
    now[0] = cosine * cos_step - sine * sin_step
    now[1] = sine * cos_step + cosine * sin_step


def place_order(ori, shares, group_rows):
    own_images = group_rows // shares
    rows = 16 // own_images * group_rows
    out_row, in_row = iota((rows, 16 * shares), 0), iota((rows, 16 * shares), 1)
    share, part = in_row // 16, in_row % 16
    image = (distance_of(share, shares) ^ ori) * own_images + part % own_images
    return jnp.where(out_row == part // own_images * group_rows + image, 1.0, 0.0).astype(bf16)


def place_images(near, far, ori, out):
    shares, group_rows = 2 * near.shape[0], out.shape[0]
    step = 16 * shares // group_rows
    order = place_order(ori, shares, group_rows)
    for q in range(out.shape[1] // SEGLEN // step):
        rows = slice(16 * q, 16 * q + 16)
        block = jnp.concatenate([near[:, rows, :], far[:, rows, :]], axis=0)
        block = block.reshape(shares * 16, SEGLEN)
        placed = jnp.dot(order, block, preferred_element_type=f32).astype(bf16)
        for jj in range(step):
            lanes = pl.ds((q * step + jj) * SEGLEN, SEGLEN)
            out[:, lanes] = placed[jj * group_rows : (jj + 1) * group_rows]


def score_kernel(
    shift_count,
    near,
    far,
    references,
    phases,
    pick,
    slots,
    owners,
    place,
    message,
    piece,
    own,
    now,
):
    group_rows, coef = own.shape
    half_len = coef // 2
    place_images(near, far, place[0], own)
    tiles = piece.shape[0] // group_rows // 2
    for h in range(2):
        for t in range(tiles):
            first = h * half_len + (place[0] * tiles + t) * SEGLEN
            row = (h * tiles + t) * group_rows
            piece[row : row + group_rows, :] = own[:, pl.ds(pl.multiple_of(first, SEGLEN), SEGLEN)]
    now[0] = phases[0, 0]
    now[1] = phases[1, 0]

    def step(t, total):
        re_lanes = pl.ds(pl.multiple_of(t * CHUNK, CHUNK), CHUNK)
        im_lanes = pl.ds(pl.multiple_of(half_len + t * CHUNK, CHUNK), CHUNK)
        real_part = references[:, re_lanes].astype(f32)
        imag_part = references[:, im_lanes].astype(f32)
        rotated_re, rotated_im = [], []
        for s in range(shift_count):
            c, d = now[0, s : s + 1, :], now[1, s : s + 1, :]
            rotated_re.append((real_part * c - imag_part * d).astype(bf16))
            rotated_im.append((real_part * d + imag_part * c).astype(bf16))
        total += lax.dot_general(
            own[:, re_lanes], jnp.concatenate(rotated_re, axis=0), LANES, preferred_element_type=f32
        )
        total += lax.dot_general(
            own[:, im_lanes], jnp.concatenate(rotated_im, axis=0), LANES, preferred_element_type=f32
        )
        turn(phases, now)
        return total

    columns = shift_count * references.shape[0]
    total = lax.fori_loop(
        0, half_len // CHUNK, step, jnp.zeros((group_rows, columns), f32), unroll=True
    )
    scores = total * (2.0 / math.sqrt(coef))
    peak = jnp.max(scores, axis=1, keepdims=True)
    exponents = jnp.exp(scores - peak)
    total = jnp.sum(exponents, axis=1, keepdims=True)
    picked = jnp.dot(exponents.astype(bf16), pick[...], preferred_element_type=f32)
    blocks = pick.shape[1] // SEGLEN
    shares = message.shape[0] // blocks
    valid = columns // blocks
    lane = iota((group_rows, SEGLEN), 1)
    rest = jnp.concatenate(
        [
            part
            for fact in (slots, owners)
            for part in (
                pltpu.roll(fact[...].astype(f32), SEGLEN // 2, 1),
                fact[...].astype(f32),
            )
        ],
        axis=0,
    )
    at = valid
    for value in (peak, total):
        for _ in range(3):
            part = value.astype(bf16).astype(f32)
            rest = jnp.where(lane == at, part, rest)
            value = value - part
            at += 1
    for b in range(blocks):
        block = picked[:, b * SEGLEN : (b + 1) * SEGLEN]
        block = jnp.where(lane < valid, block, rest).astype(bf16)
        for p in range(shares):
            message[b * shares + p] = block


def beside_kernel(rows, *refs):
    *parts, kernel, regularizer, out, brick = refs
    brick[:SEGLEN, :] = kernel[...].astype(bf16)
    high = regularizer[...].astype(bf16).astype(f32)
    spare = jnp.zeros((brick.shape[0] - SEGLEN - 2 * high.shape[0], SEGLEN), f32)
    brick[SEGLEN:, :] = jnp.concatenate([high, regularizer[...] - high, spare], axis=0).astype(bf16)
    count = len(parts)
    for tile in range(parts[0].shape[0] // rows):
        for k, part in enumerate(parts):
            row = (tile * count + k) * rows
            out[row : row + rows, :] = part[tile * rows : (tile + 1) * rows, :]


def facts_of(got, share, sub_rows):
    part = got[share].astype(f32)
    rolled = pltpu.roll(part, SEGLEN // 2, 1)
    lane = iota((sub_rows, SEGLEN), 1)

    def rows(first):
        return jnp.where(
            lane < SEGLEN // 2,
            rolled[first : first + sub_rows],
            part[first + sub_rows : first + 2 * sub_rows],
        )

    return rows(0), rows(2 * sub_rows)


def flat_facts(sub_rows, shares, got, place, upright, flat):
    orients = shares * sub_rows
    blocks = flat.shape[1]
    lot = SEGLEN // orients
    pairs = [facts_of(got, place[1] * shares + p, sub_rows) for p in range(shares)]
    facts = [pair[h] for h in range(2) for pair in pairs]
    facts = jnp.concatenate(facts + [jnp.zeros((SEGLEN - 2 * orients, SEGLEN), f32)], axis=0)
    upright[...] = jnp.swapaxes(facts, 0, 1)
    parts = [upright[pl.ds(b, blocks, stride=lot), :] for b in range(lot)]
    for h in range(2):
        lanes = slice(h * orients, (h + 1) * orients)
        flat[h] = jnp.concatenate([part[:, lanes] for part in parts], axis=1)
    run = blocks // (2 * shares)
    taken = []
    for p in range(shares):
        share = place[0] ^ distance_of(p, shares)
        taken += [h * (blocks // 2) + share * run + i for h in range(2) for i in range(run)]
    slots = jnp.concatenate([flat[0, pl.ds(a, 1), :] for a in taken], axis=0)
    owners = jnp.concatenate([flat[1, pl.ds(a, 1), :] for a in taken], axis=0)
    return slots, owners


def fact_kernel(
    sub_rows,
    shares,
    got,
    after,
    place,
    chosen,
    parity_lanes,
    counts,
    own_slots,
    own_owner_lanes,
    upright,
    flat,
):
    row_count = own_slots.shape[1]
    orients = shares * sub_rows
    blocks = flat.shape[1]
    tiles = SEGLEN
    pairs = shares // 2
    slots, owners = flat_facts(sub_rows, shares, got, place, upright, flat)
    pair = (owners.astype(jnp.int32) // 2).astype(f32)
    parity = owners - 2.0 * pair
    columns = jnp.concatenate(
        [owners, parity, jnp.zeros((SEGLEN - 2 * blocks, SEGLEN), f32)], axis=0
    )
    columns = jnp.swapaxes(columns, 0, 1)
    groups = row_count // 16
    slot_row = iota((row_count, SEGLEN), 0).astype(f32).astype(bf16).reshape(groups, 16, SEGLEN)
    zeros = jnp.zeros((groups, 16, SEGLEN), bf16)
    ones = jnp.ones((groups, 16, SEGLEN), bf16)
    count_lane = iota((SEGLEN, shares * orients), 1)
    lane_owner = (count_lane // orients).astype(f32)
    same = iota((SEGLEN, shares * orients), 0) % orients == count_lane % orients
    lane_owner = jnp.where(same, lane_owner, -1.0)
    total = jnp.zeros((row_count, shares * orients), f32)
    for a in range(0, blocks, 2):
        slot_chosen, owned = [], []
        for b in (a, a + 1):
            block = slice(b * SEGLEN, (b + 1) * SEGLEN)
            slot = jnp.broadcast_to(slots[b : b + 1, :], (16, SEGLEN)).astype(bf16)
            match = slot_row == slot[None]
            for q in range(pairs):
                held = jnp.broadcast_to(pair[b : b + 1, :], (16, SEGLEN))
                held = jnp.where(held == float(q), 1.0, 0.0).astype(bf16)
                part = jnp.where(match, jnp.broadcast_to(held[None], zeros.shape), zeros)
                chosen[q * row_count : (q + 1) * row_count, block] = part.reshape(row_count, SEGLEN)
            slot_chosen.append(jnp.where(match, ones, zeros).reshape(row_count, SEGLEN))
            parity_lanes[block, :] = jnp.broadcast_to(
                columns[:, blocks + b : blocks + b + 1], (SEGLEN, SEGLEN)
            ).astype(bf16)
            owned.append(jnp.where(columns[:, b : b + 1] == lane_owner, 1.0, 0.0).astype(bf16))
        total += jnp.dot(
            jnp.concatenate(slot_chosen, axis=1),
            jnp.concatenate(owned, axis=0),
            preferred_element_type=f32,
        )
    counts[...] = total.astype(bf16)
    own = jnp.concatenate(facts_of(got, place[1] * shares + place[0], sub_rows), axis=0)
    own = jnp.concatenate([own, jnp.zeros((SEGLEN - own.shape[0], SEGLEN), f32)], axis=0)
    own = jnp.swapaxes(own, 0, 1)
    slot_lane = iota((tiles, row_count), 1).astype(f32)
    for o in range(sub_rows):
        rows = slice(o * tiles, (o + 1) * tiles)
        own_slots[rows, :] = jnp.where(slot_lane == own[:, o : o + 1], 1.0, 0.0).astype(bf16)
        own_owner_lanes[rows, :] = jnp.broadcast_to(
            own[:, sub_rows + o : sub_rows + o + 1], (tiles, SEGLEN)
        ).astype(bf16)


def slice_kernel(shift_count, group_rows, *refs):
    got, images, tables, arrange, after, place, segments, masses = refs
    length = tables.shape[2]
    shares = 2 * arrange.shape[1] // SEGLEN
    orients = arrange.shape[0] // shift_count
    lot = CHUNK // SEGLEN
    valid = shift_count * orients // shares
    img_count = got.shape[0] // shares
    image_rows = img_count * group_rows
    everything = jnp.concatenate(
        [got[(place[1] ^ k) * shares + p] for p in range(shares) for k in range(img_count)], axis=0
    )
    row, lane = iota((SEGLEN, 2 * SEGLEN), 0), iota((SEGLEN, 2 * SEGLEN), 1)
    first = jnp.where(lane < SEGLEN, valid, valid + 3)
    spread = jnp.where((row >= first) & (row < first + 3), 1.0, 0.0).astype(bf16)
    values = jnp.dot(everything, spread, preferred_element_type=f32)
    parts = [slice(p * image_rows, (p + 1) * image_rows) for p in range(shares)]
    peak = functools.reduce(jnp.maximum, [values[part, :SEGLEN] for part in parts])
    factors = [jnp.exp(values[part, :SEGLEN] - peak) for part in parts]
    total = sum(values[part, SEGLEN:] * factor for part, factor in zip(parts, factors, strict=True))
    inverse = 1.0 / total
    lane = iota((image_rows, SEGLEN), 1)
    weighted = [
        jnp.where(lane < valid, everything[part].astype(f32) * (factor * inverse), 0.0)
        for part, factor in zip(parts, factors, strict=True)
    ]
    stacked = jnp.concatenate(
        [
            (weighted[p] + pltpu.roll(weighted[p + 1], SEGLEN // 2, 1)).astype(bf16)
            for p in range(0, shares, 2)
        ],
        axis=1,
    )
    weights = lax.dot_general(arrange[...], stacked, LANES, preferred_element_type=f32)
    mass = jnp.sum(weights, axis=1, keepdims=True)
    mass = sum(mass[s * orients : (s + 1) * orients] for s in range(shift_count))
    masses[...] = jnp.broadcast_to(mass, masses.shape)
    weights = weights.astype(bf16)

    def images_at(tile):
        return images[tile * image_rows : (tile + 1) * image_rows, :]

    for t in range(length // CHUNK):
        lanes = slice(t * CHUNK, (t + 1) * CHUNK)
        tiles = range(t * lot, (t + 1) * lot)
        real_part = jnp.concatenate([images_at(j) for j in tiles], axis=1)
        imag_part = jnp.concatenate([images_at(length // SEGLEN + j) for j in tiles], axis=1)
        summed_re = jnp.dot(weights, real_part, preferred_element_type=f32)
        summed_im = jnp.dot(weights, imag_part, preferred_element_type=f32)
        total_re = jnp.zeros((orients, CHUNK), f32)
        total_im = jnp.zeros((orients, CHUNK), f32)
        for s in range(shift_count):
            c, d = tables[0, s : s + 1, lanes], tables[1, s : s + 1, lanes]
            part_re = summed_re[s * orients : (s + 1) * orients]
            part_im = summed_im[s * orients : (s + 1) * orients]
            total_re += part_re * c + part_im * d
            total_im += part_im * c - part_re * d
        for h in range(lot):
            lanes = slice(h * SEGLEN, (h + 1) * SEGLEN)
            row = (t * lot + h) * orients
            segments[row : row + orients, :] = total_re[:, lanes].astype(bf16)
            row += length // SEGLEN * orients
            segments[row : row + orients, :] = total_im[:, lanes].astype(bf16)


def insert(shares, first, chosen, parity_lanes, segments):
    rows = segments.shape[0] // len(shares)
    zero = jnp.zeros((rows, SEGLEN), bf16)
    for p in range(len(shares)):
        part = shares[p][:rows, :]
        parity = parity_lanes[(first + p) * rows : (first + p + 1) * rows, :]
        for w in range(2):
            segments[p * rows : (p + 1) * rows, w * SEGLEN : (w + 1) * SEGLEN] = jnp.where(
                parity == float(w), part, zero
            )
    lanes = slice(first * rows, (first + len(shares)) * rows)
    return jnp.dot(chosen[:, lanes], segments[...], preferred_element_type=f32)


def next_kernel(first, *refs):
    *shares, chosen, parity_lanes, before, inserted, segments = refs
    inserted[...] = before[...] + insert(shares, first, chosen, parity_lanes, segments)


def near_kernel(
    own, other, chosen, parity_lanes, counts, masses, inserted, weight_sum, sent, segments
):
    sent[...] = own[...]
    inserted[...] = insert([own, other], 0, chosen, parity_lanes, segments)
    shares = weight_sum.shape[1]
    mass = masses[...]
    mass_hi = mass.astype(bf16).astype(f32)
    lane = iota(mass.shape, 1)
    both = jnp.where(lane < shares, mass_hi, jnp.where(lane < 2 * shares, mass - mass_hi, 0.0))
    spread = jnp.concatenate([jnp.where(lane % shares == w, both, 0.0) for w in range(shares)], axis=0)
    total = jnp.dot(counts[...], spread.astype(bf16), preferred_element_type=f32)
    weight_sum[...] = total[:, :shares] + total[:, shares : 2 * shares]


def volume_kernel(half, *refs):
    far, refs = refs[:half], refs[half:]
    (
        near_bricks,
        far_bricks,
        near_inserted,
        chosen,
        parity_lanes,
        weight_sum,
        own_slots,
        own_owner_lanes,
        place,
        volume,
        resampled,
        segments,
        kernels,
        bricks,
        result,
        rows_out,
        regularizer,
        signals,
    ) = refs
    shares = 2 * half
    rows = segments.shape[0] // half
    row_count = bricks.shape[1]
    sub_rows, coef = rows_out.shape
    tiles = coef // SEGLEN
    reg_rows = row_count // SEGLEN
    kernels[...] = jnp.zeros(kernels.shape, bf16)
    regularizer[...] = jnp.zeros(regularizer.shape, f32)
    for p in range(shares):
        w = place[0] ^ distance_of(p, shares)
        at = pl.ds(pl.multiple_of(w % 2 * SEGLEN, SEGLEN), SEGLEN)
        brick = near_bricks[p] if p < half else far_bricks[p - half]
        kernels[w // 2, at, at] = brick[:SEGLEN]
        parts = brick[SEGLEN:].astype(f32)
        for h in range(reg_rows):
            regularizer[pl.ds(h * shares + w, 1), :] = (
                parts[h : h + 1, :] + parts[reg_rows + h : reg_rows + h + 1, :]
            )
    columns = jnp.swapaxes(regularizer[...], 0, 1)
    columns = [columns[:, h * shares : (h + 1) * shares] for h in range(reg_rows)]
    inverse = 1.0 / (weight_sum[...] + jnp.concatenate(columns, axis=0))
    inserted = insert(far, half, chosen, parity_lanes, segments) + near_inserted[...]
    inserted = inserted.astype(bf16)
    mapped = []
    for a in range(half):
        pair = jnp.dot(
            inserted[a * row_count : (a + 1) * row_count, :],
            kernels[a],
            preferred_element_type=f32,
        )
        sides = []
        for w in (2 * a, 2 * a + 1):
            side = pair[:, w % 2 * SEGLEN : (w % 2 + 1) * SEGLEN] * inverse[:, w : w + 1]
            bricks[w] = side
            sides.append(side.astype(bf16))
        mapped.append(jnp.concatenate(sides, axis=1))
    own = pltpu.make_async_copy(bricks.at[place[0]], volume, signals.at[0])
    own.start()
    back = [
        lax.dot_general(pair, kernels[a], LANES, preferred_element_type=f32).astype(bf16)
        for a, pair in enumerate(mapped)
    ]
    taken = jnp.dot(own_slots[...], jnp.concatenate(back, axis=1), preferred_element_type=f32)
    owner = own_owner_lanes[...].astype(f32)
    total = taken[:, :SEGLEN]
    for w in range(1, shares):
        total = jnp.where(owner == float(w), taken[:, w * SEGLEN : (w + 1) * SEGLEN], total)
    result[...] = total
    for j in range(tiles):
        rows_out[:, j * SEGLEN : (j + 1) * SEGLEN] = result[pl.ds(j, sub_rows, stride=tiles), :]
    back_again = pltpu.make_async_copy(rows_out, resampled, signals.at[1])
    back_again.start()
    own.wait()
    back_again.wait()


def call(kernel, inputs, outputs, scratch=(), cost=1.0, small=(), out_space=pltpu.VMEM):
    inside = pl.BlockSpec(memory_space=pltpu.VMEM)
    scalars = pl.BlockSpec(memory_space=pltpu.SMEM)
    return pl.pallas_call(
        kernel,
        out_shape=[jax.ShapeDtypeStruct(shape, dtype) for shape, dtype in outputs],
        in_specs=[inside] * len(inputs) + [scalars] * len(small),
        out_specs=[pl.BlockSpec(memory_space=out_space)] * len(outputs),
        scratch_shapes=list(scratch),
        compiler_params=pltpu.CompilerParams(vmem_limit_bytes=24 * 2**20),
        cost_estimate=pl.CostEstimate(
            flops=int(cost * 1.15e9), bytes_accessed=0, transcendentals=0
        ),
    )(*inputs, *small)


def whole_plane(images, references, shifts, owners, slot_rows, interpolation, regularizer):
    ori_count, img_count = lax.axis_size("ori"), lax.axis_size("img")
    ori, img = lax.axis_index("ori"), lax.axis_index("img")
    shift_count = shifts.shape[0]
    own_images, coef = images.shape
    tiles = coef // SEGLEN
    half = ori_count // 2
    row_count = regularizer.shape[0]
    orient_count = references.shape[0]
    sub_rows = orient_count // img_count
    group_rows = own_images * ori_count
    columns = shift_count * orient_count
    orients = ori_count * sub_rows
    length = coef // 2 // ori_count
    place = jnp.stack([ori, img]).astype(jnp.int32)

    piece = images.reshape(own_images, tiles, SEGLEN).transpose(1, 0, 2).reshape(-1, SEGLEN)
    column = np.arange(columns)
    orient = column % orient_count
    lane = orient // sub_rows * SEGLEN + column // orient_count * sub_rows + orient % sub_rows
    pick = jnp.asarray(lane[:, None] == np.arange(img_count * SEGLEN), bf16)
    row = np.arange(shift_count * orients)
    source = row % orients // sub_rows * (SEGLEN // 2) + row // orients * sub_rows + row % sub_rows
    arrange = jnp.asarray(source[:, None] == np.arange(half * SEGLEN), bf16)
    phases, tables = call(
        phase_kernel,
        (shifts,),
        (((2, 2, -(-shift_count // 8) * 8, CHUNK), f32), ((2, -(-shift_count // 8) * 8, length), f32)),
        small=(place,),
        cost=COST_PHASE,
    )
    near, far = gather_pair(piece, phases)
    message, part = call(
        functools.partial(score_kernel, shift_count),
        (
            near,
            far,
            references,
            phases,
            pick,
            slot_rows.reshape(-1, SEGLEN),
            owners.reshape(-1, SEGLEN),
        ),
        (
            ((img_count * ori_count, group_rows, SEGLEN), bf16),
            ((2 * length // SEGLEN * group_rows, SEGLEN), bf16),
        ),
        scratch=(pltpu.VMEM((group_rows, coef), bf16), pltpu.VMEM(phases.shape[1:], f32)),
        small=(place,),
        cost=COST_SCORE,
    )
    got = lax.all_to_all(message, ("img", "ori"), split_axis=0, concat_axis=0, tiled=True)
    pieces = [part] + [hop(part, "img", k) for k in range(1, img_count)]
    beside, brick = call(
        functools.partial(beside_kernel, group_rows),
        (*pieces, interpolation, regularizer.reshape(-1, SEGLEN)),
        (((img_count * part.shape[0], SEGLEN), bf16), ((SEGLEN + 16, SEGLEN), bf16)),
        cost=COST_BESIDE,
    )
    near_bricks, far_bricks = gather_pair(brick)

    rows = 2 * (length // SEGLEN) * orients
    segments, masses = call(
        functools.partial(slice_kernel, shift_count, group_rows),
        (got, beside, tables, arrange, near_bricks),
        (((rows, SEGLEN), bf16), ((orients, SEGLEN), f32)),
        small=(place,),
        cost=COST_SLICE,
    )
    chosen, parity_lanes, counts, own_slots, own_owner_lanes = call(
        functools.partial(fact_kernel, sub_rows, ori_count),
        (got, masses),
        (
            ((half * row_count, orients * tiles), bf16),
            ((orients * tiles, SEGLEN), bf16),
            ((row_count, ori_count * orients), bf16),
            ((sub_rows * tiles, row_count), bf16),
            ((sub_rows * tiles, SEGLEN), bf16),
        ),
        scratch=(
            pltpu.VMEM((SEGLEN, SEGLEN), f32),
            pltpu.VMEM((2, orients * tiles // SEGLEN, SEGLEN), f32),
        ),
        small=(place,),
        cost=COST_FACT,
    )

    others = hops_in_plane(segments)

    def masked(count):
        return pltpu.VMEM((count * rows, 2 * SEGLEN), bf16)

    shape = ((half * row_count, 2 * SEGLEN), f32)
    inserted, weight_sum, sent = call(
        near_kernel,
        (segments, others[0], chosen, parity_lanes, counts, masses),
        (shape, ((row_count, ori_count), f32), (segments.shape, bf16)),
        scratch=(masked(2),),
        cost=COST_NEAR,
    )
    far = [hop(part, "ori", 1) for part in [sent, *others]]
    (inserted,) = call(
        functools.partial(next_kernel, 2),
        (*others[1:], chosen, parity_lanes, inserted),
        (shape,),
        scratch=(masked(half - 2),),
        cost=COST_NEAR,
    )
    volume, resampled = call(
        functools.partial(volume_kernel, half),
        (
            *far,
            near_bricks,
            far_bricks,
            inserted,
            chosen,
            parity_lanes,
            weight_sum,
            own_slots,
            own_owner_lanes,
        ),
        (((row_count, SEGLEN), f32), ((sub_rows, coef), f32)),
        scratch=(
            masked(half),
            pltpu.VMEM((half, 2 * SEGLEN, 2 * SEGLEN), bf16),
            pltpu.VMEM((ori_count, row_count, SEGLEN), f32),
            pltpu.VMEM((sub_rows * tiles, SEGLEN), f32),
            pltpu.VMEM((sub_rows, coef), f32),
            pltpu.VMEM((SEGLEN, SEGLEN), f32),
            pltpu.SemaphoreType.DMA((2,)),
        ),
        small=(place,),
        cost=COST_VOLUME,
        out_space=pl.ANY,
    )
    return (volume, resampled)


def shards(images, references, shifts, owners, slot_rows, interpolation, regularizer):
    arguments = (images, references, shifts, owners, slot_rows, interpolation, regularizer)
    whole_bytes = images.size * 2 * lax.axis_size("img") * lax.axis_size("ori")
    if whole_bytes <= 4 * 2**20:
        return whole_plane(*arguments)
    return reduced(*arguments)


def solution(mesh):
    in_specs = (
        P(("img", "ori"), None),
        P("ori", None),
        P(),
        P(("ori", "img"), None),
        P(("ori", "img")),
        P(("ori", "img"), None),
        P(("ori", "img")),
    )
    out_specs = (P(("ori", "img"), None), P(("ori", "img"), None))
    return jax.shard_map(shards, mesh=mesh, in_specs=in_specs, out_specs=out_specs, check_vma=False)
```
